32 devices in a mesh: dp: 4 (over z), expert: 8 (over y, x, core).
Axes of the slice: x: 2, y: 2, z: 4, core: 2. Of those that a mesh axis runs over, the one named last changes fastest.
Arguments:
- tokens: bfloat16 [16384, 768], P(('dp', 'expert')), may hold values from -6 to 6
- out_grad: bfloat16 [16384, 768], P(('dp', 'expert')), may hold values from -6 to 6
- routes: int32 [16384, 2], P(('dp', 'expert')), may hold values from 0 to 7, all different within a row; in each aligned block of 256 rows (0 to 255, 256 to 511, ...) at most 128 rows name the same one
- lengths: int32 [64], P(('dp', 'expert')), may hold values from 128 to 256, as said below
- attention: float32 [4, 768, 768], P(None, ('dp', 'expert'))
- gain_bias: float32 [7, 768], P(None, ('dp', 'expert')), may hold values from -2 to 2
- router: float32 [8, 768], P(None, ('dp', 'expert')), may hold values from -0.21875 to 0.21875
- expert_up: float32 [8, 3072, 768], P('expert', 'dp'), may hold values from -0.625 to 0.625
- up_bias: float32 [8, 3072], P('expert', 'dp'), may hold values from -3 to 3
- expert_down: float32 [8, 3072, 768], P('expert', 'dp'), may hold values from -0.109375 to 0.109375
- down_bias: float32 [8, 768], P('expert', 'dp'), may hold values from -3 to 3
- first_attention: float32 [4, 768, 768], P(None, ('dp', 'expert'))
- first_gain_bias: float32 [7, 768], P(None, ('dp', 'expert'))
- first_router: float32 [8, 768], P(None, ('dp', 'expert'))
- first_expert_up: float32 [8, 3072, 768], P('expert', 'dp')
- first_up_bias: float32 [8, 3072], P('expert', 'dp')
- first_expert_down: float32 [8, 3072, 768], P('expert', 'dp')
- first_down_bias: float32 [8, 768], P('expert', 'dp')
- square_attention: float32 [4, 768, 768], P(None, ('dp', 'expert')), as said below
- square_gain_bias: float32 [7, 768], P(None, ('dp', 'expert')), as said below
- square_router: float32 [8, 768], P(None, ('dp', 'expert')), as said below
- square_expert_up: float32 [8, 3072, 768], P('expert', 'dp'), as said below
- square_up_bias: float32 [8, 3072], P('expert', 'dp'), as said below
- square_expert_down: float32 [8, 3072, 768], P('expert', 'dp'), as said below
- square_down_bias: float32 [8, 768], P('expert', 'dp'), as said below
Outputs:
- output: float32 [16384, 768], P(('dp', 'expert'))
- input_grad: float32 [16384, 768], P(('dp', 'expert'))
- grad_attention: float32 [4, 768, 768], P(None, ('dp', 'expert'))
- grad_gain_bias: float32 [7, 768], P(None, ('dp', 'expert'))
- grad_router: float32 [8, 768], P(None, ('dp', 'expert'))
- grad_expert_up: float32 [8, 3072, 768], P('expert', 'dp')
- grad_up_bias: float32 [8, 3072], P('expert', 'dp')
- grad_expert_down: float32 [8, 3072, 768], P('expert', 'dp')
- grad_down_bias: float32 [8, 768], P('expert', 'dp')
- new_attention: float32 [4, 768, 768], P(None, ('dp', 'expert'))
- new_gain_bias: float32 [7, 768], P(None, ('dp', 'expert'))
- new_router: float32 [8, 768], P(None, ('dp', 'expert'))
- new_expert_up: float32 [8, 3072, 768], P('expert', 'dp')
- new_up_bias: float32 [8, 3072], P('expert', 'dp')
- new_expert_down: float32 [8, 3072, 768], P('expert', 'dp')
- new_down_bias: float32 [8, 768], P('expert', 'dp')
- new_first_attention: float32 [4, 768, 768], P(None, ('dp', 'expert'))
- new_first_gain_bias: float32 [7, 768], P(None, ('dp', 'expert'))
- new_first_router: float32 [8, 768], P(None, ('dp', 'expert'))
- new_first_expert_up: float32 [8, 3072, 768], P('expert', 'dp')
- new_first_up_bias: float32 [8, 3072], P('expert', 'dp')
- new_first_expert_down: float32 [8, 3072, 768], P('expert', 'dp')
- new_first_down_bias: float32 [8, 768], P('expert', 'dp')
- new_square_attention: float32 [4, 768, 768], P(None, ('dp', 'expert'))
- new_square_gain_bias: float32 [7, 768], P(None, ('dp', 'expert'))
- new_square_router: float32 [8, 768], P(None, ('dp', 'expert'))
- new_square_expert_up: float32 [8, 3072, 768], P('expert', 'dp')
- new_square_up_bias: float32 [8, 3072], P('expert', 'dp')
- new_square_expert_down: float32 [8, 3072, 768], P('expert', 'dp')
- new_square_down_bias: float32 [8, 768], P('expert', 'dp')
The draws below stay inside these ranges and needn't reach their ends.
Inputs may be any that keep to these rules, and one draw needn't show every extreme that they name: `routes`: each row names two different experts. In each aligned block of 256 rows (the rows of one device's micro-batch) no expert is named by more than 128 rows, and some block reaches 128. `lengths`: the first sequence is full. `square_attention`: Positive. `square_gain_bias`: Positive. `square_router`: Positive. `square_expert_up`: Positive. `square_up_bias`: Positive. `square_expert_down`: Positive. `square_down_bias`: Positive.
All inputs are finite; a program needn't handle non-finite values.
Results may differ from the reference program's by a relative error of at most 0.018.
Values may be sent and summed in bfloat16 or wider, within the bound.
A program may use at most 256 MiB of HBM per device.

```python
import math
import jax
import jax.numpy as jnp
import numpy as np
from jax import lax

D = 768
HEADS = 12
HEAD_DIM = 64
FF = 3072
EXPERTS = 8
LEN = 256
STEP = 3
ROWS = 256
TOKENS = 16384
SEQS = 64
CAP = 128


def draw_lengths(key, part):
    key = jax.random.fold_in(key, 3)
    drawn = jax.random.randint(key, (SEQS,), LEN // 2, LEN + 1, dtype=jnp.int32)
    return drawn.at[0].set(LEN)


def draw_attention(key, part):
    key = jax.random.fold_in(key, 5)
    base = jnp.clip(jax.random.normal(key, (4, D, D), jnp.float32), -6.0, 6.0)
    factors = jnp.array([1.0, 1.0, 1.0, 6.0], jnp.float32)
    return base * factors[:, None, None] * D ** (-0.5)


def draw_gain_bias(key, part):
    key = jax.random.fold_in(key, 7)
    base = jnp.clip(jax.random.normal(key, (7, D), jnp.float32), -4.0, 4.0)
    centre = jnp.array([1.0, 0.0, 0.0, 0.0, 0.0, 1.0, 0.0], jnp.float32)[:, None]
    spread = jnp.array([0.25, 0.5, 0.5, 0.5, 0.5, 0.25, 0.5], jnp.float32)[:, None]
    return centre + spread * base


def past_pair(key, label, shape, level):
    key = jax.random.fold_in(key, label)
    early_key, later_key = jax.random.split(key)
    early = jnp.clip(jax.random.normal(early_key, shape, jnp.float32), -5.0, 5.0) * (0.8 * level)
    later = jnp.clip(jax.random.normal(later_key, shape, jnp.float32), -5.0, 5.0) * (0.8 * level)
    return (early, later)


def first_state(pair):
    return 0.09 * pair[0] + 0.1 * pair[1]


def square_state(pair, level):
    return 0.0475 * pair[0] * pair[0] + 0.05 * pair[1] * pair[1] + 0.001 * level * level


def attention_level():
    return 1.5 * TOKENS ** 0.5


def vector_level():
    return 6.0 * TOKENS ** 0.5


def router_level():
    return 26.0 * (TOKENS / EXPERTS) ** 0.5


def expert_rows():
    return (2.0 * TOKENS / EXPERTS) ** 0.5


def draw_first_attention(key, part):
    return first_state(past_pair(key, 31, (4, D, D), attention_level()))


def draw_square_attention(key, part):
    return square_state(past_pair(key, 31, (4, D, D), attention_level()), attention_level())


def draw_first_gain_bias(key, part):
    return first_state(past_pair(key, 32, (7, D), vector_level()))


def draw_square_gain_bias(key, part):
    return square_state(past_pair(key, 32, (7, D), vector_level()), vector_level())


def draw_first_router(key, part):
    return first_state(past_pair(key, 33, (EXPERTS, D), router_level()))


def draw_square_router(key, part):
    return square_state(past_pair(key, 33, (EXPERTS, D), router_level()), router_level())


def draw_first_expert_up(key, part):
    return first_state(past_pair(key, 34, (EXPERTS, FF, D), 0.3 * expert_rows()))


def draw_square_expert_up(key, part):
    return square_state(past_pair(key, 34, (EXPERTS, FF, D), 0.3 * expert_rows()), 0.3 * expert_rows())


def draw_first_up_bias(key, part):
    return first_state(past_pair(key, 35, (EXPERTS, FF), 0.22 * expert_rows()))


def draw_square_up_bias(key, part):
    return square_state(past_pair(key, 35, (EXPERTS, FF), 0.22 * expert_rows()), 0.22 * expert_rows())


def draw_first_expert_down(key, part):
    return first_state(past_pair(key, 36, (EXPERTS, FF, D), 1.5 * expert_rows()))


def draw_square_expert_down(key, part):
    return square_state(past_pair(key, 36, (EXPERTS, FF, D), 1.5 * expert_rows()), 1.5 * expert_rows())


def draw_first_down_bias(key, part):
    return first_state(past_pair(key, 37, (EXPERTS, D), 0.55 * expert_rows()))


def draw_square_down_bias(key, part):
    return square_state(past_pair(key, 37, (EXPERTS, D), 0.55 * expert_rows()), 0.55 * expert_rows())


def levels(own_key, extent, pieces, least, high):
    level = 1.0
    for dim, blocks in pieces:
        draws = jax.random.uniform(jax.random.fold_in(jax.random.fold_in(own_key, 6), dim), (blocks,), jnp.float32, least / len(pieces), high / len(pieces))
        level = level * jnp.repeat(jnp.exp(draws), extent[dim] // blocks).reshape((-1,) + (1,) * (len(extent) - 1 - dim))
    return level


def deal_out(rng, own, number, rows, number_of, top, reach, slope):
    order = jax.random.permutation(rng, number_of)
    packed, common = load_shares(number_of, rows * top, reach, slope, True), load_shares(number_of, rows * top, reach, slope, False)
    places = jnp.arange(number_of)

    def named(sizes, offset_by):
        used = int((sizes > 0).sum())
        fixed = max(1, used // 4)
        moved = fixed + (places - fixed + offset_by * (used - fixed)) % max(1, number_of - fixed)
        return jnp.zeros((number_of,), jnp.int32).at[order[jnp.where(places < fixed, places, moved)]].set(jnp.asarray(sizes, jnp.int32))

    sizes = jnp.where(number % 4 == 0, named(packed, number // 4), named(common, number - number // 4 - 1))
    mixed = jax.random.permutation(jax.random.fold_in(own, 3), number_of)
    giver, receiver = mixed[0:number_of // 2 * 2:2], mixed[1:number_of // 2 * 2:2]
    margin = jnp.minimum(sizes[giver] - 1, reach - sizes[receiver]) // 2
    margin = jnp.where((giver == order[0]) | (receiver == order[0]) | (sizes[receiver] == 0), 0, jnp.maximum(margin, 0))
    moved = jax.random.randint(jax.random.fold_in(own, 4), (number_of // 2,), 0, 1 << 20) % (margin + 1)
    sizes = sizes.at[giver].add(-moved).at[receiver].add(moved)
    labels = jnp.searchsorted(jnp.cumsum(sizes), jnp.arange(rows * top), side="right").astype(jnp.int32)
    grid = labels.reshape(top, rows).T
    grid = grid[jax.random.permutation(jax.random.fold_in(own, 1), rows)]
    offset_by = jax.random.randint(jax.random.fold_in(own, 2), (rows, 1), 0, top)
    return jnp.take_along_axis(grid, (jnp.arange(top)[None, :] + offset_by) % top, axis=1)


def load_shares(amount, total, reach, lean, full):
    loads = [(1 << 20) // math.isqrt(rank ** lean) + 1 for rank in range(1, amount + 1)]
    largest = reach if full else min(reach, max(-(-total // amount), total * loads[0] // sum(loads)))
    least = 1 if total - largest >= amount - 1 else 0
    given, surplus = [largest] + [least] * (amount - 1), total - largest - least * (amount - 1)
    while surplus > 0:
        movable = [i for i in range(1, amount) if given[i] < largest] or [i for i in range(1, amount) if given[i] < reach]
        whole, remaining = sum([loads[i] for i in movable]), surplus
        for i in movable:
            more = min(reach - given[i], max(1, remaining * loads[i] // whole), surplus)
            given[i] = given[i] + more
            surplus = surplus - more
    return np.array(given)


def bell_draw(own_key, dims, scale, limit, cuts=(), kind=jnp.bfloat16):
    values = scale * jax.random.normal(own_key, dims, jnp.float32)
    if cuts:
        values = values * levels(own_key, dims, cuts, -0.22, 0.18)
    return jnp.clip(values, -limit, limit).astype(kind)


def setup_inputs(seed: int = 0) -> dict:
    seeds = jax.random.split(jax.random.key(seed), 26)
    tokens = bell_draw(seeds[0], (TOKENS, D), 1.0, 6.0, ((0, 32),))
    out_grad = bell_draw(seeds[1], (TOKENS, D), 1.0, 6.0, ((0, 32),))
    routes_keys = jax.random.split(jax.random.fold_in(seeds[2], 1), TOKENS // ROWS)
    routes_turns = jax.random.permutation(jax.random.fold_in(seeds[2], 3), TOKENS // ROWS)
    routes = jax.vmap(lambda own, number: deal_out(jax.random.fold_in(seeds[2], 2), own, number, ROWS, EXPERTS, 2, CAP, 2))(routes_keys, routes_turns).reshape((TOKENS, 2))
    lengths = draw_lengths(jax.random.fold_in(seeds[25], 71), 0)
    attention = draw_attention(jax.random.fold_in(seeds[25], 71), 0)
    gain_bias = draw_gain_bias(jax.random.fold_in(seeds[25], 71), 0)
    router = bell_draw(seeds[6], (EXPERTS, D), D ** -0.5, 0.21875, ((1, 32),), jnp.float32)
    expert_up = bell_draw(seeds[7], (EXPERTS, FF, D), (D // 9) ** -0.5, 0.625, ((0, 8), (1, 4)), jnp.float32)
    up_bias = bell_draw(seeds[8], (EXPERTS, FF), 0.5, 3.0, ((0, 8), (1, 4)), jnp.float32)
    expert_down = bell_draw(seeds[9], (EXPERTS, FF, D), FF ** -0.5, 0.109375, ((0, 8), (1, 4)), jnp.float32)
    down_bias = bell_draw(seeds[10], (EXPERTS, D), 0.5, 3.0, ((0, 8), (1, 4)), jnp.float32)
    first_attention = draw_first_attention(jax.random.fold_in(seeds[25], 71), 0)
    first_gain_bias = draw_first_gain_bias(jax.random.fold_in(seeds[25], 71), 0)
    first_router = draw_first_router(jax.random.fold_in(seeds[25], 71), 0)
    first_expert_up = draw_first_expert_up(jax.random.fold_in(seeds[25], 71), 0)
    first_up_bias = draw_first_up_bias(jax.random.fold_in(seeds[25], 71), 0)
    first_expert_down = draw_first_expert_down(jax.random.fold_in(seeds[25], 71), 0)
    first_down_bias = draw_first_down_bias(jax.random.fold_in(seeds[25], 71), 0)
    square_attention = draw_square_attention(jax.random.fold_in(seeds[25], 71), 0)
    square_gain_bias = draw_square_gain_bias(jax.random.fold_in(seeds[25], 71), 0)
    square_router = draw_square_router(jax.random.fold_in(seeds[25], 71), 0)
    square_expert_up = draw_square_expert_up(jax.random.fold_in(seeds[25], 71), 0)
    square_up_bias = draw_square_up_bias(jax.random.fold_in(seeds[25], 71), 0)
    square_expert_down = draw_square_expert_down(jax.random.fold_in(seeds[25], 71), 0)
    square_down_bias = draw_square_down_bias(jax.random.fold_in(seeds[25], 71), 0)
    return {"tokens": tokens, "out_grad": out_grad, "routes": routes, "lengths": lengths, "attention": attention, "gain_bias": gain_bias, "router": router, "expert_up": expert_up, "up_bias": up_bias, "expert_down": expert_down, "down_bias": down_bias, "first_attention": first_attention, "first_gain_bias": first_gain_bias, "first_router": first_router, "first_expert_up": first_expert_up, "first_up_bias": first_up_bias, "first_expert_down": first_expert_down, "first_down_bias": first_down_bias, "square_attention": square_attention, "square_gain_bias": square_gain_bias, "square_router": square_router, "square_expert_up": square_expert_up, "square_up_bias": square_up_bias, "square_expert_down": square_expert_down, "square_down_bias": square_down_bias}


NORM_EPS = 1e-06
NEG_FILL = -1000000000.0
BETA_ONE = 0.9
BETA_TWO = 0.95
WEIGHT_DECAY = 0.1
ADAM_EPS = 1e-08
HIGHEST = lax.Precision.HIGHEST

@jax.custom_vjp
def low(v):
    return lax.optimization_barrier(v.astype(jnp.bfloat16)).astype(jnp.float32)

@jax.custom_vjp
def low_back(v):
    return v

def low_keep(v):
    return (low(v), None)

def low_pass(kept, grad):
    return (grad,)

def back_keep(v):
    return (v, None)

def back_low(kept, grad):
    return (low(grad),)
low.defvjp(low_keep, low_pass)
low_back.defvjp(back_keep, back_low)

def norm_rows(values, gain, bias):
    center = values - lax.optimization_barrier(jnp.mean(values, axis=-1, keepdims=True))
    spread = lax.optimization_barrier(jnp.mean(center * center, axis=-1, keepdims=True))
    return center * lax.rsqrt(spread + NORM_EPS) * gain + bias

def slot_tables(route_rows, experts_all, capacity):
    flat = route_rows.reshape(-1)
    count = flat.shape[0]
    onehot = (flat[:, None] == jnp.arange(experts_all, dtype=jnp.int32)[None, :]).astype(jnp.int32)
    before = (jnp.cumsum(onehot, axis=0) - onehot).astype(jnp.int32)
    slot = lax.optimization_barrier(jnp.sum(before * onehot, axis=1)).astype(jnp.int32)
    positions = (flat * capacity + slot).astype(jnp.int32)
    table = jnp.full((experts_all * capacity,), count, jnp.int32).at[positions].set(jnp.arange(count, dtype=jnp.int32))
    return (positions.reshape(route_rows.shape), table)

def gate_pair(picked):
    return jnp.stack([jax.nn.sigmoid(picked[:, 0] - picked[:, 1]), jax.nn.sigmoid(picked[:, 1] - picked[:, 0])], axis=1)

def adam_step(weight, grad, first, square, rate):
    new_first = BETA_ONE * first + (1.0 - BETA_ONE) * grad
    new_square = BETA_TWO * square + (1.0 - BETA_TWO) * grad * grad
    first_hat = new_first / (1.0 - BETA_ONE ** STEP)
    square_hat = new_square / (1.0 - BETA_TWO ** STEP)
    update = -rate * (first_hat / (jnp.sqrt(square_hat) + ADAM_EPS) + WEIGHT_DECAY * weight)
    return (weight + update, new_first, new_square)

def reference(tokens, out_grad, routes, lengths, attention, gain_bias, router, expert_up, up_bias, expert_down, down_bias, first_attention, first_gain_bias, first_router, first_expert_up, first_up_bias, first_expert_down, first_down_bias, square_attention, square_gain_bias, square_router, square_expert_up, square_up_bias, square_expert_down, square_down_bias):
    blocks = TOKENS // ROWS
    group = math.gcd(SEQS, max(1, 4096 // LEN))
    scale = HEAD_DIM ** (-0.5)
    route_blocks = routes.reshape(blocks, ROWS, 2)
    positions, tables = jax.vmap(lambda rows: slot_tables(rows, EXPERTS, CAP))(route_blocks)
    token_of_slot = (tables // 2).astype(jnp.int32).reshape(blocks, EXPERTS, CAP).transpose(1, 0, 2)
    flat_positions = positions.reshape(blocks, 2 * ROWS)

    def forward(attention_f, gain_f, router_f, up_f, upb_f, down_f, downb_f, tokens_f):
        weights = low(attention_f)
        vector = low(gain_f)
        router_b = low(router_f)
        up_b = low(up_f)
        upb_b = low(upb_f)
        down_b = low(down_f)
        downb_b = low(downb_f)

        def attend(pair):
            rows_x, seq_len = pair
            normed = low(norm_rows(rows_x, vector[0], vector[1]))
            proj = jnp.einsum('gsd,jde->jgse', normed, weights[:3], precision=HIGHEST)
            queries = low_back(low(proj[0] + vector[2])).reshape(group, LEN, HEADS, HEAD_DIM)
            key_rows = low_back(low(proj[1])).reshape(group, LEN, HEADS, HEAD_DIM)
            values = low_back(low(proj[2] + vector[3])).reshape(group, LEN, HEADS, HEAD_DIM)
            scores = jnp.einsum('gqhe,gkhe->ghqk', queries, key_rows, precision=HIGHEST) * scale
            scores = low_back(scores)
            valid = jnp.arange(LEN, dtype=jnp.int32)[None, :] < seq_len[:, None]
            scores = jnp.where(valid[:, None, None, :], scores, NEG_FILL)
            chance = low(jax.nn.softmax(scores, axis=-1))
            context = jnp.einsum('ghqk,gkhe->gqhe', chance, values, precision=HIGHEST)
            context = low_back(low(context)).reshape(group, LEN, D)
            branch = low_back(jnp.einsum('gsd,de->gse', context, weights[3], precision=HIGHEST) + vector[4])
            return rows_x + branch
        seq_rows = tokens_f.reshape(SEQS // group, group, LEN, D)
        resid = lax.map(jax.checkpoint(attend), (seq_rows, lengths.reshape(SEQS // group, group))).reshape(TOKENS, D)
        normed_two = low(norm_rows(resid, vector[5], vector[6]))
        logits = jnp.dot(normed_two, router_b.T, precision=HIGHEST)
        picked = jnp.take_along_axis(logits, routes, axis=1)
        gates = gate_pair(picked)
        padded = jnp.concatenate([normed_two.reshape(blocks, ROWS, D), jnp.zeros((blocks, 1, D), jnp.float32)], axis=1)

        def expert(pack):
            up_one, upb_one, down_one, downb_one, slot_rows = pack
            taken = low_back(jnp.take_along_axis(padded, slot_rows[:, :, None], axis=1))
            pre = low_back(jnp.einsum('bcd,fd->bcf', taken, up_one, precision=HIGHEST) + upb_one)
            hidden = low(jax.nn.gelu(pre))
            result = jnp.einsum('bcf,fd->bcd', hidden, down_one, precision=HIGHEST) + downb_one
            return low_back(low(result))
        expert_outs = lax.map(jax.checkpoint(expert), (up_b, upb_b, down_b, downb_b, token_of_slot))
        flat_outs = expert_outs.transpose(1, 0, 2, 3).reshape(blocks, EXPERTS * CAP, D)
        combined = jnp.take_along_axis(flat_outs, flat_positions[:, :, None], axis=1).reshape(TOKENS, 2, D)
        return resid + gates[:, 0:1] * combined[:, 0] + gates[:, 1:2] * combined[:, 1]
    params = (attention, gain_bias, router, expert_up, up_bias, expert_down, down_bias)
    result, pull = jax.vjp(forward, *params, tokens.astype(jnp.float32))
    grads = pull(out_grad.astype(jnp.float32))
    firsts = (first_attention, first_gain_bias, first_router, first_expert_up, first_up_bias, first_expert_down, first_down_bias)
    squares = (square_attention, square_gain_bias, square_router, square_expert_up, square_up_bias, square_expert_down, square_down_bias)
    rates = (1.6 * D ** (-0.5), 0.3, 0.5 * D ** (-0.5), 1.5 * D ** (-0.5), 0.25, 0.5 * FF ** (-0.5), 0.25)
    updated = [adam_step(params[i], grads[i], firsts[i], squares[i], rates[i]) for i in range(7)]
    return (result, grads[7], grads[0], grads[1], grads[2], grads[3], grads[4], grads[5], grads[6], updated[0][0], updated[1][0], updated[2][0], updated[3][0], updated[4][0], updated[5][0], updated[6][0], updated[0][1], updated[1][1], updated[2][1], updated[3][1], updated[4][1], updated[5][1], updated[6][1], updated[0][2], updated[1][2], updated[2][2], updated[3][2], updated[4][2], updated[5][2], updated[6][2])
```

```python
import jax
import jax.numpy as jnp
from jax import lax
from jax.sharding import PartitionSpec as P

D = 768
HEADS = 12
HEAD_DIM = 64
LEN = 256
STEP = 3
ROWS = 256
BIAS_ROWS = 16

NORM_EPS = 1e-06
NEG_FILL = -1000000000.0
BETA_ONE = 0.9
BETA_TWO = 0.95
WEIGHT_DECAY = 0.1
ADAM_EPS = 1e-08
HIGHEST = lax.Precision.HIGHEST
GELU_C = 0.7978845608028654
GELU_K = 0.044715
f32 = jnp.float32
b16 = jnp.bfloat16


def norm_rows(values, gain, bias):
    center = values - jnp.mean(values, axis=-1, keepdims=True)
    spread = jnp.mean(center * center, axis=-1, keepdims=True)
    return center * lax.rsqrt(spread + NORM_EPS) * gain + bias


def gate_pair(picked):
    return jnp.stack(
        [jax.nn.sigmoid(picked[:, 0] - picked[:, 1]), jax.nn.sigmoid(picked[:, 1] - picked[:, 0])],
        axis=1,
    )


def adam_step(weight, grad, first, square, rate):
    new_first = BETA_ONE * first + (1.0 - BETA_ONE) * grad
    new_square = BETA_TWO * square + (1.0 - BETA_TWO) * grad * grad
    first_hat = new_first / (1.0 - BETA_ONE**STEP)
    square_hat = new_square / (1.0 - BETA_TWO**STEP)
    update = -rate * (first_hat / (jnp.sqrt(square_hat) + ADAM_EPS) + WEIGHT_DECAY * weight)
    return (weight + update, new_first, new_square)


def slots_of(routes, experts, capacity):
    flat = routes.reshape(-1, 2 * ROWS)
    onehot = (flat[:, :, None] == jnp.arange(experts, dtype=jnp.int32)).astype(b16)
    row = lax.broadcasted_iota(jnp.int32, (2 * ROWS, 2 * ROWS), 0)
    col = lax.broadcasted_iota(jnp.int32, (2 * ROWS, 2 * ROWS), 1)
    earlier = (col < row).astype(b16)
    before = jnp.einsum("ij,bje->bie", earlier, onehot, preferred_element_type=f32)
    slot = jnp.sum(before * onehot.astype(f32), axis=-1).astype(jnp.int32)
    return (flat * capacity + slot).reshape(-1, ROWS, 2)


def expert_chunk(x, dout, up, up_bias, down):
    pre = jnp.einsum("sd,fd->sf", x, up, preferred_element_type=f32) + up_bias
    inner = jnp.tanh(GELU_C * (pre + GELU_K * pre * pre * pre))
    hidden = (0.5 * pre * (1.0 + inner)).astype(b16)
    slope = 0.5 * (1.0 + inner) + 0.5 * pre * (1.0 - inner * inner) * (
        GELU_C * (1.0 + 3.0 * GELU_K * pre * pre)
    )
    out = jnp.einsum("sf,fd->sd", hidden, down, preferred_element_type=f32)
    grad_down = jnp.einsum("sf,sd->fd", hidden, dout, preferred_element_type=f32)
    grad_hidden = jnp.einsum("sd,fd->sf", dout, down, preferred_element_type=f32)
    grad_pre = (slope * grad_hidden).astype(b16)
    grad_up = jnp.einsum("sf,sd->fd", grad_pre, x, preferred_element_type=f32)
    grad_up_bias = jnp.sum(grad_pre.astype(f32), axis=0)
    grad_x = jnp.einsum("sf,fd->sd", grad_pre, up, preferred_element_type=f32)
    return out, grad_x, grad_up, grad_up_bias, grad_down


def pack_expert(up, down, up_bias, down_bias, dtype):
    part = up.shape[0]
    tail = jnp.zeros((BIAS_ROWS, D), dtype)
    tail = tail.at[0, :part].set(up_bias.astype(dtype))
    tail = tail.at[1, : down_bias.shape[0]].set(down_bias.astype(dtype))
    return jnp.concatenate([up.astype(dtype), down.astype(dtype), tail], axis=0)


def shift(x, step, least):
    n = lax.axis_size("dp")
    if step > 0:
        pairs = [(i, i + 1) for i in range(least, n - 1)]
    else:
        pairs = [(i, i - 1) for i in range(1, n - least)]
    return lax.ppermute(x, "dp", pairs)


def body(
    tokens, out_grad, routes, lengths,
    attention, gain_bias, router, expert_up, up_bias, expert_down, down_bias,
    first_attention, first_gain_bias, first_router, first_expert_up, first_up_bias, first_expert_down, first_down_bias,
    square_attention, square_gain_bias, square_router, square_expert_up, square_up_bias, square_expert_down, square_down_bias,
):
    experts = router.shape[0]
    capacity = 4 * ROWS // experts
    count = tokens.shape[0]
    blocks = count // ROWS
    seqs = count // LEN
    part = expert_up.shape[1]
    narrow = down_bias.shape[1]
    cols = attention.shape[1]
    devices = D // cols
    n_dp = lax.axis_size("dp")
    assert n_dp == 4 and expert_up.shape[0] == 1
    me = lax.axis_index("dp")
    mine = lax.axis_index("expert")
    scale = HEAD_DIM ** (-0.5)
    both = ("dp", "expert")

    own = pack_expert(expert_up[0], expert_down[0], up_bias[0], down_bias[0], b16)
    right, left = [own], [own]
    for step in range(n_dp - 1):
        right.append(shift(right[-1], 1, step))
        left.append(shift(left[-1], -1, step))

    flat_len = (7 + experts) * cols
    extra = -(-flat_len // D)
    small = jnp.concatenate([gain_bias, router], axis=0).astype(b16).reshape(-1)
    small = jnp.pad(small, (0, extra * D - flat_len)).reshape(extra, D)
    packed = jnp.concatenate([attention.astype(b16).reshape(4 * cols, D), small], axis=0)
    whole = lax.all_gather(packed, both, axis=0, tiled=False)
    weights_b = whole[:, : 4 * cols].reshape(devices, 4, cols, D).transpose(1, 0, 2, 3).reshape(4, D, D)
    small = whole[:, 4 * cols :].reshape(devices, extra * D)[:, :flat_len].reshape(devices, 7 + experts, cols)
    small = small.transpose(1, 0, 2).reshape(7 + experts, D)
    vector = small[:7].astype(f32)
    router_b = small[7:]

    positions = slots_of(routes, experts, capacity)
    slot_ids = jnp.arange(experts * capacity, dtype=jnp.int32)
    hit = positions[:, :, :, None] == slot_ids
    choose = hit.astype(b16)
    both_choose = choose[:, :, 0] + choose[:, :, 1]
    split = both_choose.reshape(blocks, ROWS, experts, capacity)
    other = jnp.flip(routes, axis=1).reshape(blocks, ROWS, 2)
    partner = jnp.sum(jnp.where(hit, other[:, :, :, None], 0), axis=(1, 2)).astype(f32)
    partner = partner.reshape(blocks, experts, capacity).transpose(1, 0, 2)
    partner = lax.all_to_all(partner, "expert", split_axis=0, concat_axis=0, tiled=True)
    grad_rows = out_grad.reshape(blocks, ROWS, D)

    def dispatch(rows):
        sent = jnp.einsum("btec,btd->ebcd", split, rows, preferred_element_type=f32).astype(b16)
        got = lax.all_to_all(sent, "expert", split_axis=0, concat_axis=0, tiled=True)
        return got.reshape(experts * blocks * capacity, D)

    grad_slots = dispatch(grad_rows)

    head_shape = (seqs, LEN, HEADS, HEAD_DIM)
    rows_in = tokens.astype(f32)
    grad_out = out_grad.astype(f32)
    normed_one_b = norm_rows(rows_in, vector[0], vector[1]).astype(b16)
    proj = jnp.einsum("rd,jde->jre", normed_one_b, weights_b[:3], preferred_element_type=f32)
    queries = (proj[0] + vector[2]).astype(b16).reshape(head_shape)
    key_rows = proj[1].astype(b16).reshape(head_shape)
    values = (proj[2] + vector[3]).astype(b16).reshape(head_shape)
    valid = (jnp.arange(LEN, dtype=jnp.int32)[None, :] < lengths[:, None])[:, None, None, :]
    scores = jnp.einsum("bqhe,bkhe->bhqk", queries, key_rows, preferred_element_type=f32) * scale
    scores = jnp.where(valid, scores, NEG_FILL)
    top_score = jnp.max(scores, axis=-1, keepdims=True)
    log_total = top_score + jnp.log(jnp.sum(jnp.exp(scores - top_score), axis=-1, keepdims=True))
    chance_b = jnp.exp(scores - log_total).astype(b16)
    context_b = (
        jnp.einsum("bhqk,bkhe->bqhe", chance_b, values, preferred_element_type=f32)
        .astype(b16)
        .reshape(count, D)
    )
    resid = rows_in + (jnp.dot(context_b, weights_b[3], preferred_element_type=f32) + vector[4])
    normed_two_b = norm_rows(resid, vector[5], vector[6]).astype(b16)
    slots_in = dispatch(normed_two_b.reshape(blocks, ROWS, D))
    logits = jnp.einsum("rd,ed->re", normed_two_b, router_b, preferred_element_type=f32)
    chooser = (routes[:, :, None] == jnp.arange(experts, dtype=jnp.int32)).astype(f32)
    picked = jnp.sum(logits[:, None, :] * chooser, axis=-1)
    gates = gate_pair(picked)

    slot_logits = jnp.einsum("sd,ed->se", slots_in, router_b, preferred_element_type=f32)
    ids = jnp.arange(experts, dtype=jnp.int32)
    rival = partner.reshape(-1).astype(jnp.int32)
    margin = jnp.sum(
        slot_logits * ((ids == mine).astype(f32) - (rival[:, None] == ids).astype(f32)), axis=-1
    )
    dout = (jax.nn.sigmoid(margin)[:, None] * grad_slots.astype(f32)).astype(b16)
    grad_down_bias = jnp.sum(dout.astype(f32), axis=0)

    def pick(*arrays):
        out = arrays[-1]
        for i in range(len(arrays) - 2, -1, -1):
            out = jnp.where(me == i, arrays[i], out)
        return out

    parts = [
        own,
        pick(left[1], right[1], left[1], right[1]),
        pick(left[2], left[1], right[1], right[2]),
        pick(left[3], left[2], right[2], right[3]),
    ]
    names = [
        me,
        pick(1, 0, 3, 2),
        pick(2, 2, 1, 1),
        pick(3, 3, 0, 0),
    ]
    out_slots = jnp.zeros((slots_in.shape[0], D), f32)
    grad_slots_in = jnp.zeros((slots_in.shape[0], D), f32)
    part_grads = []
    bias_rows = []
    for packed_part, name in zip(parts, names):
        up, down, tail = packed_part[:part], packed_part[part : 2 * part], packed_part[2 * part :]
        out, grad_x, grad_up, grad_up_bias, grad_down = expert_chunk(
            slots_in, dout, up, tail[0, :part].astype(f32), down
        )
        out_slots = out_slots + out
        grad_slots_in = grad_slots_in + grad_x
        bias_rows.append(tail[1, :narrow])
        part_grads.append(
            (
                grad_up,
                grad_down,
                grad_up_bias,
                lax.dynamic_slice(grad_down_bias, (name * narrow,), (narrow,)),
            )
        )
    place = jnp.stack(names)
    down_bias_full = jnp.zeros((n_dp, narrow), b16).at[place].set(jnp.stack(bias_rows)).reshape(D)
    out_b = (out_slots + down_bias_full.astype(f32)).astype(b16)
    grad_b = grad_slots_in.astype(b16)

    def give_back(rows):
        sent = rows.reshape(experts, blocks, capacity, D)
        got = lax.all_to_all(sent, "expert", split_axis=0, concat_axis=0, tiled=True)
        return got.transpose(1, 0, 2, 3).reshape(blocks, experts * capacity, D)

    back = give_back(out_b)
    returned = give_back(grad_b)

    packs = [pack_expert(g[0], g[1], g[2], g[3], b16) for g in part_grads]
    zero = jnp.zeros_like(packs[0])
    ahead = [pick(p, q, r, s) for p, q, r, s in (
        (packs[1], packs[2], packs[1], zero),
        (packs[2], packs[3], zero, zero),
        (packs[3], zero, zero, zero),
    )]
    behind = [pick(p, q, r, s) for p, q, r, s in (
        (zero, packs[1], packs[2], packs[1]),
        (zero, zero, packs[3], packs[2]),
        (zero, zero, zero, packs[3]),
    )]
    going, coming = None, None
    for offset in range(n_dp - 1, 0, -1):
        send = ahead[offset - 1]
        if going is not None:
            send = (send.astype(f32) + going.astype(f32)).astype(b16)
        n = n_dp
        going = lax.ppermute(send, "dp", [(i, i + 1) for i in range(n - offset)])
        send = behind[offset - 1]
        if coming is not None:
            send = (send.astype(f32) + coming.astype(f32)).astype(b16)
        coming = lax.ppermute(send, "dp", [(i, i - 1) for i in range(offset, n)])
    arrived = going.astype(f32) + coming.astype(f32)
    mine_up, mine_down, mine_up_bias, mine_down_bias = part_grads[0]
    shard_up = (mine_up + arrived[:part])[None]
    shard_down = (mine_down + arrived[part : 2 * part])[None]
    shard_up_bias = (mine_up_bias + arrived[2 * part, :part])[None]
    shard_down_bias = (mine_down_bias + arrived[2 * part + 1, :narrow])[None]

    expert_out = jnp.einsum("btks,bsd->kbtd", choose, back, preferred_element_type=f32)
    expert_out = expert_out.reshape(2, count, D)
    output = resid + gates[:, 0:1] * expert_out[0] + gates[:, 1:2] * expert_out[1]
    gate_grad = jnp.stack([jnp.sum(grad_out * expert_out[k], axis=-1) for k in range(2)], axis=1)
    pair_back = jax.vjp(gate_pair, picked)[1]
    grad_picked = pair_back(gate_grad)[0]
    grad_logits = jnp.sum(grad_picked[:, :, None] * chooser, axis=1)
    grad_router = jnp.einsum("re,rd->ed", grad_logits, normed_two_b.astype(f32), precision=HIGHEST)
    grad_normed = jnp.einsum("bts,bsd->btd", both_choose, returned, preferred_element_type=f32)
    grad_normed = grad_normed.reshape(count, D) + jnp.dot(
        grad_logits, router_b.astype(f32), precision=HIGHEST
    )
    norm_back_two = jax.vjp(norm_rows, resid, vector[5], vector[6])[1]
    grad_from_norm, grad_gain_two, grad_bias_two = norm_back_two(grad_normed)
    grad_resid = grad_out + grad_from_norm
    grad_branch_b = grad_resid.astype(b16)
    grad_out_proj = jnp.einsum("rd,re->de", context_b, grad_branch_b, preferred_element_type=f32)
    grad_context_b = (
        jnp.einsum("re,de->rd", grad_branch_b, weights_b[3], preferred_element_type=f32)
        .astype(b16)
        .reshape(head_shape)
    )
    scores = jnp.einsum("bqhe,bkhe->bhqk", queries, key_rows, preferred_element_type=f32) * scale
    scores = jnp.where(valid, scores, NEG_FILL)
    chance = jnp.exp(scores - log_total)
    chance_b = chance.astype(b16)
    grad_values = jnp.einsum(
        "bhqk,bqhe->bkhe", chance_b, grad_context_b, preferred_element_type=f32
    ).astype(b16)
    grad_chance = jnp.einsum("bqhe,bkhe->bhqk", grad_context_b, values, preferred_element_type=f32)
    grad_scores_b = (
        chance * (grad_chance - jnp.sum(chance * grad_chance, axis=-1, keepdims=True))
    ).astype(b16)
    grad_queries = (
        jnp.einsum("bhqk,bkhe->bqhe", grad_scores_b, key_rows, preferred_element_type=f32) * scale
    ).astype(b16)
    grad_keys = (
        jnp.einsum("bhqk,bqhe->bkhe", grad_scores_b, queries, preferred_element_type=f32) * scale
    ).astype(b16)
    grad_proj = jnp.stack([g.reshape(count, D) for g in (grad_queries, grad_keys, grad_values)])
    grad_in_proj = jnp.einsum("rd,jre->jde", normed_one_b, grad_proj, preferred_element_type=f32)
    grad_weights = jnp.concatenate([grad_in_proj, grad_out_proj[None]], axis=0)
    grad_normed_one = jnp.einsum("jre,jde->rd", grad_proj, weights_b[:3], preferred_element_type=f32)
    norm_back_one = jax.vjp(norm_rows, rows_in, vector[0], vector[1])[1]
    grad_from_first, grad_gain_one, grad_bias_one = norm_back_one(grad_normed_one)
    grad_vector = jnp.stack(
        [
            grad_gain_one,
            grad_bias_one,
            jnp.sum(grad_proj[0], axis=0, dtype=f32),
            jnp.sum(grad_proj[2], axis=0, dtype=f32),
            jnp.sum(grad_branch_b, axis=0, dtype=f32),
            grad_gain_two,
            grad_bias_two,
        ]
    )
    input_grad = grad_resid + grad_from_first

    small = jnp.concatenate([grad_vector, grad_router], axis=0).reshape(7 + experts, devices, cols)
    small = jnp.pad(small.transpose(1, 0, 2).reshape(devices, flat_len), ((0, 0), (0, extra * D - flat_len)))
    big = grad_weights.reshape(4, devices, cols, D).transpose(1, 0, 2, 3).reshape(devices, 4 * cols, D)
    packed = jnp.concatenate([big, small.reshape(devices, extra, D)], axis=1).astype(b16)
    packed = lax.psum_scatter(packed, both, scatter_dimension=0, tiled=False).astype(f32)
    shard_weights = packed[: 4 * cols].reshape(4, cols, D)
    small = packed[4 * cols :].reshape(extra * D)[:flat_len].reshape(7 + experts, cols)
    shard_vector, shard_router = small[:7], small[7:]

    params = (attention, gain_bias, router, expert_up, up_bias, expert_down, down_bias)
    grads = (shard_weights, shard_vector, shard_router, shard_up, shard_up_bias, shard_down, shard_down_bias)
    firsts = (first_attention, first_gain_bias, first_router, first_expert_up, first_up_bias, first_expert_down, first_down_bias)
    squares = (square_attention, square_gain_bias, square_router, square_expert_up, square_up_bias, square_expert_down, square_down_bias)
    hidden_units = n_dp * part
    rates = (1.6 * D ** (-0.5), 0.3, 0.5 * D ** (-0.5), 1.5 * D ** (-0.5), 0.25, 0.5 * hidden_units ** (-0.5), 0.25)
    updated = [adam_step(params[i], grads[i], firsts[i], squares[i], rates[i]) for i in range(7)]
    return (output, input_grad, *grads, *(u[0] for u in updated), *(u[1] for u in updated), *(u[2] for u in updated))


def solution(mesh):
    rows = P(("dp", "expert"), None)
    state = (
        P(None, ("dp", "expert"), None),
        P(None, ("dp", "expert")),
        P(None, ("dp", "expert")),
        P("expert", "dp", None),
        P("expert", "dp"),
        P("expert", "dp", None),
        P("expert", "dp"),
    )
    return jax.shard_map(
        body,
        mesh=mesh,
        in_specs=(rows, rows, rows, P(("dp", "expert")), *state, *state, *state),
        out_specs=(rows, rows, *state, *state, *state, *state),
        check_vma=False,
    )
```

```python
import functools
import math

import jax
import jax.numpy as jnp
from jax import lax
from jax.experimental import pallas as pl
from jax.experimental.pallas import tpu as pltpu
from jax.sharding import PartitionSpec as P

D = 768
HEADS = 12
HEAD_DIM = 64
LEN = 256
STEP = 3
ROWS = 256
BIAS_ROWS = 16

NORM_EPS = 1e-06
NEG_FILL = -1000000000.0
BETA_ONE = 0.9
BETA_TWO = 0.95
WEIGHT_DECAY = 0.1
ADAM_EPS = 1e-08
GELU_C = 0.7978845608028654
GELU_K = 0.044715
f32 = jnp.float32
b16 = jnp.bfloat16
MESH = pl.DeviceIdType.MESH


def adam_step(weight, grad, first, square, rate):
    new_first = BETA_ONE * first + (1.0 - BETA_ONE) * grad
    new_square = BETA_TWO * square + (1.0 - BETA_TWO) * grad * grad
    first_hat = new_first / (1.0 - BETA_ONE**STEP)
    square_hat = new_square / (1.0 - BETA_TWO**STEP)
    update = -rate * (first_hat / (jnp.sqrt(square_hat) + ADAM_EPS) + WEIGHT_DECAY * weight)
    return (weight + update, new_first, new_square)


def slots_of(routes, experts, capacity):
    flat = routes.reshape(-1, 2 * ROWS)
    onehot = (flat[:, :, None] == jnp.arange(experts, dtype=jnp.int32)).astype(b16)
    row = lax.broadcasted_iota(jnp.int32, (2 * ROWS, 2 * ROWS), 0)
    col = lax.broadcasted_iota(jnp.int32, (2 * ROWS, 2 * ROWS), 1)
    earlier = (col < row).astype(b16)
    before = jnp.einsum("ij,bje->bie", earlier, onehot, preferred_element_type=f32)
    slot = jnp.sum(before * onehot.astype(f32), axis=-1).astype(jnp.int32)
    return (flat * capacity + slot).reshape(-1, ROWS, 2)


def where_am_i():
    side = math.isqrt(lax.axis_size("expert") // 2)
    spot = lax.axis_index("expert")
    return side, lax.axis_index("dp"), spot // (2 * side), spot // 2 % side, spot % 2


def greet(peers):
    barrier = pltpu.get_barrier_semaphore()
    for peer in peers:
        pl.semaphore_signal(barrier, inc=1, device_id=peer, device_id_type=MESH)
    pl.semaphore_wait(barrier, len(peers))


def peers_of(n, side, z, y, x, core):
    def at(z_, y_, x_, core_):
        return (z_, (y_ * side + x_) * 2 + core_)

    along_z = [at((z + k) % n, y, x, core) for k in range(1, n)]
    first = [at(z, (y + core * k) % side, (x + (1 - core) * k) % side, core) for k in range(1, side)]
    second = [at(z, (y + (1 - core) * k) % side, (x + core * k) % side, core) for k in range(1, side)]
    return along_z, first, second, at(z, y, x, 1 - core)


def gather_kernel(n, in_ref, out_ref, local_sem, z_s, z_r, a_s, a_r, b_s, b_r, c_s, c_r):
    side, z, y, x, core = where_am_i()
    along_z, first, second, sibling = peers_of(n, side, z, y, x, core)
    greet([*along_z, *first, *second, sibling])

    def block(j, ka, kb, core_):
        y_ = (y - core * ka - (1 - core) * kb + 2 * side) % side
        x_ = (x - (1 - core) * ka - core * kb + 2 * side) % side
        return out_ref.at[((((z - j + n) % n) * side + y_) * side + x_) * 2 + core_]

    def remote(src, dst, send, recv, peer):
        return pltpu.make_async_remote_copy(
            src_ref=src, dst_ref=dst, send_sem=send, recv_sem=recv, device_id=peer, device_id_type=MESH
        )

    own = pltpu.make_async_copy(in_ref, block(0, 0, 0, core), local_sem)
    own.start()
    sent = []

    def pass_on(src, dst, j, ka, kb):
        if kb == 0:
            if ka == 0:
                for k in range(1, side):
                    copy = remote(src, dst, a_s.at[j * side + k], a_r.at[j * side + k], first[k - 1])
                    copy.start()
                    sent.append(copy)
            for k in range(1, side):
                place = (j * side + ka) * side + k
                copy = remote(src, dst, b_s.at[place], b_r.at[place], second[k - 1])
                copy.start()
                sent.append(copy)
        place = (j * side + kb) * side + ka
        copy = remote(src, dst, c_s.at[place], c_r.at[place], sibling)
        copy.start()
        sent.append(copy)

    for k in range(1, n):
        copy = remote(in_ref, block(0, 0, 0, core), z_s.at[k], z_r.at[k], along_z[k - 1])
        copy.start()
        sent.append(copy)
    pass_on(in_ref, block(0, 0, 0, core), 0, 0, 0)
    for j in range(1, n):
        here = block(j, 0, 0, core)
        remote(here, here, z_s.at[j], z_r.at[j], sibling).wait_recv()
        pass_on(here, here, j, 0, 0)
    for j in range(n):
        for ka in range(1, side):
            here = block(j, ka, 0, core)
            remote(here, here, a_s.at[j * side + ka], a_r.at[j * side + ka], sibling).wait_recv()
            pass_on(here, here, j, ka, 0)
    for j in range(n):
        for ka in range(side):
            for kb in range(1, side):
                here = block(j, ka, kb, core)
                place = (j * side + ka) * side + kb
                remote(here, here, b_s.at[place], b_r.at[place], sibling).wait_recv()
                pass_on(here, here, j, ka, kb)
    for j in range(n):
        for ka in range(side):
            for kb in range(side):
                here = block(j, ka, kb, 1 - core)
                place = (j * side + ka) * side + kb
                remote(here, here, c_s.at[place], c_r.at[place], sibling).wait_recv()
    for copy in sent:
        copy.wait_send()
    own.wait()


def gather_dense(packed, n, side):
    devices = n * side * side * 2
    sems = [
        pltpu.SemaphoreType.DMA,
        *[pltpu.SemaphoreType.DMA((n,))] * 2,
        *[pltpu.SemaphoreType.DMA((n * side,))] * 2,
        *[pltpu.SemaphoreType.DMA((n * side * side,))] * 4,
    ]
    size = devices * packed.size * 2
    return pl.pallas_call(
        functools.partial(gather_kernel, n),
        out_shape=jax.ShapeDtypeStruct((devices, *packed.shape), packed.dtype),
        in_specs=[pl.BlockSpec(memory_space=pltpu.VMEM)],
        out_specs=pl.BlockSpec(memory_space=pltpu.VMEM),
        scratch_shapes=sems,
        compiler_params=pltpu.CompilerParams(
            collective_id=0, has_side_effects=True, vmem_limit_bytes=size + (4 << 20)
        ),
        cost_estimate=CHEAP,
        name="gather_dense",
    )(packed)


def scatter_kernel(n, in_ref, out_ref, stage, c_buf, b_buf, a_buf, z_buf, c_s, c_r, b_s, b_r, a_s, a_r, z_s, z_r):
    side, z, y, x, core = where_am_i()
    along_z, first, second, sibling = peers_of(n, side, z, y, x, core)
    greet([*along_z, *first, *second, sibling])

    def piece(ka, kb, core_):
        y_ = (y + core * ka + (1 - core) * kb) % side
        x_ = (x + (1 - core) * ka + core * kb) % side
        return (core_ * side + y_) * side + x_

    def remote(src, dst, send, recv, peer):
        return pltpu.make_async_remote_copy(
            src_ref=src, dst_ref=dst, send_sem=send, recv_sem=recv, device_id=peer, device_id_type=MESH
        )

    sent = []

    def send(src, dst, send_sem, recv_sem, peer):
        copy = remote(src, dst, send_sem, recv_sem, peer)
        copy.start()
        sent.append(copy)

    order = [(ka, kb) for kb in [*range(1, side), 0] for ka in [*range(1, side), 0]]
    for ka, kb in order:
        place = ka * side + kb
        send(in_ref.at[piece(kb, ka, 1 - core)], c_buf.at[place], c_s.at[place], c_r.at[place], sibling)
    for ka, kb in order:
        place = ka * side + kb
        remote(c_buf.at[place], c_buf.at[place], c_s.at[place], c_r.at[place], sibling).wait_recv()
        mine = piece(ka, kb, core)
        if kb:
            stage[place] = (in_ref[mine].astype(f32) + c_buf[place].astype(f32)).astype(b16)
            slot = ka * side + kb
            send(stage.at[place], b_buf.at[slot], b_s.at[slot], b_r.at[slot], second[kb - 1])
        else:
            total = in_ref[mine].astype(f32) + c_buf[place].astype(f32)
            for k in range(1, side):
                slot = ka * side + k
                remote(b_buf.at[slot], b_buf.at[slot], b_s.at[slot], b_r.at[slot], sibling).wait_recv()
                total = total + b_buf[slot].astype(f32)
            if ka:
                stage[place] = total.astype(b16)
                send(stage.at[place], a_buf.at[ka], a_s.at[ka], a_r.at[ka], first[ka - 1])
            else:
                for k in range(1, side):
                    remote(a_buf.at[k], a_buf.at[k], a_s.at[k], a_r.at[k], sibling).wait_recv()
                    total = total + a_buf[k].astype(f32)
                stage[place] = total.astype(b16)
    for k in range(1, n):
        send(stage.at[0, (z + k) % n], z_buf.at[k], z_s.at[k], z_r.at[k], along_z[k - 1])
    result = stage[0, z].astype(f32)
    for k in range(1, n):
        remote(z_buf.at[k], z_buf.at[k], z_s.at[k], z_r.at[k], sibling).wait_recv()
        result = result + z_buf[k].astype(f32)
    out_ref[...] = result
    for copy in sent:
        copy.wait_send()


def scatter_dense(parts, n, side):
    rows, width = parts.shape[-2:]
    parts = parts.reshape(2 * side * side, n, rows, width)
    shape = (n, rows, width)
    dma = pltpu.SemaphoreType.DMA
    size = parts.size * 2
    return pl.pallas_call(
        functools.partial(scatter_kernel, n),
        out_shape=jax.ShapeDtypeStruct((rows, width), f32),
        in_specs=[pl.BlockSpec(memory_space=pltpu.VMEM)],
        out_specs=pl.BlockSpec(memory_space=pltpu.VMEM),
        scratch_shapes=[
            pltpu.VMEM((side * side, *shape), b16),
            pltpu.VMEM((side * side, *shape), b16),
            pltpu.VMEM((side * side, *shape), b16),
            pltpu.VMEM((side, *shape), b16),
            pltpu.VMEM((n, rows, width), b16),
            *[dma((side * side,))] * 4,
            *[dma((side,))] * 2,
            *[dma((n,))] * 2,
        ],
        compiler_params=pltpu.CompilerParams(
            collective_id=1, has_side_effects=True, vmem_limit_bytes=3 * size + (8 << 20)
        ),
        cost_estimate=CHEAP,
        name="scatter_dense",
    )(parts)


TILE = 512


def dot(a, b, contract):
    return lax.dot_general(a, b, (contract, ((), ())), preferred_element_type=f32)


NN = ((1,), (0,))
NT = ((1,), (1,))
TN = ((0,), (0,))


def expert_kernel(sources, first, last, part, *refs):
    refs = list(refs)
    weights = [refs.pop(0) for _ in range(sources)]
    x_ref, dout_ref, bias_ref = refs[:3]
    refs = refs[3:]
    sums = [None, None] if first else [refs.pop(0), refs.pop(0)]
    out_ref, grad_x_ref, grad_up_ref, grad_down_ref, w_ref, up_acc, down_acc, bias_acc, sem = refs
    step = pl.program_id(0)

    @pl.when(step == 0)
    def _():
        if sources == 1:
            copy = pltpu.make_async_copy(weights[0], w_ref, sem)
            copy.start()
            copy.wait()
        else:
            me = lax.axis_index("dp")
            inner = (me + 1) // 2 % 2

            @pl.when(inner == 1)
            def _():
                pltpu.make_async_copy(weights[0], w_ref, sem).start()

            @pl.when(inner == 0)
            def _():
                pltpu.make_async_copy(weights[1], w_ref, sem).start()

            pltpu.make_async_copy(weights[0], w_ref, sem).wait()
        up_acc[...] = jnp.zeros_like(up_acc)
        down_acc[...] = jnp.zeros_like(down_acc)
        bias_acc[...] = jnp.zeros_like(bias_acc)

    x = x_ref[...]
    dout = dout_ref[...]
    up = w_ref[:part]
    down = w_ref[part : 2 * part]
    up_bias = w_ref[2 * part :][0:1, :part].astype(f32)
    pre = dot(x, up, NT) + up_bias
    grad_hidden = dot(dout, down, NT)
    square = pre * pre
    inner = jnp.tanh(pre * (GELU_C + GELU_C * GELU_K * square))
    half = 0.5 * pre
    hidden = (half + half * inner).astype(b16)
    slope = 0.5 + 0.5 * inner + half * (1.0 - inner * inner) * (GELU_C + 3.0 * GELU_C * GELU_K * square)
    grad_pre = slope * grad_hidden
    grad_pre_b = grad_pre.astype(b16)
    out = dot(hidden, down, NN)
    grad_x = dot(grad_pre_b, up, NN)
    if not first:
        out = out + sums[0][...]
        grad_x = grad_x + sums[1][...]
    if last:
        out = out + bias_ref[1:2, :]
    out_ref[...] = out.astype(out_ref.dtype)
    grad_x_ref[...] = grad_x.astype(grad_x_ref.dtype)
    down_acc[...] += dot(hidden, dout, TN)
    up_acc[...] += dot(grad_pre_b, x, TN)
    bias_acc[0:1, :] += jnp.sum(grad_pre_b.astype(f32), axis=0, keepdims=True)

    @pl.when(step == pl.num_programs(0) - 1)
    def _():
        grad_up_ref[...] = up_acc[...].astype(grad_up_ref.dtype)
        grad_down_ref[:part] = down_acc[...].astype(grad_down_ref.dtype)
        row = lax.broadcasted_iota(jnp.int32, (BIAS_ROWS, D), 0)
        tail = jnp.where(row == 0, bias_acc[0:1, :], jnp.where(row == 1, bias_ref[0:1, :], 0.0))
        grad_down_ref[part:] = tail.astype(grad_down_ref.dtype)


def expert_part(weights, x, dout, biases, sums, last, grad_type, name):
    first = sums is None
    slots = x.shape[0]
    rows = weights[0].shape[0]
    part = (rows - BIAS_ROWS) // 2
    tile = pl.BlockSpec((TILE, D), lambda i: (i, 0))
    kept = b16 if last else f32
    n = len(weights)
    return pl.pallas_call(
        functools.partial(expert_kernel, n, first, last, part),
        grid=(slots // TILE,),
        in_specs=[
            *[pl.BlockSpec(memory_space=pl.ANY)] * n,
            tile,
            tile,
            pl.BlockSpec((2, D), lambda i: (0, 0)),
            *([] if first else [tile, tile]),
        ],
        out_specs=[
            tile,
            tile,
            pl.BlockSpec((part, D), lambda i: (0, 0)),
            pl.BlockSpec((part + BIAS_ROWS, D), lambda i: (0, 0)),
        ],
        out_shape=[
            jax.ShapeDtypeStruct((slots, D), kept),
            jax.ShapeDtypeStruct((slots, D), kept),
            jax.ShapeDtypeStruct((part, D), grad_type),
            jax.ShapeDtypeStruct((part + BIAS_ROWS, D), grad_type),
        ],
        scratch_shapes=[
            pltpu.VMEM((rows, D), b16),
            pltpu.VMEM((part, D), f32),
            pltpu.VMEM((part, D), f32),
            pltpu.VMEM((8, part), f32),
            pltpu.SemaphoreType.DMA,
        ],
        compiler_params=pltpu.CompilerParams(vmem_limit_bytes=56 << 20, dimension_semantics=("arbitrary",)),
        cost_estimate=pl.CostEstimate(flops=12 * slots * part * D, bytes_accessed=slots * D * 20, transcendentals=0),
        name=name,
    )(*weights, x, dout, biases, *([] if first else sums))


SCALE = HEAD_DIM ** (-0.5)
PAIRS = HEADS // 2
WIDE = 2 * HEAD_DIM
CHEAP = pl.CostEstimate(flops=0, bytes_accessed=1024, transcendentals=0)


def normal(values):
    center = values - jnp.mean(values, axis=-1, keepdims=True)
    rate = lax.rsqrt(jnp.mean(center * center, axis=-1, keepdims=True) + NORM_EPS)
    return center * rate, rate


def lanes_like(values):
    return lax.broadcasted_iota(jnp.int32, values.shape, values.ndim - 1)


def scores_of(part_q, pair_k, length):
    scores = dot(part_q, pair_k, NT) * SCALE
    return jnp.where(lanes_like(scores) < length, scores, NEG_FILL)


def halves(pair):
    low = lanes_like(pair) < HEAD_DIM
    zero = jnp.zeros_like(pair)
    return jnp.where(low, pair, zero), jnp.where(low, zero, pair)


def joined(even, odd):
    return jnp.where(lanes_like(even) < HEAD_DIM, even, odd)


def attention_kernel(
    lengths_ref, tokens_ref, weights_ref, vector_ref, router_ref, routes_ref, places_ref,
    normed_ref, q_ref, k_ref, v_ref, context_ref, lse_ref, resid_ref, normed_two_ref, gates_ref, slots_ref,
):
    length = lengths_ref[pl.program_id(0)]
    rows = tokens_ref[...].astype(f32)
    hat, _ = normal(rows)
    normed = (hat * vector_ref[0:1, :] + vector_ref[1:2, :]).astype(b16)
    normed_ref[...] = normed
    q_ref[...] = (dot(normed, weights_ref[0], NN) + vector_ref[2:3, :]).astype(b16)
    k_ref[...] = dot(normed, weights_ref[1], NN).astype(b16)
    v_ref[...] = (dot(normed, weights_ref[2], NN) + vector_ref[3:4, :]).astype(b16)
    lse = jnp.zeros((LEN, 128), f32)
    for pair in range(PAIRS):
        lanes = slice(pair * WIDE, (pair + 1) * WIDE)
        keys, values = k_ref[:, lanes], v_ref[:, lanes]
        mixed = []
        for half, part in enumerate(halves(q_ref[:, lanes])):
            scores = scores_of(part, keys, length)
            top = jnp.max(scores, axis=-1, keepdims=True)
            total = top + jnp.log(jnp.sum(jnp.exp(scores - top), axis=-1, keepdims=True))
            chance = jnp.exp(scores - total).astype(b16)
            mixed.append(dot(chance, values, NN))
            lse = jnp.where(lanes_like(lse) == 2 * pair + half, total, lse)
        context_ref[:, lanes] = joined(*mixed).astype(b16)
    lse_ref[...] = lse
    resid = rows + (dot(context_ref[...], weights_ref[3], NN) + vector_ref[4:5, :])
    resid_ref[...] = resid
    hat, _ = normal(resid)
    normed_two = (hat * vector_ref[5:6, :] + vector_ref[6:7, :]).astype(b16)
    normed_two_ref[...] = normed_two
    logits = dot(normed_two, router_ref[...], NT)
    names = lanes_like(logits)
    first = jnp.sum(jnp.where(names == routes_ref[:, 0:1], logits, 0.0), axis=-1, keepdims=True)
    second = jnp.sum(jnp.where(names == routes_ref[:, 1:2], logits, 0.0), axis=-1, keepdims=True)
    gate = lanes_like(gates_ref[...])
    gates_ref[...] = jnp.where(gate == 0, jax.nn.sigmoid(first - second), jax.nn.sigmoid(second - first))
    experts, _, capacity, _ = slots_ref.shape
    slots = experts * capacity
    ids = lax.broadcasted_iota(jnp.int32, (slots, ROWS), 0)
    places = places_ref[0]
    chosen = jnp.where((ids == places[0:1, :]) | (ids == places[1:2, :]), 1.0, 0.0).astype(b16)
    sent = dot(chosen, normed_two, NN).astype(b16)
    slots_ref[...] = sent.reshape(experts, 1, capacity, D)


def attention_forward(lengths, tokens, weights, vector, router, routes, places, experts, capacity):
    count = tokens.shape[0]
    rows = pl.BlockSpec((LEN, D), lambda i: (i, 0))
    lanes = pl.BlockSpec((LEN, 128), lambda i: (i, 0))
    once = pl.Buffered(1)
    return pl.pallas_call(
        attention_kernel,
        grid=(count // LEN,),
        in_specs=[
            pl.BlockSpec(memory_space=pltpu.SMEM),
            rows,
            pl.BlockSpec((4, D, D), lambda i: (0, 0, 0), pipeline_mode=once),
            pl.BlockSpec((8, D), lambda i: (0, 0)),
            pl.BlockSpec((128, D), lambda i: (0, 0)),
            pl.BlockSpec((LEN, 2), lambda i: (i, 0)),
            pl.BlockSpec((1, 2, ROWS), lambda i: (i, 0, 0)),
        ],
        out_specs=[
            rows, rows, rows, rows, rows, lanes, rows, rows, lanes,
            pl.BlockSpec((experts, 1, capacity, D), lambda i: (0, i, 0, 0)),
        ],
        out_shape=[
            *[jax.ShapeDtypeStruct((count, D), b16)] * 5,
            jax.ShapeDtypeStruct((count, 128), f32),
            jax.ShapeDtypeStruct((count, D), f32),
            jax.ShapeDtypeStruct((count, D), b16),
            jax.ShapeDtypeStruct((count, 128), f32),
            jax.ShapeDtypeStruct((experts, count // ROWS, capacity, D), b16),
        ],
        compiler_params=pltpu.CompilerParams(vmem_limit_bytes=48 << 20),
        cost_estimate=CHEAP,
        name="attention_forward",
    )(lengths, tokens, weights, vector, router, routes, places)


def norm_back(grad, hat, rate, gain):
    inner = grad * gain
    return rate * (
        inner
        - jnp.mean(inner, axis=-1, keepdims=True)
        - hat * jnp.mean(inner * hat, axis=-1, keepdims=True)
    )


def two_terms(values):
    high = values.astype(b16)
    return high, (values - high.astype(f32)).astype(b16)


def column_sum(values):
    return jnp.sum(values, axis=0, keepdims=True)


def backward_kernel(
    lengths_ref, tokens_ref, grad_ref, weights_ref, vector_ref, router_ref, routes_ref, places_ref,
    normed_ref, q_ref, k_ref, v_ref, context_ref, lse_ref, resid_ref, normed_two_ref, gates_ref, outs_ref, returned_ref,
    output_ref, input_grad_ref, grad_weights_ref, grad_vector_ref, grad_router_ref,
    weights_acc, vector_acc, router_acc, dq_ref, dk_ref, dv_ref,
):
    step = pl.program_id(0)
    length = lengths_ref[step]

    @pl.when(step == 0)
    def _():
        weights_acc[...] = jnp.zeros_like(weights_acc)
        vector_acc[...] = jnp.zeros_like(vector_acc)
        router_acc[...] = jnp.zeros_like(router_acc)

    slots = outs_ref.shape[0] * outs_ref.shape[2]
    ids = lax.broadcasted_iota(jnp.int32, (ROWS, slots), 1)
    outs = outs_ref[...].reshape(slots, D)
    returned = returned_ref[...].reshape(slots, D)
    grad_out = grad_ref[...].astype(f32)
    take = [jnp.where(ids == places_ref[:, k : k + 1], 1.0, 0.0).astype(b16) for k in range(2)]
    out = [dot(t, outs, NN) for t in take]
    gates = [gates_ref[:, k : k + 1] for k in range(2)]
    resid = resid_ref[...]
    output_ref[...] = resid + gates[0] * out[0] + gates[1] * out[1]
    slopes = [
        jnp.sum(grad_out * out[k], axis=-1, keepdims=True) * (gates[k] * (1.0 - gates[k])) for k in range(2)
    ]
    pull = slopes[0] - slopes[1]
    names = lax.broadcasted_iota(jnp.int32, (ROWS, 128), 1)
    grad_logits = jnp.where(names == routes_ref[:, 0:1], pull, jnp.where(names == routes_ref[:, 1:2], -pull, 0.0))
    high, low = two_terms(grad_logits)
    normed_two = normed_two_ref[...]
    router = router_ref[...]
    router_acc[...] += dot(high, normed_two, TN) + dot(low, normed_two, TN)
    grad_two = dot(take[0] + take[1], returned, NN) + (dot(high, router, NN) + dot(low, router, NN))
    hat, rate = normal(resid)
    vector_acc[5:6, :] += column_sum(grad_two * hat)
    vector_acc[6:7, :] += column_sum(grad_two)
    grad_resid = grad_out + norm_back(grad_two, hat, rate, vector_ref[5:6, :])
    input_grad_ref[...] = grad_resid
    branch = grad_resid.astype(b16)
    vector_acc[4:5, :] += column_sum(branch.astype(f32))
    weights_acc[3] += dot(context_ref[...], branch, TN)
    grad_context = dot(branch, weights_ref[3], NT).astype(b16)
    for pair in range(PAIRS):
        lanes = slice(pair * WIDE, (pair + 1) * WIDE)
        queries, keys, values = q_ref[:, lanes], k_ref[:, lanes], v_ref[:, lanes]
        given = grad_context[:, lanes]
        grads = []
        for half, (part, part_given) in enumerate(zip(halves(queries), halves(given))):
            head = 2 * pair + half
            chance = jnp.exp(scores_of(part, keys, length) - lse_ref[:, head : head + 1])
            grad_v = dot(chance.astype(b16), given, TN)
            grad_chance = dot(part_given, values, NT)
            mean = jnp.sum(chance * grad_chance, axis=-1, keepdims=True)
            grad_scores = (chance * (grad_chance - mean)).astype(b16)
            grads.append((dot(grad_scores, keys, NN), dot(grad_scores, queries, TN), grad_v))
        dq_ref[:, lanes] = (joined(grads[0][0], grads[1][0]) * SCALE).astype(b16)
        dk_ref[:, lanes] = (joined(grads[0][1], grads[1][1]) * SCALE).astype(b16)
        dv_ref[:, lanes] = joined(grads[0][2], grads[1][2]).astype(b16)
    normed = normed_ref[...]
    grad_one = jnp.zeros((LEN, D), f32)
    for k, ref in enumerate((dq_ref, dk_ref, dv_ref)):
        weights_acc[k] += dot(normed, ref[...], TN)
        grad_one += dot(ref[...], weights_ref[k], NT)
    vector_acc[2:3, :] += column_sum(dq_ref[...].astype(f32))
    vector_acc[3:4, :] += column_sum(dv_ref[...].astype(f32))
    hat, rate = normal(tokens_ref[...].astype(f32))
    vector_acc[0:1, :] += column_sum(grad_one * hat)
    vector_acc[1:2, :] += column_sum(grad_one)
    input_grad_ref[...] += norm_back(grad_one, hat, rate, vector_ref[0:1, :])

    @pl.when(step == pl.num_programs(0) - 1)
    def _():
        for k in range(4):
            grad_weights_ref[k] = weights_acc[k].astype(b16)
        grad_vector_ref[...] = vector_acc[...]
        grad_router_ref[...] = router_acc[...]


def attention_backward(lengths, tokens, out_grad, weights, vector, router, routes, places, kept, outs, returned):
    count = tokens.shape[0]
    experts, _, capacity, _ = outs.shape
    rows = pl.BlockSpec((LEN, D), lambda i: (i, 0))
    lanes = pl.BlockSpec((LEN, 128), lambda i: (i, 0))
    pairs = pl.BlockSpec((LEN, 2), lambda i: (i, 0))
    slots = pl.BlockSpec((experts, 1, capacity, D), lambda i: (0, i, 0, 0))

    def fixed(*shape):
        return pl.BlockSpec(shape, lambda i: (0,) * len(shape), pipeline_mode=pl.Buffered(1))

    return pl.pallas_call(
        backward_kernel,
        grid=(count // LEN,),
        in_specs=[
            pl.BlockSpec(memory_space=pltpu.SMEM),
            rows, rows, fixed(4, D, D), fixed(8, D), fixed(128, D), pairs, pairs,
            rows, rows, rows, rows, rows, lanes, rows, rows, lanes, slots, slots,
        ],
        out_specs=[rows, rows, fixed(4, D, D), fixed(8, D), fixed(128, D)],
        out_shape=[
            jax.ShapeDtypeStruct((count, D), f32),
            jax.ShapeDtypeStruct((count, D), f32),
            jax.ShapeDtypeStruct((4, D, D), b16),
            jax.ShapeDtypeStruct((8, D), f32),
            jax.ShapeDtypeStruct((128, D), f32),
        ],
        scratch_shapes=[
            pltpu.VMEM((4, D, D), f32),
            pltpu.VMEM((8, D), f32),
            pltpu.VMEM((128, D), f32),
            *[pltpu.VMEM((LEN, D), b16)] * 3,
        ],
        compiler_params=pltpu.CompilerParams(vmem_limit_bytes=58 << 20),
        cost_estimate=CHEAP,
        name="attention_backward",
    )(lengths, tokens, out_grad, weights, vector, router, routes, places, *kept, outs, returned)


def pack_expert(up, down, up_bias, down_bias, dtype):
    part = up.shape[0]
    tail = jnp.zeros((BIAS_ROWS, D), dtype)
    tail = tail.at[0, :part].set(up_bias.astype(dtype))
    tail = tail.at[1, : down_bias.shape[0]].set(down_bias.astype(dtype))
    return jnp.concatenate([up.astype(dtype), down.astype(dtype), tail], axis=0)


def after(x, *others):
    return lax.optimization_barrier((x, *others))[0]


def along(x, *pairs):
    return lax.ppermute(x, "dp", pairs)


def body(
    tokens, out_grad, routes, lengths,
    attention, gain_bias, router, expert_up, up_bias, expert_down, down_bias,
    first_attention, first_gain_bias, first_router, first_expert_up, first_up_bias, first_expert_down, first_down_bias,
    square_attention, square_gain_bias, square_router, square_expert_up, square_up_bias, square_expert_down, square_down_bias,
):
    experts = router.shape[0]
    capacity = 4 * ROWS // experts
    count = tokens.shape[0]
    blocks = count // ROWS
    part = expert_up.shape[1]
    narrow = down_bias.shape[1]
    cols = attention.shape[1]
    devices = D // cols
    n_dp = lax.axis_size("dp")
    assert n_dp == 4 and expert_up.shape[0] == 1
    me = lax.axis_index("dp")
    mine = lax.axis_index("expert")
    both = ("dp", "expert")

    flat_len = (7 + experts) * cols
    extra = -(-(4 * cols + -(-flat_len // D)) // 16) * 16 - 4 * cols
    side = math.isqrt(experts // 2)
    small = jnp.concatenate([gain_bias, router], axis=0).astype(b16).reshape(-1)
    small = jnp.pad(small, (0, extra * D - flat_len)).reshape(extra, D)
    packed = jnp.concatenate([attention.astype(b16).reshape(4 * cols, D), small], axis=0)
    whole = gather_dense(packed, n_dp, side)
    own = after(pack_expert(expert_up[0], expert_down[0], up_bias[0], down_bias[0], b16), whole)

    second = along(own, (0, 1), (1, 0), (2, 3), (3, 2))
    third_inner = along(own, (1, 2), (2, 1))
    third_outer = along(third_inner, (1, 0), (2, 3))
    fourth_inner = along(second, (1, 2), (2, 1))
    fourth_outer = along(fourth_inner, (1, 0), (2, 3))

    weights_b = whole[:, : 4 * cols].reshape(devices, 4, cols, D).transpose(1, 0, 2, 3).reshape(4, D, D)
    small = whole[:, 4 * cols :].reshape(devices, extra * D)[:, :flat_len].reshape(devices, 7 + experts, cols)
    small = small.transpose(1, 0, 2).reshape(7 + experts, D)
    vector = small[:7].astype(f32)
    router_b = small[7:]

    positions = slots_of(routes, experts, capacity)
    slot_ids = jnp.arange(experts * capacity, dtype=jnp.int32)
    hit = positions[:, :, :, None] == slot_ids
    split = jnp.any(hit, axis=2).astype(b16).reshape(blocks, ROWS, experts, capacity)
    other = jnp.flip(routes, axis=1).reshape(blocks, ROWS, 2)
    partner = jnp.sum(jnp.where(hit, other[:, :, :, None], 0), axis=(1, 2)).astype(f32)
    partner = partner.reshape(blocks, experts, capacity).transpose(1, 0, 2)
    partner = lax.all_to_all(partner, "expert", split_axis=0, concat_axis=0, tiled=True)
    grad_rows = out_grad.reshape(blocks, ROWS, D)

    sent = jnp.einsum("btec,btd->ebcd", split, grad_rows, preferred_element_type=f32).astype(b16)
    sent = after(sent, whole)
    grad_slots = lax.all_to_all(sent, "expert", split_axis=0, concat_axis=0, tiled=True)
    grad_slots = grad_slots.reshape(experts * blocks * capacity, D)

    router_all = jnp.pad(router_b, ((0, 128 - experts), (0, 0)))
    vector_all = jnp.pad(vector, ((0, 1), (0, 0)))
    *kept, slots_out = attention_forward(
        lengths, tokens, weights_b, vector_all, router_all, routes, positions.transpose(0, 2, 1), experts, capacity
    )

    def exchange(sent):
        return lax.all_to_all(sent, "expert", split_axis=0, concat_axis=0, tiled=True)

    slots_in = exchange(after(slots_out, grad_slots)).reshape(experts * blocks * capacity, D)

    slot_logits = jnp.einsum("sd,ed->se", slots_in, router_b, preferred_element_type=f32)
    ids = jnp.arange(experts, dtype=jnp.int32)
    rival = partner.reshape(-1).astype(jnp.int32)
    margin = jnp.sum(
        slot_logits * ((ids == mine).astype(f32) - (rival[:, None] == ids).astype(f32)), axis=-1
    )
    dout = (jax.nn.sigmoid(margin)[:, None] * grad_slots.astype(f32)).astype(b16)
    grad_down_bias = jnp.sum(dout.astype(f32), axis=0)

    def pick(*arrays):
        out = arrays[-1]
        for i in range(len(arrays) - 2, -1, -1):
            out = jnp.where(me == i, arrays[i], out)
        return out

    inner = (me == 1) | (me == 2)
    tail = 2 * part + 1
    names = [me, pick(1, 0, 3, 2), pick(2, 2, 1, 1), pick(3, 3, 0, 0)]
    bias_rows = [
        own[tail, :narrow],
        second[tail, :narrow],
        jnp.where(inner, third_inner[tail, :narrow], third_outer[tail, :narrow]),
        jnp.where(inner, fourth_inner[tail, :narrow], fourth_outer[tail, :narrow]),
    ]
    place = jnp.stack(names)
    down_bias_full = jnp.zeros((n_dp, narrow), b16).at[place].set(jnp.stack(bias_rows)).reshape(D)
    weights = [(own,), (second,), (third_inner, third_outer), (fourth_inner, fourth_outer)]
    sums = None
    part_grads = []
    for i in range(4):
        share = lax.dynamic_slice(grad_down_bias, (names[i] * narrow,), (narrow,))
        share = jnp.pad(share, (0, D - narrow))
        biases = jnp.stack([share, down_bias_full.astype(f32) if i == 3 else share])
        *sums, grad_up, grad_down = expert_part(
            weights[i], slots_in, dout, biases, sums, i == 3, b16 if i else f32, f"expert_part_{i}"
        )
        part_grads.append((grad_up, grad_down))
    out_b, grad_b = sums

    back = exchange(out_b.reshape(experts, blocks, capacity, D))
    returned = exchange(grad_b.reshape(experts, blocks, capacity, D))

    def add(a, b):
        return (a.astype(f32) + b.astype(f32)).astype(b16)

    both_halves = range(2)
    nearest, middle, far = ([part_grads[k][i] for i in both_halves] for k in (1, 2, 3))
    near = [along(nearest[i], (0, 1), (3, 2)) for i in both_halves]
    mid = [along(after(middle[i], near[i]), (0, 1), (3, 2)) for i in both_halves]
    end = [along(after(far[i], mid[i]), (0, 1), (3, 2)) for i in both_halves]
    mid = [along(add(middle[i], mid[i]), (1, 2), (2, 1)) for i in both_halves]
    end = [along(add(far[i], end[i]), (1, 2), (2, 1)) for i in both_halves]
    end = [along(add(nearest[i], end[i]), (1, 0), (2, 3)) for i in both_halves]
    totals = [
        part_grads[0][i] + (near[i].astype(f32) + mid[i].astype(f32) + end[i].astype(f32)) for i in both_halves
    ]
    shard_up = totals[0][None]
    shard_down = totals[1][:part][None]
    shard_up_bias = totals[1][part, :part][None]
    shard_down_bias = totals[1][part + 1, :narrow][None]

    output, input_grad, grad_weights, grad_vector, grad_router = attention_backward(
        lengths, tokens, out_grad, weights_b, vector_all, router_all, routes, positions.reshape(count, 2), kept, back, returned
    )

    small = jnp.concatenate([grad_vector[:7], grad_router[:experts]], axis=0).reshape(7 + experts, devices, cols)
    small = jnp.pad(small.transpose(1, 0, 2).reshape(devices, flat_len), ((0, 0), (0, extra * D - flat_len)))
    big = grad_weights.reshape(4, devices, cols, D).transpose(1, 0, 2, 3).reshape(devices, 4 * cols, D)
    packed = jnp.concatenate([big, small.reshape(devices, extra, D).astype(b16)], axis=1)
    packed = packed.reshape(n_dp, side, side, 2, 4 * cols + extra, D).transpose(3, 1, 2, 0, 4, 5)
    packed = scatter_dense(packed, n_dp, side)
    shard_weights = packed[: 4 * cols].reshape(4, cols, D)
    small = packed[4 * cols :].reshape(extra * D)[:flat_len].reshape(7 + experts, cols)
    shard_vector, shard_router = small[:7], small[7:]

    params = (attention, gain_bias, router, expert_up, up_bias, expert_down, down_bias)
    grads = (shard_weights, shard_vector, shard_router, shard_up, shard_up_bias, shard_down, shard_down_bias)
    firsts = (first_attention, first_gain_bias, first_router, first_expert_up, first_up_bias, first_expert_down, first_down_bias)
    squares = (square_attention, square_gain_bias, square_router, square_expert_up, square_up_bias, square_expert_down, square_down_bias)
    hidden_units = n_dp * part
    rates = (1.6 * D ** (-0.5), 0.3, 0.5 * D ** (-0.5), 1.5 * D ** (-0.5), 0.25, 0.5 * hidden_units ** (-0.5), 0.25)
    updated = [adam_step(params[i], grads[i], firsts[i], squares[i], rates[i]) for i in range(7)]
    return (output, input_grad, *grads, *(u[0] for u in updated), *(u[1] for u in updated), *(u[2] for u in updated))


def solution(mesh):
    rows = P(("dp", "expert"), None)
    state = (
        P(None, ("dp", "expert"), None),
        P(None, ("dp", "expert")),
        P(None, ("dp", "expert")),
        P("expert", "dp", None),
        P("expert", "dp"),
        P("expert", "dp", None),
        P("expert", "dp"),
    )
    return jax.shard_map(
        body,
        mesh=mesh,
        in_specs=(rows, rows, rows, P(("dp", "expert")), *state, *state, *state),
        out_specs=(rows, rows, *state, *state, *state, *state),
        check_vma=False,
    )
```

```python
import functools
import math

import jax
import jax.numpy as jnp
from jax import lax
from jax.experimental import pallas as pl
from jax.experimental.pallas import tpu as pltpu
from jax.sharding import PartitionSpec as P

D = 768
HEADS = 12
HEAD_DIM = 64
LEN = 256
STEP = 3
ROWS = 256
BIAS_ROWS = 16

NORM_EPS = 1e-06
NEG_FILL = -1000000000.0
BETA_ONE = 0.9
BETA_TWO = 0.95
WEIGHT_DECAY = 0.1
ADAM_EPS = 1e-08
GELU_C = 0.7978845608028654
GELU_K = 0.044715
f32 = jnp.float32
b16 = jnp.bfloat16
MESH = pl.DeviceIdType.MESH


def adam_step(weight, grad, first, square, rate):
    new_first = BETA_ONE * first + (1.0 - BETA_ONE) * grad
    new_square = BETA_TWO * square + (1.0 - BETA_TWO) * grad * grad
    first_hat = new_first / (1.0 - BETA_ONE**STEP)
    square_hat = new_square / (1.0 - BETA_TWO**STEP)
    update = -rate * (first_hat / (jnp.sqrt(square_hat) + ADAM_EPS) + WEIGHT_DECAY * weight)
    return (weight + update, new_first, new_square)


def slots_of(routes, experts, capacity):
    flat = routes.reshape(-1, 2 * ROWS)
    onehot = (flat[:, :, None] == jnp.arange(experts, dtype=jnp.int32)).astype(b16)
    row = lax.broadcasted_iota(jnp.int32, (2 * ROWS, 2 * ROWS), 0)
    col = lax.broadcasted_iota(jnp.int32, (2 * ROWS, 2 * ROWS), 1)
    earlier = (col < row).astype(b16)
    before = jnp.einsum("ij,bje->bie", earlier, onehot, preferred_element_type=f32)
    slot = jnp.sum(before * onehot.astype(f32), axis=-1).astype(jnp.int32)
    return (flat * capacity + slot).reshape(-1, ROWS, 2)


def where_am_i():
    side = math.isqrt(lax.axis_size("expert") // 2)
    spot = lax.axis_index("expert")
    return side, lax.axis_index("dp"), spot // (2 * side), spot // 2 % side, spot % 2


def greet(peers):
    barrier = pltpu.get_barrier_semaphore()
    for peer in peers:
        pl.semaphore_signal(barrier, inc=1, device_id=peer, device_id_type=MESH)
    pl.semaphore_wait(barrier, len(peers))


def peers_of(n, side, z, y, x, core):
    def at(z_, y_, x_, core_):
        return (z_, (y_ * side + x_) * 2 + core_)

    along_z = [at((z + k) % n, y, x, core) for k in range(1, n)]
    first = [at(z, (y + core * k) % side, (x + (1 - core) * k) % side, core) for k in range(1, side)]
    second = [at(z, (y + (1 - core) * k) % side, (x + core * k) % side, core) for k in range(1, side)]
    return along_z, first, second, at(z, y, x, 1 - core)


def gather_kernel(n, in_ref, out_ref, local_sem, z_s, z_r, a_s, a_r, b_s, b_r, c_s, c_r):
    side, z, y, x, core = where_am_i()
    along_z, first, second, sibling = peers_of(n, side, z, y, x, core)
    greet([*along_z, *first, *second, sibling])

    def block(j, ka, kb, core_):
        y_ = (y - core * ka - (1 - core) * kb + 2 * side) % side
        x_ = (x - (1 - core) * ka - core * kb + 2 * side) % side
        return out_ref.at[((((z - j + n) % n) * side + y_) * side + x_) * 2 + core_]

    def remote(src, dst, send, recv, peer):
        return pltpu.make_async_remote_copy(
            src_ref=src, dst_ref=dst, send_sem=send, recv_sem=recv, device_id=peer, device_id_type=MESH
        )

    own = pltpu.make_async_copy(in_ref, block(0, 0, 0, core), local_sem)
    own.start()
    sent = []

    def pass_on(src, dst, j, ka, kb):
        if kb == 0:
            if ka == 0:
                for k in range(1, side):
                    copy = remote(src, dst, a_s.at[j * side + k], a_r.at[j * side + k], first[k - 1])
                    copy.start()
                    sent.append(copy)
            for k in range(1, side):
                place = (j * side + ka) * side + k
                copy = remote(src, dst, b_s.at[place], b_r.at[place], second[k - 1])
                copy.start()
                sent.append(copy)
        place = (j * side + kb) * side + ka
        copy = remote(src, dst, c_s.at[place], c_r.at[place], sibling)
        copy.start()
        sent.append(copy)

    for k in range(1, n):
        copy = remote(in_ref, block(0, 0, 0, core), z_s.at[k], z_r.at[k], along_z[k - 1])
        copy.start()
        sent.append(copy)
    pass_on(in_ref, block(0, 0, 0, core), 0, 0, 0)
    for j in range(1, n):
        here = block(j, 0, 0, core)
        remote(here, here, z_s.at[j], z_r.at[j], sibling).wait_recv()
        pass_on(here, here, j, 0, 0)
    for j in range(n):
        for ka in range(1, side):
            here = block(j, ka, 0, core)
            remote(here, here, a_s.at[j * side + ka], a_r.at[j * side + ka], sibling).wait_recv()
            pass_on(here, here, j, ka, 0)
    for j in range(n):
        for ka in range(side):
            for kb in range(1, side):
                here = block(j, ka, kb, core)
                place = (j * side + ka) * side + kb
                remote(here, here, b_s.at[place], b_r.at[place], sibling).wait_recv()
                pass_on(here, here, j, ka, kb)
    for j in range(n):
        for ka in range(side):
            for kb in range(side):
                here = block(j, ka, kb, 1 - core)
                place = (j * side + ka) * side + kb
                remote(here, here, c_s.at[place], c_r.at[place], sibling).wait_recv()
    for copy in sent:
        copy.wait_send()
    own.wait()


def gather_dense(packed, n, side):
    devices = n * side * side * 2
    sems = [
        pltpu.SemaphoreType.DMA,
        *[pltpu.SemaphoreType.DMA((n,))] * 2,
        *[pltpu.SemaphoreType.DMA((n * side,))] * 2,
        *[pltpu.SemaphoreType.DMA((n * side * side,))] * 4,
    ]
    size = devices * packed.size * 2
    return pl.pallas_call(
        functools.partial(gather_kernel, n),
        out_shape=jax.ShapeDtypeStruct((devices, *packed.shape), packed.dtype),
        in_specs=[pl.BlockSpec(memory_space=pltpu.VMEM)],
        out_specs=pl.BlockSpec(memory_space=pltpu.VMEM),
        scratch_shapes=sems,
        compiler_params=pltpu.CompilerParams(
            collective_id=0, has_side_effects=True, vmem_limit_bytes=size + (4 << 20)
        ),
        cost_estimate=CHEAP,
        name="gather_dense",
    )(packed)


def scatter_kernel(n, in_ref, out_ref, stage, c_buf, b_buf, a_buf, z_buf, c_s, c_r, b_s, b_r, a_s, a_r, z_s, z_r):
    side, z, y, x, core = where_am_i()
    along_z, first, second, sibling = peers_of(n, side, z, y, x, core)
    greet([*along_z, *first, *second, sibling])

    def piece(ka, kb, core_):
        y_ = (y + core * ka + (1 - core) * kb) % side
        x_ = (x + (1 - core) * ka + core * kb) % side
        return (core_ * side + y_) * side + x_

    def remote(src, dst, send, recv, peer):
        return pltpu.make_async_remote_copy(
            src_ref=src, dst_ref=dst, send_sem=send, recv_sem=recv, device_id=peer, device_id_type=MESH
        )

    sent = []

    def send(src, dst, send_sem, recv_sem, peer):
        copy = remote(src, dst, send_sem, recv_sem, peer)
        copy.start()
        sent.append(copy)

    order = [(ka, kb) for kb in [*range(1, side), 0] for ka in [*range(1, side), 0]]
    for ka, kb in order:
        place = ka * side + kb
        send(in_ref.at[piece(kb, ka, 1 - core)], c_buf.at[place], c_s.at[place], c_r.at[place], sibling)
    for ka, kb in order:
        place = ka * side + kb
        remote(c_buf.at[place], c_buf.at[place], c_s.at[place], c_r.at[place], sibling).wait_recv()
        mine = piece(ka, kb, core)
        if kb:
            stage[place] = (in_ref[mine].astype(f32) + c_buf[place].astype(f32)).astype(b16)
            slot = ka * side + kb
            send(stage.at[place], b_buf.at[slot], b_s.at[slot], b_r.at[slot], second[kb - 1])
        else:
            total = in_ref[mine].astype(f32) + c_buf[place].astype(f32)
            for k in range(1, side):
                slot = ka * side + k
                remote(b_buf.at[slot], b_buf.at[slot], b_s.at[slot], b_r.at[slot], sibling).wait_recv()
                total = total + b_buf[slot].astype(f32)
            if ka:
                stage[place] = total.astype(b16)
                send(stage.at[place], a_buf.at[ka], a_s.at[ka], a_r.at[ka], first[ka - 1])
            else:
                for k in range(1, side):
                    remote(a_buf.at[k], a_buf.at[k], a_s.at[k], a_r.at[k], sibling).wait_recv()
                    total = total + a_buf[k].astype(f32)
                stage[place] = total.astype(b16)
    for k in range(1, n):
        send(stage.at[0, (z + k) % n], z_buf.at[k], z_s.at[k], z_r.at[k], along_z[k - 1])
    result = stage[0, z].astype(f32)
    for k in range(1, n):
        remote(z_buf.at[k], z_buf.at[k], z_s.at[k], z_r.at[k], sibling).wait_recv()
        result = result + z_buf[k].astype(f32)
    out_ref[...] = result
    for copy in sent:
        copy.wait_send()


def scatter_dense(parts, n, side):
    rows, width = parts.shape[-2:]
    parts = parts.reshape(2 * side * side, n, rows, width)
    shape = (n, rows, width)
    dma = pltpu.SemaphoreType.DMA
    size = parts.size * 2
    return pl.pallas_call(
        functools.partial(scatter_kernel, n),
        out_shape=jax.ShapeDtypeStruct((rows, width), f32),
        in_specs=[pl.BlockSpec(memory_space=pltpu.VMEM)],
        out_specs=pl.BlockSpec(memory_space=pltpu.VMEM),
        scratch_shapes=[
            pltpu.VMEM((side * side, *shape), b16),
            pltpu.VMEM((side * side, *shape), b16),
            pltpu.VMEM((side * side, *shape), b16),
            pltpu.VMEM((side, *shape), b16),
            pltpu.VMEM((n, rows, width), b16),
            *[dma((side * side,))] * 4,
            *[dma((side,))] * 2,
            *[dma((n,))] * 2,
        ],
        compiler_params=pltpu.CompilerParams(
            collective_id=1, has_side_effects=True, vmem_limit_bytes=3 * size + (8 << 20)
        ),
        cost_estimate=CHEAP,
        name="scatter_dense",
    )(parts)


TILE = 512


def dot(a, b, contract):
    return lax.dot_general(a, b, (contract, ((), ())), preferred_element_type=f32)


NN = ((1,), (0,))
NT = ((1,), (1,))
TN = ((0,), (0,))


def expert_kernel(sources, first, last, part, *refs):
    refs = list(refs)
    weights = [refs.pop(0) for _ in range(sources)]
    x_ref, dout_ref, bias_ref = refs[:3]
    refs = refs[3:]
    sums = [None, None] if first else [refs.pop(0), refs.pop(0)]
    out_ref, grad_x_ref, grad_up_ref, grad_down_ref, w_ref, up_acc, down_acc, bias_acc, sem = refs
    step = pl.program_id(0)

    @pl.when(step == 0)
    def _():
        if sources == 1:
            copy = pltpu.make_async_copy(weights[0], w_ref, sem)
            copy.start()
            copy.wait()
        else:
            me = lax.axis_index("dp")
            inner = (me + 1) // 2 % 2

            @pl.when(inner == 1)
            def _():
                pltpu.make_async_copy(weights[0], w_ref, sem).start()

            @pl.when(inner == 0)
            def _():
                pltpu.make_async_copy(weights[1], w_ref, sem).start()

            pltpu.make_async_copy(weights[0], w_ref, sem).wait()
        up_acc[...] = jnp.zeros_like(up_acc)
        down_acc[...] = jnp.zeros_like(down_acc)
        bias_acc[...] = jnp.zeros_like(bias_acc)

    x = x_ref[...]
    dout = dout_ref[...]
    up = w_ref[:part]
    down = w_ref[part : 2 * part]
    up_bias = w_ref[2 * part :][0:1, :part].astype(f32)
    pre = dot(x, up, NT) + up_bias
    grad_hidden = dot(dout, down, NT)
    square = pre * pre
    inner = jnp.tanh(pre * (GELU_C + GELU_C * GELU_K * square))
    half = 0.5 * pre
    hidden = (half + half * inner).astype(b16)
    slope = 0.5 + 0.5 * inner + half * (1.0 - inner * inner) * (GELU_C + 3.0 * GELU_C * GELU_K * square)
    grad_pre = slope * grad_hidden
    grad_pre_b = grad_pre.astype(b16)
    out = dot(hidden, down, NN)
    grad_x = dot(grad_pre_b, up, NN)
    if not first:
        out = out + sums[0][...]
        grad_x = grad_x + sums[1][...]
    if last:
        out = out + bias_ref[1:2, :]
    out_ref[...] = out.astype(out_ref.dtype)
    grad_x_ref[...] = grad_x.astype(grad_x_ref.dtype)
    down_acc[...] += dot(hidden, dout, TN)
    up_acc[...] += dot(grad_pre_b, x, TN)
    bias_acc[0:1, :] += jnp.sum(grad_pre_b.astype(f32), axis=0, keepdims=True)

    @pl.when(step == pl.num_programs(0) - 1)
    def _():
        grad_up_ref[...] = up_acc[...].astype(grad_up_ref.dtype)
        grad_down_ref[:part] = down_acc[...].astype(grad_down_ref.dtype)
        row = lax.broadcasted_iota(jnp.int32, (BIAS_ROWS, D), 0)
        tail = jnp.where(row == 0, bias_acc[0:1, :], jnp.where(row == 1, bias_ref[0:1, :], 0.0))
        grad_down_ref[part:] = tail.astype(grad_down_ref.dtype)


def expert_part(weights, x, dout, biases, sums, last, grad_type, name):
    first = sums is None
    slots = x.shape[0]
    rows = weights[0].shape[0]
    part = (rows - BIAS_ROWS) // 2
    tile = pl.BlockSpec((TILE, D), lambda i: (i, 0))
    kept = b16 if last else f32
    n = len(weights)
    return pl.pallas_call(
        functools.partial(expert_kernel, n, first, last, part),
        grid=(slots // TILE,),
        in_specs=[
            *[pl.BlockSpec(memory_space=pl.ANY)] * n,
            tile,
            tile,
            pl.BlockSpec((2, D), lambda i: (0, 0)),
            *([] if first else [tile, tile]),
        ],
        out_specs=[
            tile,
            tile,
            pl.BlockSpec((part, D), lambda i: (0, 0)),
            pl.BlockSpec((part + BIAS_ROWS, D), lambda i: (0, 0)),
        ],
        out_shape=[
            jax.ShapeDtypeStruct((slots, D), kept),
            jax.ShapeDtypeStruct((slots, D), kept),
            jax.ShapeDtypeStruct((part, D), grad_type),
            jax.ShapeDtypeStruct((part + BIAS_ROWS, D), grad_type),
        ],
        scratch_shapes=[
            pltpu.VMEM((rows, D), b16),
            pltpu.VMEM((part, D), f32),
            pltpu.VMEM((part, D), f32),
            pltpu.VMEM((8, part), f32),
            pltpu.SemaphoreType.DMA,
        ],
        compiler_params=pltpu.CompilerParams(vmem_limit_bytes=56 << 20, dimension_semantics=("arbitrary",)),
        cost_estimate=pl.CostEstimate(flops=12 * slots * part * D, bytes_accessed=slots * D * 20, transcendentals=0),
        name=name,
    )(*weights, x, dout, biases, *([] if first else sums))


SCALE = HEAD_DIM ** (-0.5)
PAIRS = HEADS // 2
WIDE = 2 * HEAD_DIM
CHEAP = pl.CostEstimate(flops=0, bytes_accessed=1024, transcendentals=0)


def normal(values):
    center = values - jnp.mean(values, axis=-1, keepdims=True)
    rate = lax.rsqrt(jnp.mean(center * center, axis=-1, keepdims=True) + NORM_EPS)
    return center * rate, rate


def lanes_like(values):
    return lax.broadcasted_iota(jnp.int32, values.shape, values.ndim - 1)


def scores_of(part_q, pair_k, length):
    scores = dot(part_q, pair_k, NT) * SCALE
    return jnp.where(lanes_like(scores) < length, scores, NEG_FILL)


def halves(pair):
    low = lanes_like(pair) < HEAD_DIM
    zero = jnp.zeros_like(pair)
    return jnp.where(low, pair, zero), jnp.where(low, zero, pair)


def joined(even, odd):
    return jnp.where(lanes_like(even) < HEAD_DIM, even, odd)


def attention_kernel(
    lengths_ref, tokens_ref, weights_ref, vector_ref, router_ref, routes_ref, places_ref,
    normed_ref, q_ref, k_ref, v_ref, context_ref, lse_ref, resid_ref, normed_two_ref, gates_ref, slots_ref,
):
    length = lengths_ref[pl.program_id(0)]
    rows = tokens_ref[...].astype(f32)
    hat, _ = normal(rows)
    normed = (hat * vector_ref[0:1, :] + vector_ref[1:2, :]).astype(b16)
    normed_ref[...] = normed
    q_ref[...] = (dot(normed, weights_ref[0], NN) + vector_ref[2:3, :]).astype(b16)
    k_ref[...] = dot(normed, weights_ref[1], NN).astype(b16)
    v_ref[...] = (dot(normed, weights_ref[2], NN) + vector_ref[3:4, :]).astype(b16)
    lse = jnp.zeros((LEN, 128), f32)
    for pair in range(PAIRS):
        lanes = slice(pair * WIDE, (pair + 1) * WIDE)
        keys, values = k_ref[:, lanes], v_ref[:, lanes]
        mixed = []
        for half, part in enumerate(halves(q_ref[:, lanes])):
            scores = scores_of(part, keys, length)
            top = jnp.max(scores, axis=-1, keepdims=True)
            total = top + jnp.log(jnp.sum(jnp.exp(scores - top), axis=-1, keepdims=True))
            chance = jnp.exp(scores - total).astype(b16)
            mixed.append(dot(chance, values, NN))
            lse = jnp.where(lanes_like(lse) == 2 * pair + half, total, lse)
        context_ref[:, lanes] = joined(*mixed).astype(b16)
    lse_ref[...] = lse
    resid = rows + (dot(context_ref[...], weights_ref[3], NN) + vector_ref[4:5, :])
    resid_ref[...] = resid
    hat, _ = normal(resid)
    normed_two = (hat * vector_ref[5:6, :] + vector_ref[6:7, :]).astype(b16)
    normed_two_ref[...] = normed_two
    logits = dot(normed_two, router_ref[...], NT)
    names = lanes_like(logits)
    first = jnp.sum(jnp.where(names == routes_ref[:, 0:1], logits, 0.0), axis=-1, keepdims=True)
    second = jnp.sum(jnp.where(names == routes_ref[:, 1:2], logits, 0.0), axis=-1, keepdims=True)
    gate = lanes_like(gates_ref[...])
    gates_ref[...] = jnp.where(gate == 0, jax.nn.sigmoid(first - second), jax.nn.sigmoid(second - first))
    experts, _, capacity, _ = slots_ref.shape
    slots = experts * capacity
    ids = lax.broadcasted_iota(jnp.int32, (slots, ROWS), 0)
    places = places_ref[0]
    chosen = jnp.where((ids == places[0:1, :]) | (ids == places[1:2, :]), 1.0, 0.0).astype(b16)
    sent = dot(chosen, normed_two, NN).astype(b16)
    slots_ref[...] = sent.reshape(experts, 1, capacity, D)


def attention_forward(lengths, tokens, weights, vector, router, routes, places, experts, capacity):
    count = tokens.shape[0]
    rows = pl.BlockSpec((LEN, D), lambda i: (i, 0))
    lanes = pl.BlockSpec((LEN, 128), lambda i: (i, 0))
    once = pl.Buffered(1)
    return pl.pallas_call(
        attention_kernel,
        grid=(count // LEN,),
        in_specs=[
            pl.BlockSpec(memory_space=pltpu.SMEM),
            rows,
            pl.BlockSpec((4, D, D), lambda i: (0, 0, 0), pipeline_mode=once),
            pl.BlockSpec((8, D), lambda i: (0, 0)),
            pl.BlockSpec((128, D), lambda i: (0, 0)),
            pl.BlockSpec((LEN, 2), lambda i: (i, 0)),
            pl.BlockSpec((1, 2, ROWS), lambda i: (i, 0, 0)),
        ],
        out_specs=[
            rows, rows, rows, rows, rows, lanes, rows, rows, lanes,
            pl.BlockSpec((experts, 1, capacity, D), lambda i: (0, i, 0, 0)),
        ],
        out_shape=[
            *[jax.ShapeDtypeStruct((count, D), b16)] * 5,
            jax.ShapeDtypeStruct((count, 128), f32),
            jax.ShapeDtypeStruct((count, D), f32),
            jax.ShapeDtypeStruct((count, D), b16),
            jax.ShapeDtypeStruct((count, 128), f32),
            jax.ShapeDtypeStruct((experts, count // ROWS, capacity, D), b16),
        ],
        compiler_params=pltpu.CompilerParams(vmem_limit_bytes=48 << 20),
        cost_estimate=CHEAP,
        name="attention_forward",
    )(lengths, tokens, weights, vector, router, routes, places)


def norm_back(grad, hat, rate, gain):
    inner = grad * gain
    return rate * (
        inner
        - jnp.mean(inner, axis=-1, keepdims=True)
        - hat * jnp.mean(inner * hat, axis=-1, keepdims=True)
    )


def two_terms(values):
    high = values.astype(b16)
    return high, (values - high.astype(f32)).astype(b16)


def column_sum(values):
    return jnp.sum(values, axis=0, keepdims=True)


def sequence_backward(
    s, lengths_ref, tokens_ref, grad_ref, weights_ref, vector_ref, router_ref, routes_ref, places_ref,
    normed_ref, q_ref, k_ref, v_ref, context_ref, lse_ref, resid_ref, normed_two_ref, gates_ref, outs_ref, returned_ref,
    output_ref, input_grad_ref, weights_acc, vector_acc, router_acc, dq_ref, dk_ref, dv_ref,
):
    at = pl.ds(s * LEN, LEN)
    length = lengths_ref[s]
    experts, _, capacity, _ = outs_ref.shape
    slots = experts * capacity
    ids = lax.broadcasted_iota(jnp.int32, (ROWS, slots), 1)
    outs = outs_ref[:, s].reshape(slots, D)
    grad_out = grad_ref[at, :].astype(f32)
    places = places_ref[at, :]
    take = [jnp.where(ids == places[:, k : k + 1], 1.0, 0.0).astype(b16) for k in range(2)]
    out = [dot(t, outs, NN) for t in take]
    both_gates = gates_ref[at, :]
    gates = [both_gates[:, k : k + 1] for k in range(2)]
    resid = resid_ref[at, :]
    output_ref[at, :] = resid + gates[0] * out[0] + gates[1] * out[1]
    slopes = [
        jnp.sum(grad_out * out[k], axis=-1, keepdims=True) * (gates[k] * (1.0 - gates[k])) for k in range(2)
    ]
    pull = slopes[0] - slopes[1]
    names = lax.broadcasted_iota(jnp.int32, (ROWS, 128), 1)
    routes = routes_ref[at, :]
    grad_logits = jnp.where(names == routes[:, 0:1], pull, jnp.where(names == routes[:, 1:2], -pull, 0.0))
    high, low = two_terms(grad_logits)
    normed_two = normed_two_ref[at, :]
    router = router_ref[...]
    router_acc[...] += dot(high, normed_two, TN) + dot(low, normed_two, TN)
    returned = returned_ref[:, s].reshape(slots, D)
    grad_two = dot(take[0] + take[1], returned, NN) + (dot(high, router, NN) + dot(low, router, NN))
    hat, rate = normal(resid)
    vector_acc[5:6, :] += column_sum(grad_two * hat)
    vector_acc[6:7, :] += column_sum(grad_two)
    grad_resid = grad_out + norm_back(grad_two, hat, rate, vector_ref[5:6, :])
    input_grad_ref[at, :] = grad_resid
    branch = grad_resid.astype(b16)
    vector_acc[4:5, :] += column_sum(branch.astype(f32))
    weights_acc[3] += dot(context_ref[at, :], branch, TN)
    grad_context = dot(branch, weights_ref[3], NT).astype(b16)
    for pair in range(PAIRS):
        lanes = slice(pair * WIDE, (pair + 1) * WIDE)
        queries, keys, values = q_ref[at, lanes], k_ref[at, lanes], v_ref[at, lanes]
        given = grad_context[:, lanes]
        grads = []
        for half, (part, part_given) in enumerate(zip(halves(queries), halves(given))):
            head = 2 * pair + half
            chance = jnp.exp(scores_of(part, keys, length) - lse_ref[at, head : head + 1])
            grad_v = dot(chance.astype(b16), given, TN)
            grad_chance = dot(part_given, values, NT)
            mean = jnp.sum(chance * grad_chance, axis=-1, keepdims=True)
            grad_scores = (chance * (grad_chance - mean)).astype(b16)
            grads.append((dot(grad_scores, keys, NN), dot(grad_scores, queries, TN), grad_v))
        dq_ref[:, lanes] = (joined(grads[0][0], grads[1][0]) * SCALE).astype(b16)
        dk_ref[:, lanes] = (joined(grads[0][1], grads[1][1]) * SCALE).astype(b16)
        dv_ref[:, lanes] = joined(grads[0][2], grads[1][2]).astype(b16)
    normed = normed_ref[at, :]
    grad_one = jnp.zeros((LEN, D), f32)
    for k, ref in enumerate((dq_ref, dk_ref, dv_ref)):
        weights_acc[k] += dot(normed, ref[...], TN)
        grad_one += dot(ref[...], weights_ref[k], NT)
    vector_acc[2:3, :] += column_sum(dq_ref[...].astype(f32))
    vector_acc[3:4, :] += column_sum(dv_ref[...].astype(f32))
    hat, rate = normal(tokens_ref[at, :].astype(f32))
    vector_acc[0:1, :] += column_sum(grad_one * hat)
    vector_acc[1:2, :] += column_sum(grad_one)
    input_grad_ref[at, :] += norm_back(grad_one, hat, rate, vector_ref[0:1, :])


KINDS = 6
FAR, MIDDLE, NEAR, FAR_ON, MIDDLE_ON, FAR_LAST = range(KINDS)


def finish_kernel(
    n, cols, extra, seqs,
    lengths_ref, tokens_ref, grad_ref, weights_ref, vector_ref, router_ref, routes_ref, places_ref,
    normed_ref, q_ref, k_ref, v_ref, context_ref, lse_ref, resid_ref, normed_two_ref, gates_ref, outs_ref, backs_ref,
    near_up, near_down, middle_up, middle_down, far_up, far_down,
    output_ref, input_grad_ref, dense_ref, near_up_in, near_down_in, middle_up_in, middle_down_in, end_up_in, end_down_in,
    outs_in, backs_in, weights_acc, vector_acc, router_acc, dq_ref, dk_ref, dv_ref,
    far_up_buf, far_down_buf, middle_up_buf, middle_down_buf, on_up_buf, on_down_buf, load_up, load_down,
    parts, stage, c_buf, b_buf, a_buf, z_buf,
    own_s, out_s, out_r, back_s, back_r, chain_s, chain_r, load_s, c_s, c_r, b_s, b_r, a_s, a_r, z_s, z_r,
):
    inside = cols % 8 == 0
    side, z, y, x, core = where_am_i()
    mine = lax.axis_index("expert")
    experts = outs_in.shape[0]
    along_z, first, second, sibling = peers_of(n, side, z, y, x, core)
    plane = [(z, (mine + k) % experts) for k in range(1, experts)]
    greet([*along_z, *plane])
    area = side * side if inside else 0
    sent = []

    def remote(src, dst, send, recv, peer):
        return pltpu.make_async_remote_copy(
            src_ref=src, dst_ref=dst, send_sem=send, recv_sem=recv, device_id=peer, device_id_type=MESH
        )

    def send(src, dst, send_sem, recv_sem, peer):
        copy = remote(src, dst, send_sem, recv_sem, peer)
        copy.start()
        sent.append(copy)

    for k in range(1, experts):
        to = (mine + k) % experts
        send(outs_ref.at[to], outs_in.at[mine], out_s.at[k], out_r.at[k], plane[k - 1])
    for k in range(1, experts):
        to = (mine + k) % experts
        send(backs_ref.at[to], backs_in.at[mine], back_s.at[k], back_r.at[k], plane[k - 1])
    own = [
        pltpu.make_async_copy(outs_ref.at[mine], outs_in.at[mine], own_s.at[0]),
        pltpu.make_async_copy(backs_ref.at[mine], backs_in.at[mine], own_s.at[1]),
    ]
    for copy in own:
        copy.start()

    inner = (z + 1) // 2 % 2 == 1
    outer = jnp.logical_not(inner)
    inward = (z - z + 1 + z // 2, mine)
    across = (3 - z, mine)
    outward = (3 * (z // 2), mine)
    near, middle, far = (near_up, near_down), (middle_up, middle_down), (far_up, far_down)
    near_in, middle_in = (near_up_in, near_down_in), (middle_up_in, middle_down_in)
    end_in = (end_up_in, end_down_in)
    far_buf, middle_buf, on_buf = (far_up_buf, far_down_buf), (middle_up_buf, middle_down_buf), (on_up_buf, on_down_buf)
    loads = (load_up, load_down)

    def hop(kind, half, src, dst, peer):
        return remote(src, dst, chain_s.at[kind, half], chain_r.at[kind, half], peer)

    from_ends = [(FAR, far, far_buf), (MIDDLE, middle, middle_buf), (NEAR, near, near_in)]

    @pl.when(outer)
    def _():
        for kind, src, dst in from_ends:
            for half in range(2):
                hop(kind, half, src[half], dst[half], inward).start()

    def chain_step(kind, half, buf, term, next_kind, target, peer):
        @pl.when(inner)
        def _():
            load = pltpu.make_async_copy(term[half], loads[half], load_s)
            load.start()
            hop(kind, half, buf[half], buf[half], across).wait_recv()
            load.wait()
            buf[half][...] = (buf[half][...].astype(f32) + loads[half][...].astype(f32)).astype(b16)
            hop(next_kind, half, buf[half], target[half], peer).start()

    def step_far(half):
        chain_step(FAR, half, far_buf, far, FAR_ON, on_buf, across)

    def step_on(half):
        chain_step(FAR_ON, half, on_buf, near, FAR_LAST, end_in, outward)

    def step_middle(half):
        chain_step(MIDDLE, half, middle_buf, middle, MIDDLE_ON, middle_in, across)

    weights_acc[...] = jnp.zeros_like(weights_acc)
    vector_acc[...] = jnp.zeros_like(vector_acc)
    router_acc[...] = jnp.zeros_like(router_acc)
    step_far(0)
    step_far(1)
    step_on(0)
    for copy in own:
        copy.wait()
    for k in range(1, experts):
        block = outs_in.at[(mine - k + experts) % experts]
        remote(block, block, out_s.at[k], out_r.at[k], sibling).wait_recv()
        block = backs_in.at[(mine - k + experts) % experts]
        remote(block, block, back_s.at[k], back_r.at[k], sibling).wait_recv()
    for s in range(seqs):
        sequence_backward(
            s, lengths_ref, tokens_ref, grad_ref, weights_ref, vector_ref, router_ref, routes_ref, places_ref,
            normed_ref, q_ref, k_ref, v_ref, context_ref, lse_ref, resid_ref, normed_two_ref, gates_ref, outs_in, backs_in,
            output_ref, input_grad_ref, weights_acc, vector_acc, router_acc, dq_ref, dk_ref, dv_ref,
        )
        if s == 0:
            step_on(1)
            step_middle(0)

    small = jnp.concatenate([vector_acc[...], router_acc[: extra - 8, :]], axis=0).astype(b16)
    if not inside:
        dense_ref[:extra, :] = jnp.concatenate([vector_acc[...], router_acc[: extra - 8, :]], axis=0)
        for k in range(4):
            dense_ref[extra + k * D : extra + (k + 1) * D, :] = weights_acc[k]
        step_middle(1)
    for core_ in range(2 if inside else 0):
        for y_ in range(side):
            for x_ in range(side):
                for z_ in range(n):
                    owner = ((z_ * side + y_) * side + x_) * 2 + core_
                    rows = [weights_acc[k, owner * cols : (owner + 1) * cols, :] for k in range(4)]
                    place = parts.at[(core_ * side + y_) * side + x_, z_]
                    place[: 4 * cols, :] = jnp.concatenate(rows, axis=0).astype(b16)
                    place[4 * cols :, :] = small

    def piece(ka, kb, core_):
        y_ = (y + core * ka + (1 - core) * kb) % side
        x_ = (x + (1 - core) * ka + core * kb) % side
        return (core_ * side + y_) * side + x_

    order = [(ka, kb) for kb in [*range(1, side), 0] for ka in [*range(1, side), 0]][:area]
    for ka, kb in order:
        place = ka * side + kb
        send(parts.at[piece(kb, ka, 1 - core)], c_buf.at[place], c_s.at[place], c_r.at[place], sibling)
    for ka, kb in order:
        place = ka * side + kb
        remote(c_buf.at[place], c_buf.at[place], c_s.at[place], c_r.at[place], sibling).wait_recv()
        mine_ = piece(ka, kb, core)
        if kb:
            stage[place] = (parts[mine_].astype(f32) + c_buf[place].astype(f32)).astype(b16)
            send(stage.at[place], b_buf.at[place], b_s.at[place], b_r.at[place], second[kb - 1])
            if ka == 0:
                step_middle(1)
        else:
            total = parts[mine_].astype(f32) + c_buf[place].astype(f32)
            for k in range(1, side):
                slot = ka * side + k
                remote(b_buf.at[slot], b_buf.at[slot], b_s.at[slot], b_r.at[slot], sibling).wait_recv()
                total = total + b_buf[slot].astype(f32)
            if ka:
                stage[place] = total.astype(b16)
                send(stage.at[place], a_buf.at[ka], a_s.at[ka], a_r.at[ka], first[ka - 1])
            else:
                for k in range(1, side):
                    remote(a_buf.at[k], a_buf.at[k], a_s.at[k], a_r.at[k], sibling).wait_recv()
                    total = total + a_buf[k].astype(f32)
                stage[place] = total.astype(b16)
    if inside:
        for k in range(1, n):
            send(stage.at[0, (z + k) % n], z_buf.at[k], z_s.at[k], z_r.at[k], along_z[k - 1])
        result = stage[0, z].astype(f32)
        for k in range(1, n):
            remote(z_buf.at[k], z_buf.at[k], z_s.at[k], z_r.at[k], sibling).wait_recv()
            result = result + z_buf[k].astype(f32)
        dense_ref[...] = result
    for copy in sent:
        copy.wait_send()

    @pl.when(outer)
    def _():
        for half in range(2):
            for kind, src, dst in from_ends:
                hop(kind, half, src[half], dst[half], inward).wait_send()
            hop(FAR_LAST, half, end_in[half], end_in[half], inward).wait_recv()

    @pl.when(inner)
    def _():
        for half in range(2):
            hop(FAR_ON, half, far_buf[half], on_buf[half], across).wait_send()
            hop(FAR_LAST, half, on_buf[half], end_in[half], outward).wait_send()
            hop(MIDDLE_ON, half, middle_buf[half], middle_in[half], across).wait_send()
            hop(MIDDLE_ON, half, middle_in[half], middle_in[half], across).wait_recv()
            hop(NEAR, half, near_in[half], near_in[half], outward).wait_recv()


def finish(n, side, cols, extra, lengths, rows_in, kept, outs, backs, grads):
    count = rows_in[0].shape[0]
    slots = outs.shape
    vmem = pl.BlockSpec(memory_space=pltpu.VMEM)
    hbm = pl.BlockSpec(memory_space=pl.ANY)
    shapes = [jax.ShapeDtypeStruct(g.shape, b16) for g in grads[:2]]
    inside = cols % 8 == 0
    rows = 4 * cols + extra if inside else 4 * D + extra
    block = (n, rows, D) if inside else (1, 16, 128)
    dma = pltpu.SemaphoreType.DMA
    half = [pltpu.VMEM(g.shape, b16) for g in grads[:2]]
    area = side * side
    return pl.pallas_call(
        functools.partial(finish_kernel, n, cols, extra, count // LEN),
        in_specs=[
            pl.BlockSpec(memory_space=pltpu.SMEM),
            *[vmem] * (len(rows_in) + len(kept)),
            hbm,
            hbm,
            *[hbm] * len(grads),
        ],
        out_specs=[vmem, vmem, vmem, *[hbm] * 6],
        out_shape=[
            jax.ShapeDtypeStruct((count, D), f32),
            jax.ShapeDtypeStruct((count, D), f32),
            jax.ShapeDtypeStruct((rows, D), f32),
            *shapes * 3,
        ],
        scratch_shapes=[
            pltpu.VMEM(slots, b16),
            pltpu.VMEM(slots, b16),
            pltpu.VMEM((4, D, D), f32),
            pltpu.VMEM((8, D), f32),
            pltpu.VMEM((128, D), f32),
            *[pltpu.VMEM((LEN, D), b16)] * 3,
            *half * 4,
            pltpu.VMEM((2 * area, *block), b16),
            pltpu.VMEM((area, *block), b16),
            pltpu.VMEM((area, *block), b16),
            pltpu.VMEM((area, *block), b16),
            pltpu.VMEM((side, *block), b16),
            pltpu.VMEM(block, b16),
            dma((2,)),
            *[dma((slots[0],))] * 4,
            *[dma((KINDS, 2))] * 2,
            dma,
            *[dma((area,))] * 4,
            *[dma((side,))] * 2,
            *[dma((n,))] * 2,
        ],
        compiler_params=pltpu.CompilerParams(collective_id=1, has_side_effects=True, vmem_limit_bytes=63 << 20),
        cost_estimate=CHEAP,
        name="finish",
    )(lengths, *rows_in, *kept, outs, backs, *grads)


def pack_expert(up, down, up_bias, down_bias, dtype):
    part = up.shape[0]
    tail = jnp.zeros((BIAS_ROWS, D), dtype)
    tail = tail.at[0, :part].set(up_bias.astype(dtype))
    tail = tail.at[1, : down_bias.shape[0]].set(down_bias.astype(dtype))
    return jnp.concatenate([up.astype(dtype), down.astype(dtype), tail], axis=0)


def after(x, *others):
    return lax.optimization_barrier((x, *others))[0]


def along(x, *pairs):
    return lax.ppermute(x, "dp", pairs)


def body(
    tokens, out_grad, routes, lengths,
    attention, gain_bias, router, expert_up, up_bias, expert_down, down_bias,
    first_attention, first_gain_bias, first_router, first_expert_up, first_up_bias, first_expert_down, first_down_bias,
    square_attention, square_gain_bias, square_router, square_expert_up, square_up_bias, square_expert_down, square_down_bias,
):
    experts = router.shape[0]
    capacity = 4 * ROWS // experts
    count = tokens.shape[0]
    blocks = count // ROWS
    part = expert_up.shape[1]
    narrow = down_bias.shape[1]
    cols = attention.shape[1]
    devices = D // cols
    n_dp = lax.axis_size("dp")
    assert n_dp == 4 and expert_up.shape[0] == 1
    me = lax.axis_index("dp")
    mine = lax.axis_index("expert")
    both = ("dp", "expert")

    flat_len = (7 + experts) * cols
    extra = -(-(4 * cols + -(-flat_len // D)) // 16) * 16 - 4 * cols
    side = math.isqrt(experts // 2)
    small = jnp.concatenate([gain_bias, router], axis=0).astype(b16).reshape(-1)
    small = jnp.pad(small, (0, extra * D - flat_len)).reshape(extra, D)
    packed = jnp.concatenate([attention.astype(b16).reshape(4 * cols, D), small], axis=0)
    whole = gather_dense(packed, n_dp, side)
    own = after(pack_expert(expert_up[0], expert_down[0], up_bias[0], down_bias[0], b16), whole)

    second = along(own, (0, 1), (1, 0), (2, 3), (3, 2))
    third_inner = along(own, (1, 2), (2, 1))
    third_outer = along(third_inner, (1, 0), (2, 3))
    fourth_inner = along(second, (1, 2), (2, 1))
    fourth_outer = along(fourth_inner, (1, 0), (2, 3))

    weights_b = whole[:, : 4 * cols].reshape(devices, 4, cols, D).transpose(1, 0, 2, 3).reshape(4, D, D)
    small = whole[:, 4 * cols :].reshape(devices, extra * D)[:, :flat_len].reshape(devices, 7 + experts, cols)
    small = small.transpose(1, 0, 2).reshape(7 + experts, D)
    vector = small[:7].astype(f32)
    router_b = small[7:]

    positions = slots_of(routes, experts, capacity)
    slot_ids = jnp.arange(experts * capacity, dtype=jnp.int32)
    hit = positions[:, :, :, None] == slot_ids
    split = jnp.any(hit, axis=2).astype(b16).reshape(blocks, ROWS, experts, capacity)
    other = jnp.flip(routes, axis=1).reshape(blocks, ROWS, 2)
    partner = jnp.sum(jnp.where(hit, other[:, :, :, None], 0), axis=(1, 2)).astype(f32)
    partner = partner.reshape(blocks, experts, capacity).transpose(1, 0, 2)
    partner = lax.all_to_all(partner, "expert", split_axis=0, concat_axis=0, tiled=True)
    grad_rows = out_grad.reshape(blocks, ROWS, D)

    sent = jnp.einsum("btec,btd->ebcd", split, grad_rows, preferred_element_type=f32).astype(b16)
    sent = after(sent, whole)
    grad_slots = lax.all_to_all(sent, "expert", split_axis=0, concat_axis=0, tiled=True)
    grad_slots = grad_slots.reshape(experts * blocks * capacity, D)

    router_all = jnp.pad(router_b, ((0, 128 - experts), (0, 0)))
    vector_all = jnp.pad(vector, ((0, 1), (0, 0)))
    *kept, slots_out = attention_forward(
        lengths, tokens, weights_b, vector_all, router_all, routes, positions.transpose(0, 2, 1), experts, capacity
    )

    def exchange(sent):
        return lax.all_to_all(sent, "expert", split_axis=0, concat_axis=0, tiled=True)

    slots_in = exchange(after(slots_out, grad_slots)).reshape(experts * blocks * capacity, D)

    slot_logits = jnp.einsum("sd,ed->se", slots_in, router_b, preferred_element_type=f32)
    ids = jnp.arange(experts, dtype=jnp.int32)
    rival = partner.reshape(-1).astype(jnp.int32)
    margin = jnp.sum(
        slot_logits * ((ids == mine).astype(f32) - (rival[:, None] == ids).astype(f32)), axis=-1
    )
    dout = (jax.nn.sigmoid(margin)[:, None] * grad_slots.astype(f32)).astype(b16)
    grad_down_bias = jnp.sum(dout.astype(f32), axis=0)

    def pick(*arrays):
        out = arrays[-1]
        for i in range(len(arrays) - 2, -1, -1):
            out = jnp.where(me == i, arrays[i], out)
        return out

    inner = (me == 1) | (me == 2)
    tail = 2 * part + 1
    names = [me, pick(1, 0, 3, 2), pick(2, 2, 1, 1), pick(3, 3, 0, 0)]
    bias_rows = [
        own[tail, :narrow],
        second[tail, :narrow],
        jnp.where(inner, third_inner[tail, :narrow], third_outer[tail, :narrow]),
        jnp.where(inner, fourth_inner[tail, :narrow], fourth_outer[tail, :narrow]),
    ]
    place = jnp.stack(names)
    down_bias_full = jnp.zeros((n_dp, narrow), b16).at[place].set(jnp.stack(bias_rows)).reshape(D)
    weights = [(own,), (second,), (third_inner, third_outer), (fourth_inner, fourth_outer)]
    sums = None
    part_grads = []
    for i in range(4):
        share = lax.dynamic_slice(grad_down_bias, (names[i] * narrow,), (narrow,))
        share = jnp.pad(share, (0, D - narrow))
        biases = jnp.stack([share, down_bias_full.astype(f32) if i == 3 else share])
        *sums, grad_up, grad_down = expert_part(
            weights[i], slots_in, dout, biases, sums, i == 3, b16 if i else f32, f"expert_part_{i}"
        )
        part_grads.append((grad_up, grad_down))
    out_b, grad_b = sums

    small_rows = -(-(8 + experts) // 16) * 16
    slots_shape = (experts, blocks, capacity, D)
    output, input_grad, dense, *came = finish(
        n_dp, side, cols, small_rows, lengths,
        (tokens, out_grad, weights_b, vector_all, router_all, routes, positions.reshape(count, 2)),
        kept, out_b.reshape(slots_shape), grad_b.reshape(slots_shape), [g for i in (1, 2, 3) for g in part_grads[i]],
    )
    totals = [
        part_grads[0][i]
        + jnp.where(inner, came[i].astype(f32) + came[2 + i].astype(f32), came[4 + i].astype(f32))
        for i in range(2)
    ]
    shard_up = totals[0][None]
    shard_down = totals[1][:part][None]
    shard_up_bias = totals[1][part, :part][None]
    shard_down_bias = totals[1][part + 1, :narrow][None]
    if cols % 8:
        small = lax.psum(dense[:small_rows], both)
        big = dense[small_rows:].reshape(4, D, D).astype(b16)
        big = lax.psum_scatter(big, both, scatter_dimension=1, tiled=True).astype(f32)
        dense = jnp.concatenate([big.reshape(4 * cols, D), small], axis=0)
    shard_weights = dense[: 4 * cols].reshape(4, cols, D)
    small = lax.dynamic_slice(
        dense[4 * cols :], (0, (me * experts + mine) * cols), (small_rows, cols)
    )
    shard_vector, shard_router = small[:7], small[8 : 8 + experts]

    params = (attention, gain_bias, router, expert_up, up_bias, expert_down, down_bias)
    grads = (shard_weights, shard_vector, shard_router, shard_up, shard_up_bias, shard_down, shard_down_bias)
    firsts = (first_attention, first_gain_bias, first_router, first_expert_up, first_up_bias, first_expert_down, first_down_bias)
    squares = (square_attention, square_gain_bias, square_router, square_expert_up, square_up_bias, square_expert_down, square_down_bias)
    hidden_units = n_dp * part
    rates = (1.6 * D ** (-0.5), 0.3, 0.5 * D ** (-0.5), 1.5 * D ** (-0.5), 0.25, 0.5 * hidden_units ** (-0.5), 0.25)
    updated = [adam_step(params[i], grads[i], firsts[i], squares[i], rates[i]) for i in range(7)]
    return (output, input_grad, *grads, *(u[0] for u in updated), *(u[1] for u in updated), *(u[2] for u in updated))


def solution(mesh):
    rows = P(("dp", "expert"), None)
    state = (
        P(None, ("dp", "expert"), None),
        P(None, ("dp", "expert")),
        P(None, ("dp", "expert")),
        P("expert", "dp", None),
        P("expert", "dp"),
        P("expert", "dp", None),
        P("expert", "dp"),
    )
    return jax.shard_map(
        body,
        mesh=mesh,
        in_specs=(rows, rows, rows, P(("dp", "expert")), *state, *state, *state),
        out_specs=(rows, rows, *state, *state, *state, *state),
        check_vma=False,
    )
```

```python
import functools
import math

import jax
import jax.numpy as jnp
from jax import lax
from jax.experimental import pallas as pl
from jax.experimental.pallas import tpu as pltpu
from jax.sharding import PartitionSpec as P

D = 768
HEADS = 12
HEAD_DIM = 64
LEN = 256
STEP = 3
ROWS = 256
BIAS_ROWS = 16

NORM_EPS = 1e-06
NEG_FILL = -1000000000.0
BETA_ONE = 0.9
BETA_TWO = 0.95
WEIGHT_DECAY = 0.1
ADAM_EPS = 1e-08
GELU_C = 0.7978845608028654
GELU_K = 0.044715
f32 = jnp.float32
b16 = jnp.bfloat16
MESH = pl.DeviceIdType.MESH


def adam_step(weight, grad, first, square, rate):
    new_first = BETA_ONE * first + (1.0 - BETA_ONE) * grad
    new_square = BETA_TWO * square + (1.0 - BETA_TWO) * grad * grad
    first_hat = new_first / (1.0 - BETA_ONE**STEP)
    square_hat = new_square / (1.0 - BETA_TWO**STEP)
    update = -rate * (first_hat / (jnp.sqrt(square_hat) + ADAM_EPS) + WEIGHT_DECAY * weight)
    return (weight + update, new_first, new_square)


def slots_of(routes, experts, capacity):
    flat = routes.reshape(-1, 2 * ROWS)
    onehot = (flat[:, :, None] == jnp.arange(experts, dtype=jnp.int32)).astype(b16)
    row = lax.broadcasted_iota(jnp.int32, (2 * ROWS, 2 * ROWS), 0)
    col = lax.broadcasted_iota(jnp.int32, (2 * ROWS, 2 * ROWS), 1)
    earlier = (col < row).astype(b16)
    before = jnp.einsum("ij,bje->bie", earlier, onehot, preferred_element_type=f32)
    slot = jnp.sum(before * onehot.astype(f32), axis=-1).astype(jnp.int32)
    return (flat * capacity + slot).reshape(-1, ROWS, 2)


def where_am_i():
    side = math.isqrt(lax.axis_size("expert") // 2)
    spot = lax.axis_index("expert")
    return side, lax.axis_index("dp"), spot // (2 * side), spot // 2 % side, spot % 2


def greet(peers):
    barrier = pltpu.get_barrier_semaphore()
    for peer in peers:
        pl.semaphore_signal(barrier, inc=1, device_id=peer, device_id_type=MESH)
    pl.semaphore_wait(barrier, len(peers))


def peers_of(n, side, z, y, x, core):
    def at(z_, y_, x_, core_):
        return (z_, (y_ * side + x_) * 2 + core_)

    along_z = [at((z + k) % n, y, x, core) for k in range(1, n)]
    first = [at(z, (y + core * k) % side, (x + (1 - core) * k) % side, core) for k in range(1, side)]
    second = [at(z, (y + (1 - core) * k) % side, (x + core * k) % side, core) for k in range(1, side)]
    return along_z, first, second, at(z, y, x, 1 - core)


def remote(src, dst, send, recv, peer):
    return pltpu.make_async_remote_copy(
        src_ref=src, dst_ref=dst, send_sem=send, recv_sem=recv, device_id=peer, device_id_type=MESH
    )


def spread_blocks(n, in_ref, block_at, sems, meanwhile, at_last):
    z_s, z_r, a_s, a_r, b_s, b_r, c_s, c_r = sems
    side, z, y, x, core = where_am_i()
    along_z, first, second, sibling = peers_of(n, side, z, y, x, core)
    sent = []

    def block(j, ka, kb, core_):
        y_ = (y - core * ka - (1 - core) * kb + 2 * side) % side
        x_ = (x - (1 - core) * ka - core * kb + 2 * side) % side
        return block_at(((((z - j + n) % n) * side + y_) * side + x_) * 2 + core_)

    def send(src, dst, send_sem, recv_sem, peer):
        copy = remote(src, dst, send_sem, recv_sem, peer)
        copy.start()
        sent.append(copy)

    def pass_on(src, dst, j, ka, kb):
        if kb == 0:
            if ka == 0:
                for k in range(1, side):
                    send(src, dst, a_s.at[j * side + k], a_r.at[j * side + k], first[k - 1])
            for k in range(1, side):
                place = (j * side + ka) * side + k
                send(src, dst, b_s.at[place], b_r.at[place], second[k - 1])
        place = (j * side + kb) * side + ka
        send(src, dst, c_s.at[place], c_r.at[place], sibling)

    for k in range(1, n):
        send(in_ref, block(0, 0, 0, core), z_s.at[k], z_r.at[k], along_z[k - 1])
    meanwhile()
    pass_on(in_ref, block(0, 0, 0, core), 0, 0, 0)
    for j in range(1, n):
        here = block(j, 0, 0, core)
        remote(here, here, z_s.at[j], z_r.at[j], sibling).wait_recv()
        pass_on(here, here, j, 0, 0)
    for j in range(n):
        for ka in range(1, side):
            here = block(j, ka, 0, core)
            remote(here, here, a_s.at[j * side + ka], a_r.at[j * side + ka], sibling).wait_recv()
            pass_on(here, here, j, ka, 0)
    for j in range(n):
        for ka in range(side):
            for kb in range(1, side):
                here = block(j, ka, kb, core)
                place = (j * side + ka) * side + kb
                remote(here, here, b_s.at[place], b_r.at[place], sibling).wait_recv()
                pass_on(here, here, j, ka, kb)
    at_last()
    for j in range(n):
        for ka in range(side):
            for kb in range(side):
                here = block(j, ka, kb, 1 - core)
                place = (j * side + ka) * side + kb
                remote(here, here, c_s.at[place], c_r.at[place], sibling).wait_recv()
    return sent


def spread_sems(n, side):
    dma = pltpu.SemaphoreType.DMA
    return [*[dma((n,))] * 2, *[dma((n * side,))] * 2, *[dma((n * side * side,))] * 4]


def exchange_all(pairs, sent):
    z, mine = lax.axis_index("dp"), lax.axis_index("expert")
    experts = lax.axis_size("expert")
    for k in range(1, experts):
        to = (mine + k) % experts
        for src, dst, send, recv in pairs:
            copy = remote(src(to), dst(mine), send.at[k], recv.at[k], (z, to))
            copy.start()
            sent.append(copy)


def wait_all(pairs):
    z, mine = lax.axis_index("dp"), lax.axis_index("expert")
    experts = lax.axis_size("expert")
    for k in range(1, experts):
        came = (mine - k + experts) % experts
        for _, dst, send, recv in pairs:
            remote(dst(came), dst(came), send.at[k], recv.at[k], (z, came)).wait_recv()


def gather_kernel(
    n, in_ref, own_ref, slots_ref, marks_ref, out_ref, second_ref, third_ref, slots_in, marks_in,
    local_sem, part_s, part_r, slot_s, slot_r, mark_s, mark_r, *sems,
):
    side, z, y, x, core = where_am_i()
    mine = lax.axis_index("expert")
    experts = slots_ref.shape[0]
    greet([*peers_of(n, side, z, y, x, core)[0], *[(z, (mine + k) % experts) for k in range(1, experts)]])
    me = ((z * side + y) * side + x) * 2 + core
    stays = [
        pltpu.make_async_copy(in_ref, out_ref.at[me], local_sem.at[0]),
        pltpu.make_async_copy(slots_ref.at[mine], slots_in.at[mine], local_sem.at[1]),
        pltpu.make_async_copy(marks_ref.at[mine], marks_in.at[mine], local_sem.at[2]),
    ]
    for copy in stays:
        copy.start()
    beside = remote(own_ref, second_ref, part_s.at[0], part_r.at[0], (z + 1 - 2 * (z % 2), mine))
    across = remote(own_ref, third_ref, part_s.at[1], part_r.at[1], ((n - 1 - z) % n, mine))
    inner = (z + 1) // 2 % 2 == 1
    pairs = [
        (lambda e: slots_ref.at[e], lambda e: slots_in.at[e], slot_s, slot_r),
        (lambda e: marks_ref.at[e], lambda e: marks_in.at[e], mark_s, mark_r),
    ]
    more = []

    def weights_on():
        beside.start()

        @pl.when(inner)
        def _():
            across.start()

    sent = spread_blocks(n, in_ref, lambda d: out_ref.at[d], sems, weights_on, lambda: exchange_all(pairs, more))
    wait_all(pairs)
    for copy in [*sent, *more]:
        copy.wait_send()
    for copy in stays:
        copy.wait()
    beside.wait()

    @pl.when(inner)
    def _():
        across.wait()


def gather_dense(packed, own, slots, marks, n, side):
    devices = n * side * side * 2
    experts = slots.shape[0]
    dma = pltpu.SemaphoreType.DMA
    sems = [dma((3,)), *[dma((2,))] * 2, *[dma((experts,))] * 4, *spread_sems(n, side)]
    vmem, hbm = pl.BlockSpec(memory_space=pltpu.VMEM), pl.BlockSpec(memory_space=pl.ANY)
    gathered = jax.ShapeDtypeStruct((devices, *packed.shape), packed.dtype)
    return pl.pallas_call(
        functools.partial(gather_kernel, n),
        out_shape=[gathered, *[jax.ShapeDtypeStruct(v.shape, v.dtype) for v in (own, own, slots, marks)]],
        in_specs=[vmem, hbm, hbm, hbm],
        out_specs=[vmem, *[hbm] * 4],
        scratch_shapes=sems,
        compiler_params=pltpu.CompilerParams(collective_id=0, has_side_effects=True, vmem_limit_bytes=60 << 20),
        cost_estimate=CHEAP,
        name="gather_dense",
    )(packed, own, slots, marks)


TILE = 512


def dot(a, b, contract):
    return lax.dot_general(a, b, (contract, ((), ())), preferred_element_type=f32)


NN = ((1,), (0,))
NT = ((1,), (1,))
TN = ((0,), (0,))


def expert_tile(x, dout, up, up_bias, down):
    pre = dot(x, up, NT) + up_bias
    grad_hidden = dot(dout, down, NT)
    square = pre * pre
    inner = jnp.tanh(pre * (GELU_C + GELU_C * GELU_K * square))
    half = 0.5 * pre
    hidden = (half + half * inner).astype(b16)
    slope = 0.5 + 0.5 * inner + half * (1.0 - inner * inner) * (GELU_C + 3.0 * GELU_C * GELU_K * square)
    grad_pre = (slope * grad_hidden).astype(b16)
    return hidden, grad_pre, dot(hidden, down, NN), dot(grad_pre, up, NN)


def bias_rows(first, second):
    row = lax.broadcasted_iota(jnp.int32, (BIAS_ROWS, D), 0)
    return jnp.where(row == 0, first, jnp.where(row == 1, second, 0.0))


def expert_kernel(sources, first, last, part, *refs):
    refs = list(refs)
    weights = [refs.pop(0) for _ in range(sources)]
    x_ref, dout_ref, bias_ref = refs[:3]
    refs = refs[3:]
    sums = [None, None] if first else [refs.pop(0), refs.pop(0)]
    out_ref, grad_x_ref, grad_up_ref, grad_down_ref, w_ref, up_acc, down_acc, bias_acc, sem = refs
    step = pl.program_id(0)

    @pl.when(step == 0)
    def _():
        if sources == 1:
            copy = pltpu.make_async_copy(weights[0], w_ref, sem)
            copy.start()
            copy.wait()
        else:
            me = lax.axis_index("dp")
            inner = (me + 1) // 2 % 2

            @pl.when(inner == 1)
            def _():
                pltpu.make_async_copy(weights[0], w_ref, sem).start()

            @pl.when(inner == 0)
            def _():
                pltpu.make_async_copy(weights[1], w_ref, sem).start()

            pltpu.make_async_copy(weights[0], w_ref, sem).wait()
        up_acc[...] = jnp.zeros_like(up_acc)
        down_acc[...] = jnp.zeros_like(down_acc)
        bias_acc[...] = jnp.zeros_like(bias_acc)

    x = x_ref[...]
    dout = dout_ref[...]
    up = w_ref[:part]
    down = w_ref[part : 2 * part]
    up_bias = w_ref[2 * part :][0:1, :part].astype(f32)
    hidden, grad_pre_b, out, grad_x = expert_tile(x, dout, up, up_bias, down)
    if not first:
        out = out + sums[0][...]
        grad_x = grad_x + sums[1][...]
    if last:
        out = out + bias_ref[1:2, :]
    out_ref[...] = out.astype(out_ref.dtype)
    grad_x_ref[...] = grad_x.astype(grad_x_ref.dtype)
    down_acc[...] += dot(hidden, dout, TN)
    up_acc[...] += dot(grad_pre_b, x, TN)
    bias_acc[0:1, :] += jnp.sum(grad_pre_b.astype(f32), axis=0, keepdims=True)

    @pl.when(step == pl.num_programs(0) - 1)
    def _():
        grad_up_ref[...] = up_acc[...].astype(grad_up_ref.dtype)
        grad_down_ref[:part] = down_acc[...].astype(grad_down_ref.dtype)
        tail = bias_rows(bias_acc[0:1, :], bias_ref[0:1, :])
        grad_down_ref[part:] = tail.astype(grad_down_ref.dtype)


def expert_part(weights, x, dout, biases, sums, last, grad_type, name):
    first = sums is None
    slots = x.shape[0]
    rows = weights[0].shape[0]
    part = (rows - BIAS_ROWS) // 2
    tile = pl.BlockSpec((TILE, D), lambda i: (i, 0))
    kept = b16 if last else f32
    n = len(weights)
    return pl.pallas_call(
        functools.partial(expert_kernel, n, first, last, part),
        grid=(slots // TILE,),
        in_specs=[
            *[pl.BlockSpec(memory_space=pl.ANY)] * n,
            tile,
            tile,
            pl.BlockSpec((2, D), lambda i: (0, 0)),
            *([] if first else [tile, tile]),
        ],
        out_specs=[
            tile,
            tile,
            pl.BlockSpec((part, D), lambda i: (0, 0)),
            pl.BlockSpec((part + BIAS_ROWS, D), lambda i: (0, 0)),
        ],
        out_shape=[
            jax.ShapeDtypeStruct((slots, D), kept),
            jax.ShapeDtypeStruct((slots, D), kept),
            jax.ShapeDtypeStruct((part, D), grad_type),
            jax.ShapeDtypeStruct((part + BIAS_ROWS, D), grad_type),
        ],
        scratch_shapes=[
            pltpu.VMEM((rows, D), b16),
            pltpu.VMEM((part, D), f32),
            pltpu.VMEM((part, D), f32),
            pltpu.VMEM((8, part), f32),
            pltpu.SemaphoreType.DMA,
        ],
        compiler_params=pltpu.CompilerParams(vmem_limit_bytes=56 << 20, dimension_semantics=("arbitrary",)),
        cost_estimate=pl.CostEstimate(flops=48 * slots * part * D, bytes_accessed=slots * D * 20, transcendentals=0),
        name=name,
    )(*weights, x, dout, biases, *([] if first else sums))


SCALE = HEAD_DIM ** (-0.5)
PAIRS = HEADS // 2
WIDE = 2 * HEAD_DIM
CHEAP = pl.CostEstimate(flops=0, bytes_accessed=1024, transcendentals=0)


def normal(values):
    center = values - jnp.mean(values, axis=-1, keepdims=True)
    rate = lax.rsqrt(jnp.mean(center * center, axis=-1, keepdims=True) + NORM_EPS)
    return center * rate, rate


def lanes_like(values):
    return lax.broadcasted_iota(jnp.int32, values.shape, values.ndim - 1)


def scores_of(part_q, pair_k, length):
    scores = dot(part_q, pair_k, NT) * SCALE
    return jnp.where(lanes_like(scores) < length, scores, NEG_FILL)


def halves(pair):
    low = lanes_like(pair) < HEAD_DIM
    zero = jnp.zeros_like(pair)
    return jnp.where(low, pair, zero), jnp.where(low, zero, pair)


def joined(even, odd):
    return jnp.where(lanes_like(even) < HEAD_DIM, even, odd)


def sequence_forward(
    s, lengths_ref, tokens_ref, weights_ref, vector_ref, router_ref, routes_ref, places_ref,
    normed_ref, q_ref, k_ref, v_ref, context_ref, lse_ref, resid_ref, normed_two_ref, gates_ref, slots_ref,
):
    at = pl.ds(s * LEN, LEN)
    length = lengths_ref[s]
    rows = tokens_ref[at, :].astype(f32)
    hat, _ = normal(rows)
    normed = (hat * vector_ref[0:1, :] + vector_ref[1:2, :]).astype(b16)
    normed_ref[at, :] = normed
    q_ref[at, :] = (dot(normed, weights_ref[0], NN) + vector_ref[2:3, :]).astype(b16)
    k_ref[at, :] = dot(normed, weights_ref[1], NN).astype(b16)
    v_ref[at, :] = (dot(normed, weights_ref[2], NN) + vector_ref[3:4, :]).astype(b16)
    lse = jnp.zeros((LEN, 128), f32)
    for pair in range(PAIRS):
        lanes = slice(pair * WIDE, (pair + 1) * WIDE)
        keys, values = k_ref[at, lanes], v_ref[at, lanes]
        mixed = []
        for half, part in enumerate(halves(q_ref[at, lanes])):
            scores = scores_of(part, keys, length)
            top = jnp.max(scores, axis=-1, keepdims=True)
            total = top + jnp.log(jnp.sum(jnp.exp(scores - top), axis=-1, keepdims=True))
            chance = jnp.exp(scores - total).astype(b16)
            mixed.append(dot(chance, values, NN))
            lse = jnp.where(lanes_like(lse) == 2 * pair + half, total, lse)
        context_ref[at, lanes] = joined(*mixed).astype(b16)
    lse_ref[at, :] = lse
    resid = rows + (dot(context_ref[at, :], weights_ref[3], NN) + vector_ref[4:5, :])
    resid_ref[at, :] = resid
    hat, _ = normal(resid)
    normed_two = (hat * vector_ref[5:6, :] + vector_ref[6:7, :]).astype(b16)
    normed_two_ref[at, :] = normed_two
    logits = dot(normed_two, router_ref[...], NT)
    names = lanes_like(logits)
    routes = routes_ref[at, :]
    first = jnp.sum(jnp.where(names == routes[:, 0:1], logits, 0.0), axis=-1, keepdims=True)
    second = jnp.sum(jnp.where(names == routes[:, 1:2], logits, 0.0), axis=-1, keepdims=True)
    gates_ref[at, :] = jnp.where(names == 0, jax.nn.sigmoid(first - second), jax.nn.sigmoid(second - first))
    experts, _, capacity, _ = slots_ref.shape
    slots = experts * capacity
    ids = lax.broadcasted_iota(jnp.int32, (slots, ROWS), 0)
    places = places_ref[s]
    chosen = jnp.where((ids == places[0:1, :]) | (ids == places[1:2, :]), 1.0, 0.0).astype(b16)
    sent = dot(chosen, normed_two, NN).astype(b16)
    slots_ref[:, s] = sent.reshape(experts, capacity, D)


def kept_shapes(count, experts, capacity):
    return [
        *[jax.ShapeDtypeStruct((count, D), b16)] * 5,
        jax.ShapeDtypeStruct((count, 128), f32),
        jax.ShapeDtypeStruct((count, D), f32),
        jax.ShapeDtypeStruct((count, D), b16),
        jax.ShapeDtypeStruct((count, 128), f32),
        jax.ShapeDtypeStruct((experts, count // ROWS, capacity, D), b16),
    ]


def attention_forward(lengths, tokens, weights, vector, router, routes, places, experts, capacity):
    count = tokens.shape[0]
    vmem = pl.BlockSpec(memory_space=pltpu.VMEM)

    def kernel(*refs):
        for s in range(count // LEN):
            sequence_forward(s, *refs)

    return pl.pallas_call(
        kernel,
        in_specs=[pl.BlockSpec(memory_space=pltpu.SMEM), *[vmem] * 6],
        out_specs=[vmem] * 10,
        out_shape=kept_shapes(count, experts, capacity),
        compiler_params=pltpu.CompilerParams(vmem_limit_bytes=48 << 20),
        cost_estimate=CHEAP,
        name="attention_forward",
    )(lengths, tokens, weights, vector, router, routes, places)


def norm_back(grad, hat, rate, gain):
    inner = grad * gain
    return rate * (
        inner
        - jnp.mean(inner, axis=-1, keepdims=True)
        - hat * jnp.mean(inner * hat, axis=-1, keepdims=True)
    )


def two_terms(values):
    high = values.astype(b16)
    return high, (values - high.astype(f32)).astype(b16)


def column_sum(values):
    return jnp.sum(values, axis=0, keepdims=True)


def sequence_backward(
    s, lengths_ref, tokens_ref, grad_ref, weights_ref, vector_ref, router_ref, routes_ref, places_ref,
    normed_ref, q_ref, k_ref, v_ref, context_ref, lse_ref, resid_ref, normed_two_ref, gates_ref, outs_ref, returned_ref,
    output_ref, input_grad_ref, weights_acc, vector_acc, router_acc, dq_ref, dk_ref, dv_ref,
):
    at = pl.ds(s * LEN, LEN)
    length = lengths_ref[s]
    experts, _, capacity, _ = outs_ref.shape
    slots = experts * capacity
    ids = lax.broadcasted_iota(jnp.int32, (ROWS, slots), 1)
    outs = outs_ref[:, s].reshape(slots, D)
    grad_out = grad_ref[at, :].astype(f32)
    places = places_ref[at, :]
    take = [jnp.where(ids == places[:, k : k + 1], 1.0, 0.0).astype(b16) for k in range(2)]
    out = [dot(t, outs, NN) for t in take]
    both_gates = gates_ref[at, :]
    gates = [both_gates[:, k : k + 1] for k in range(2)]
    resid = resid_ref[at, :]
    output_ref[at, :] = resid + gates[0] * out[0] + gates[1] * out[1]
    slopes = [
        jnp.sum(grad_out * out[k], axis=-1, keepdims=True) * (gates[k] * (1.0 - gates[k])) for k in range(2)
    ]
    pull = slopes[0] - slopes[1]
    names = lax.broadcasted_iota(jnp.int32, (ROWS, 128), 1)
    routes = routes_ref[at, :]
    grad_logits = jnp.where(names == routes[:, 0:1], pull, jnp.where(names == routes[:, 1:2], -pull, 0.0))
    high, low = two_terms(grad_logits)
    normed_two = normed_two_ref[at, :]
    router = router_ref[...]
    router_acc[...] += dot(high, normed_two, TN) + dot(low, normed_two, TN)
    returned = returned_ref[:, s].reshape(slots, D)
    grad_two = dot(take[0] + take[1], returned, NN) + (dot(high, router, NN) + dot(low, router, NN))
    hat, rate = normal(resid)
    vector_acc[5:6, :] += column_sum(grad_two * hat)
    vector_acc[6:7, :] += column_sum(grad_two)
    grad_resid = grad_out + norm_back(grad_two, hat, rate, vector_ref[5:6, :])
    input_grad_ref[at, :] = grad_resid
    branch = grad_resid.astype(b16)
    vector_acc[4:5, :] += column_sum(branch.astype(f32))
    weights_acc[3] += dot(context_ref[at, :], branch, TN)
    grad_context = dot(branch, weights_ref[3], NT).astype(b16)
    for pair in range(PAIRS):
        lanes = slice(pair * WIDE, (pair + 1) * WIDE)
        queries, keys, values = q_ref[at, lanes], k_ref[at, lanes], v_ref[at, lanes]
        given = grad_context[:, lanes]
        grads = []
        for half, (part, part_given) in enumerate(zip(halves(queries), halves(given))):
            head = 2 * pair + half
            chance = jnp.exp(scores_of(part, keys, length) - lse_ref[at, head : head + 1])
            grad_v = dot(chance.astype(b16), given, TN)
            grad_chance = dot(part_given, values, NT)
            mean = jnp.sum(chance * grad_chance, axis=-1, keepdims=True)
            grad_scores = (chance * (grad_chance - mean)).astype(b16)
            grads.append((dot(grad_scores, keys, NN), dot(grad_scores, queries, TN), grad_v))
        dq_ref[:, lanes] = (joined(grads[0][0], grads[1][0]) * SCALE).astype(b16)
        dk_ref[:, lanes] = (joined(grads[0][1], grads[1][1]) * SCALE).astype(b16)
        dv_ref[:, lanes] = joined(grads[0][2], grads[1][2]).astype(b16)
    normed = normed_ref[at, :]
    grad_one = jnp.zeros((LEN, D), f32)
    for k, ref in enumerate((dq_ref, dk_ref, dv_ref)):
        weights_acc[k] += dot(normed, ref[...], TN)
        grad_one += dot(ref[...], weights_ref[k], NT)
    vector_acc[2:3, :] += column_sum(dq_ref[...].astype(f32))
    vector_acc[3:4, :] += column_sum(dv_ref[...].astype(f32))
    hat, rate = normal(tokens_ref[at, :].astype(f32))
    vector_acc[0:1, :] += column_sum(grad_one * hat)
    vector_acc[1:2, :] += column_sum(grad_one)
    input_grad_ref[at, :] += norm_back(grad_one, hat, rate, vector_ref[0:1, :])


def begin_kernel(
    n, cols, seqs, part, lengths_ref, in_ref, own_ref, slots_ref, marks_ref, tokens_ref, routes_ref, places_ref,
    weights_ref, vector_ref, router_ref, normed_ref, q_ref, k_ref, v_ref, context_ref, lse_ref, resid_ref, normed_two_ref,
    gates_ref, out_ref, back_ref, mine_up, mine_down, near_up, near_down, middle_up, middle_down, far_up, far_down,
    near_up_in, near_down_in,
    pool, acc, second_ref, third_ref, fourth_ref, going, x_in, dout_in, marks_in, out_acc, back_acc, bias_acc, tail_ref,
    local_sem, part_s, part_r, slot_s, slot_r, mark_s, mark_r, x_s, x_r, near_s, near_r, store_s, *sems,
):
    side, z, y, x, core = where_am_i()
    mine = lax.axis_index("expert")
    experts, _, capacity, _ = slots_ref.shape
    slots = experts * seqs * capacity
    greet([*peers_of(n, side, z, y, x, core)[0], *[(z, (mine + k) % experts) for k in range(1, experts)]])
    me = ((z * side + y) * side + x) * 2 + core
    block_rows = in_ref.shape[0]
    stage_rows = 2 * part + BIAS_ROWS

    def block_at(device):
        return pool.at[pl.ds(pl.multiple_of(device * block_rows, 16), block_rows), :]

    def sender(ref, e, b=0, blocks=seqs):
        return ref.at[pl.ds(pl.multiple_of((e * seqs + b) * capacity, 16), blocks * capacity), :]

    flat_slots = slots_ref.reshape(slots, D)
    flat_marks = marks_ref.reshape(slots, 128)
    stays = [
        pltpu.make_async_copy(in_ref, block_at(me), local_sem.at[0]),
        pltpu.make_async_copy(sender(flat_slots, mine), sender(dout_in, mine), local_sem.at[1]),
        pltpu.make_async_copy(sender(flat_marks, mine), sender(marks_in, mine), local_sem.at[2]),
    ]
    for copy in stays:
        copy.start()
    inner = (z + 1) // 2 % 2 == 1
    outer = jnp.logical_not(inner)
    inward, across, outward = (1 + z // 2, mine), (3 - z, mine), (3 * (z // 2), mine)

    def hop(k, src, dst, peer):
        return remote(src, dst, part_s.at[k], part_r.at[k], peer)

    beside = hop(0, own_ref, second_ref, (z + 1 - 2 * (z % 2), mine))
    own_across = hop(1, own_ref, third_ref, across)
    third_on = hop(2, third_ref, third_ref, outward)
    second_across = hop(3, second_ref, fourth_ref, across)
    fourth_on = hop(4, fourth_ref, fourth_ref, outward)

    def weights_on():
        beside.start()

        @pl.when(inner)
        def _():
            own_across.start()

    early = [
        (lambda e: sender(flat_slots, e), lambda e: sender(dout_in, e), slot_s, slot_r),
        (lambda e: sender(flat_marks, e), lambda e: sender(marks_in, e), mark_s, mark_r),
    ]
    more = []
    sent = spread_blocks(n, in_ref, block_at, sems, weights_on, lambda: exchange_all(early, more))
    stays[0].wait()

    for pair in range(2):
        def spread(device, carry):
            rows = block_at(device)[2 * pair * cols : 2 * (pair + 1) * cols, :].astype(f32)
            place = pl.ds(pl.multiple_of(device * cols, 8), cols)
            acc[0, place, :] = rows[:cols]
            acc[1, place, :] = rows[cols:]
            return carry

        lax.fori_loop(0, n * experts, spread, 0)
        weights_ref[2 * pair] = acc[0].astype(b16)
        weights_ref[2 * pair + 1] = acc[1].astype(b16)

    def gather_small(device, total):
        return total + block_at(device)[4 * cols :, :].astype(f32)

    small = lax.fori_loop(0, n * experts, gather_small, jnp.zeros((block_rows - 4 * cols, D), f32))
    vector_ref[...] = small[:8]
    router_ref[...] = jnp.zeros_like(router_ref)
    router_ref[: block_rows - 4 * cols - 8, :] = small[8:].astype(b16)

    late = []
    for s in range(seqs):
        sequence_forward(
            s, lengths_ref, tokens_ref, weights_ref, vector_ref, router_ref, routes_ref, places_ref,
            normed_ref, q_ref, k_ref, v_ref, context_ref, lse_ref, resid_ref, normed_two_ref, gates_ref, going,
        )
        dst = functools.partial(sender, x_in, b=s, blocks=1)
        late.append((functools.partial(lambda e, s: going.at[e, s], s=s), dst, x_s.at[s], x_r.at[s]))
        exchange_all(late[-1:], more)
        stays.append(pltpu.make_async_copy(going.at[mine, s], dst(mine), local_sem.at[3 + s]))
        stays[-1].start()
    beside.wait()

    @pl.when(inner)
    def _():
        second_across.start()
        own_across.wait()
        third_on.start()

    wait_all(early)
    wait_all(late)
    for copy in [*sent, *more]:
        copy.wait_send()
    for copy in stays[1:]:
        copy.wait()

    up_acc, down_acc = acc.at[0], acc.at[1]
    tiles = slots // TILE
    down_bias = jnp.zeros((1, D), f32)
    stores = []
    outs = [(mine_up, mine_down), (near_up, near_down), (middle_up, middle_down), (far_up, far_down)]
    near_in = (near_up_in, near_down_in)
    bias_acc[...] = jnp.zeros_like(bias_acc)
    for p, w_ref in enumerate((own_ref, second_ref, third_ref, fourth_ref)):
        if p == 1:

            @pl.when(inner)
            def _():
                second_across.wait()
                fourth_on.start()

        if p == 2:

            @pl.when(outer)
            def _():
                third_on.wait_recv()

        if p == 3:

            @pl.when(outer)
            def _():
                fourth_on.wait_recv()

        down_bias = down_bias + w_ref[2 * part :, :].astype(f32)[1:2, :]
        up_acc[...] = jnp.zeros_like(up_acc)
        down_acc[...] = jnp.zeros_like(down_acc)
        bias_acc[0:1, :] = jnp.zeros((1, D), f32)

        def tile(t, carry):
            rows = pl.ds(pl.multiple_of(t * TILE, TILE), TILE)
            x = x_in[rows, :]
            if p == 0:
                logits = dot(x, router_ref[...], NT)
                signs = jnp.where(lanes_like(logits) == mine, 1.0, -marks_in[rows, :].astype(f32))
                margin = jnp.sum(logits * signs, axis=-1, keepdims=True)
                dout = (jax.nn.sigmoid(margin) * dout_in[rows, :].astype(f32)).astype(b16)
                dout_in[rows, :] = dout
                bias_acc[1:2, :] += column_sum(dout.astype(f32))
            else:
                dout = dout_in[rows, :]
            up_bias = w_ref[2 * part :, :].astype(f32)[0:1, :part]
            hidden, grad_pre, out, back = expert_tile(x, dout, w_ref[:part, :], up_bias, w_ref[part : 2 * part, :])
            down_acc[...] += dot(hidden, dout, TN)
            up_acc[...] += dot(grad_pre, x, TN)
            bias_acc[0:1, :] += column_sum(grad_pre.astype(f32))
            if p == 0:
                out_acc[rows, :] = out
                back_acc[rows, :] = back
            elif p < 3:
                out_acc[rows, :] += out
                back_acc[rows, :] += back
            else:
                x_in[rows, :] = (out_acc[rows, :] + out + down_bias).astype(b16)
                dout_in[rows, :] = (back_acc[rows, :] + back).astype(b16)
            return carry

        lax.fori_loop(0, tiles, tile, 0)
        tail = bias_rows(bias_acc[0:1, :], bias_acc[1:2, :])
        base = stage_rows if p > 1 else 0
        if p == 0:
            tail_ref[...] = tail
            now = [
                pltpu.make_async_copy(up_acc, mine_up, store_s.at[0]),
                pltpu.make_async_copy(down_acc, mine_down.at[pl.ds(0, part), :], store_s.at[1]),
                pltpu.make_async_copy(tail_ref, mine_down.at[pl.ds(part, BIAS_ROWS), :], store_s.at[2]),
            ]
            for copy in now:
                copy.start()
            for copy in now:
                copy.wait()
        else:
            if p == 3:
                for copy in stores[2:]:
                    copy.wait()
                del stores[2:]
            pool[base : base + part, :] = up_acc[...].astype(b16)
            pool[base + part : base + 2 * part, :] = down_acc[...].astype(b16)
            pool[base + 2 * part : base + stage_rows, :] = tail.astype(b16)
            halves_of = [pool.at[pl.ds(base, part), :], pool.at[pl.ds(base + part, part + BIAS_ROWS), :]]
            for h in range(2):
                stores.append(pltpu.make_async_copy(halves_of[h], outs[p][h], store_s.at[1 + 2 * p + h]))
                stores[-1].start()
            if p == 1:
                nears = [remote(halves_of[h], near_in[h], near_s.at[h], near_r.at[h], inward) for h in range(2)]

                @pl.when(outer)
                def _():
                    for copy in nears:
                        copy.start()

    for src, dst, k in ((x_in, out_ref, 9), (dout_in, back_ref, 10)):
        stores.append(pltpu.make_async_copy(src, dst, store_s.at[k]))
        stores[-1].start()
    for copy in stores:
        copy.wait()

    @pl.when(inner)
    def _():
        third_on.wait_send()
        fourth_on.wait_send()
        for copy in nears:
            copy.wait_recv()

    @pl.when(outer)
    def _():
        for copy in nears:
            copy.wait_send()


def begin(n, side, cols, lengths, packed, own, slots, marks, tokens, routes, places):
    devices = n * side * side * 2
    experts, blocks, capacity, _ = slots.shape
    count = tokens.shape[0]
    total = experts * blocks * capacity
    part = (own.shape[0] - BIAS_ROWS) // 2
    dma = pltpu.SemaphoreType.DMA
    vmem, hbm = pl.BlockSpec(memory_space=pltpu.VMEM), pl.BlockSpec(memory_space=pl.ANY)
    *kept, going = kept_shapes(count, experts, capacity)

    def halves_in(dtype):
        return [jax.ShapeDtypeStruct((part, D), dtype), jax.ShapeDtypeStruct((part + BIAS_ROWS, D), dtype)]

    return pl.pallas_call(
        functools.partial(begin_kernel, n, cols, blocks, part),
        out_shape=[
            jax.ShapeDtypeStruct((4, D, D), b16),
            jax.ShapeDtypeStruct((8, D), f32),
            jax.ShapeDtypeStruct((128, D), b16),
            *kept,
            *[jax.ShapeDtypeStruct((total, D), b16)] * 2,
            *halves_in(f32),
            *halves_in(b16) * 4,
        ],
        in_specs=[pl.BlockSpec(memory_space=pltpu.SMEM), vmem, vmem, hbm, hbm, vmem, vmem, vmem],
        out_specs=[*[vmem] * 12, *[hbm] * 12],
        scratch_shapes=[
            pltpu.VMEM((max(devices * packed.shape[0], 2 * own.shape[0]), D), b16),
            pltpu.VMEM((2, D, D), f32),
            *[pltpu.VMEM(own.shape, b16)] * 3,
            pltpu.VMEM(going.shape, b16),
            *[pltpu.VMEM((total, D), b16)] * 2,
            pltpu.VMEM((total, 128), b16),
            *[pltpu.VMEM((total, D), f32)] * 2,
            pltpu.VMEM((8, D), f32),
            pltpu.VMEM((BIAS_ROWS, D), f32),
            dma((3 + blocks,)),
            *[dma((5,))] * 2,
            *[dma((experts,))] * 4,
            *[dma((blocks, experts))] * 2,
            *[dma((2,))] * 2,
            dma((11,)),
            *spread_sems(n, side),
        ],
        compiler_params=pltpu.CompilerParams(collective_id=0, has_side_effects=True, vmem_limit_bytes=63 << 20),
        cost_estimate=CHEAP,
        name="begin",
    )(lengths, packed, own, slots, marks, tokens, routes, places)


KINDS = 5
FAR, MIDDLE, FAR_ON, MIDDLE_ON, FAR_LAST = range(KINDS)


def finish_kernel(
    n, cols, extra, seqs,
    lengths_ref, tokens_ref, grad_ref, weights_ref, vector_ref, router_ref, routes_ref, places_ref,
    normed_ref, q_ref, k_ref, v_ref, context_ref, lse_ref, resid_ref, normed_two_ref, gates_ref, outs_ref, backs_ref,
    near_up, near_down, middle_up, middle_down, far_up, far_down,
    output_ref, input_grad_ref, dense_ref, middle_up_in, middle_down_in, end_up_in, end_down_in,
    outs_in, backs_in, weights_acc, vector_acc, router_acc, dq_ref, dk_ref, dv_ref,
    far_up_buf, far_down_buf, middle_up_buf, middle_down_buf, on_up_buf, on_down_buf, load_up, load_down,
    parts, stage, c_buf, b_buf, a_buf, z_buf,
    own_s, out_s, out_r, back_s, back_r, chain_s, chain_r, load_s, c_s, c_r, b_s, b_r, a_s, a_r, z_s, z_r,
):
    inside = cols % 8 == 0
    side, z, y, x, core = where_am_i()
    mine = lax.axis_index("expert")
    experts = outs_in.shape[0]
    along_z, first, second, sibling = peers_of(n, side, z, y, x, core)
    plane = [(z, (mine + k) % experts) for k in range(1, experts)]
    greet([*along_z, *plane])
    area = side * side if inside else 0
    sent = []

    def send(src, dst, send_sem, recv_sem, peer):
        copy = remote(src, dst, send_sem, recv_sem, peer)
        copy.start()
        sent.append(copy)

    for k in range(1, experts):
        to = (mine + k) % experts
        send(outs_ref.at[to], outs_in.at[mine], out_s.at[k], out_r.at[k], plane[k - 1])
    for k in range(1, experts):
        to = (mine + k) % experts
        send(backs_ref.at[to], backs_in.at[mine], back_s.at[k], back_r.at[k], plane[k - 1])
    own = [
        pltpu.make_async_copy(outs_ref.at[mine], outs_in.at[mine], own_s.at[0]),
        pltpu.make_async_copy(backs_ref.at[mine], backs_in.at[mine], own_s.at[1]),
    ]
    for copy in own:
        copy.start()

    inner = (z + 1) // 2 % 2 == 1
    outer = jnp.logical_not(inner)
    inward = (z - z + 1 + z // 2, mine)
    across = (3 - z, mine)
    outward = (3 * (z // 2), mine)
    near, middle, far = (near_up, near_down), (middle_up, middle_down), (far_up, far_down)
    middle_in = (middle_up_in, middle_down_in)
    end_in = (end_up_in, end_down_in)
    far_buf, middle_buf, on_buf = (far_up_buf, far_down_buf), (middle_up_buf, middle_down_buf), (on_up_buf, on_down_buf)
    loads = (load_up, load_down)

    def hop(kind, half, src, dst, peer):
        return remote(src, dst, chain_s.at[kind, half], chain_r.at[kind, half], peer)

    from_ends = [(FAR, far, far_buf), (MIDDLE, middle, middle_buf)]

    @pl.when(outer)
    def _():
        for kind, src, dst in from_ends:
            for half in range(2):
                hop(kind, half, src[half], dst[half], inward).start()

    def chain_step(kind, half, buf, term, next_kind, target, peer):
        @pl.when(inner)
        def _():
            load = pltpu.make_async_copy(term[half], loads[half], load_s)
            load.start()
            hop(kind, half, buf[half], buf[half], across).wait_recv()
            load.wait()
            buf[half][...] = (buf[half][...].astype(f32) + loads[half][...].astype(f32)).astype(b16)
            hop(next_kind, half, buf[half], target[half], peer).start()

    def step_far(half):
        chain_step(FAR, half, far_buf, far, FAR_ON, on_buf, across)

    def step_on(half):
        chain_step(FAR_ON, half, on_buf, near, FAR_LAST, end_in, outward)

    def step_middle(half):
        chain_step(MIDDLE, half, middle_buf, middle, MIDDLE_ON, middle_in, across)

    weights_acc[...] = jnp.zeros_like(weights_acc)
    vector_acc[...] = jnp.zeros_like(vector_acc)
    router_acc[...] = jnp.zeros_like(router_acc)
    step_far(0)
    step_far(1)
    step_on(0)
    for copy in own:
        copy.wait()
    for k in range(1, experts):
        block = outs_in.at[(mine - k + experts) % experts]
        remote(block, block, out_s.at[k], out_r.at[k], sibling).wait_recv()
        block = backs_in.at[(mine - k + experts) % experts]
        remote(block, block, back_s.at[k], back_r.at[k], sibling).wait_recv()
    for s in range(seqs):
        sequence_backward(
            s, lengths_ref, tokens_ref, grad_ref, weights_ref, vector_ref, router_ref, routes_ref, places_ref,
            normed_ref, q_ref, k_ref, v_ref, context_ref, lse_ref, resid_ref, normed_two_ref, gates_ref, outs_in, backs_in,
            output_ref, input_grad_ref, weights_acc, vector_acc, router_acc, dq_ref, dk_ref, dv_ref,
        )
        if s == 0:
            step_on(1)
            step_middle(0)

    small = jnp.concatenate([vector_acc[...], router_acc[: extra - 8, :]], axis=0).astype(b16)
    if not inside:
        dense_ref[:extra, :] = jnp.concatenate([vector_acc[...], router_acc[: extra - 8, :]], axis=0)
        for k in range(4):
            dense_ref[extra + k * D : extra + (k + 1) * D, :] = weights_acc[k]
        step_middle(1)
    for core_ in range(2 if inside else 0):
        for y_ in range(side):
            for x_ in range(side):
                for z_ in range(n):
                    owner = ((z_ * side + y_) * side + x_) * 2 + core_
                    rows = [weights_acc[k, owner * cols : (owner + 1) * cols, :] for k in range(4)]
                    place = parts.at[(core_ * side + y_) * side + x_, z_]
                    place[: 4 * cols, :] = jnp.concatenate(rows, axis=0).astype(b16)
                    place[4 * cols :, :] = small

    def piece(ka, kb, core_):
        y_ = (y + core * ka + (1 - core) * kb) % side
        x_ = (x + (1 - core) * ka + core * kb) % side
        return (core_ * side + y_) * side + x_

    order = [(ka, kb) for kb in [*range(1, side), 0] for ka in [*range(1, side), 0]][:area]
    for ka, kb in order:
        place = ka * side + kb
        send(parts.at[piece(kb, ka, 1 - core)], c_buf.at[place], c_s.at[place], c_r.at[place], sibling)
    for ka, kb in order:
        place = ka * side + kb
        remote(c_buf.at[place], c_buf.at[place], c_s.at[place], c_r.at[place], sibling).wait_recv()
        mine_ = piece(ka, kb, core)
        if kb:
            stage[place] = (parts[mine_].astype(f32) + c_buf[place].astype(f32)).astype(b16)
            send(stage.at[place], b_buf.at[place], b_s.at[place], b_r.at[place], second[kb - 1])
            if ka == 0:
                step_middle(1)
        else:
            total = parts[mine_].astype(f32) + c_buf[place].astype(f32)
            for k in range(1, side):
                slot = ka * side + k
                remote(b_buf.at[slot], b_buf.at[slot], b_s.at[slot], b_r.at[slot], sibling).wait_recv()
                total = total + b_buf[slot].astype(f32)
            if ka:
                stage[place] = total.astype(b16)
                send(stage.at[place], a_buf.at[ka], a_s.at[ka], a_r.at[ka], first[ka - 1])
            else:
                for k in range(1, side):
                    remote(a_buf.at[k], a_buf.at[k], a_s.at[k], a_r.at[k], sibling).wait_recv()
                    total = total + a_buf[k].astype(f32)
                stage[place] = total.astype(b16)
    if inside:
        for k in range(1, n):
            send(stage.at[0, (z + k) % n], z_buf.at[k], z_s.at[k], z_r.at[k], along_z[k - 1])
        result = stage[0, z].astype(f32)
        for k in range(1, n):
            remote(z_buf.at[k], z_buf.at[k], z_s.at[k], z_r.at[k], sibling).wait_recv()
            result = result + z_buf[k].astype(f32)
        dense_ref[...] = result
    for copy in sent:
        copy.wait_send()

    @pl.when(outer)
    def _():
        for half in range(2):
            for kind, src, dst in from_ends:
                hop(kind, half, src[half], dst[half], inward).wait_send()
            hop(FAR_LAST, half, end_in[half], end_in[half], inward).wait_recv()

    @pl.when(inner)
    def _():
        for half in range(2):
            hop(FAR_ON, half, far_buf[half], on_buf[half], across).wait_send()
            hop(FAR_LAST, half, on_buf[half], end_in[half], outward).wait_send()
            hop(MIDDLE_ON, half, middle_buf[half], middle_in[half], across).wait_send()
            hop(MIDDLE_ON, half, middle_in[half], middle_in[half], across).wait_recv()


def finish(n, side, cols, extra, lengths, rows_in, kept, outs, backs, grads):
    count = rows_in[0].shape[0]
    slots = outs.shape
    vmem = pl.BlockSpec(memory_space=pltpu.VMEM)
    hbm = pl.BlockSpec(memory_space=pl.ANY)
    shapes = [jax.ShapeDtypeStruct(g.shape, b16) for g in grads[:2]]
    inside = cols % 8 == 0
    rows = 4 * cols + extra if inside else 4 * D + extra
    block = (n, rows, D) if inside else (1, 16, 128)
    dma = pltpu.SemaphoreType.DMA
    half = [pltpu.VMEM(g.shape, b16) for g in grads[:2]]
    area = side * side
    return pl.pallas_call(
        functools.partial(finish_kernel, n, cols, extra, count // LEN),
        in_specs=[
            pl.BlockSpec(memory_space=pltpu.SMEM),
            *[vmem] * (len(rows_in) + len(kept)),
            hbm,
            hbm,
            *[hbm] * len(grads),
        ],
        out_specs=[vmem, vmem, vmem, *[hbm] * 4],
        out_shape=[
            jax.ShapeDtypeStruct((count, D), f32),
            jax.ShapeDtypeStruct((count, D), f32),
            jax.ShapeDtypeStruct((rows, D), f32),
            *shapes * 2,
        ],
        scratch_shapes=[
            pltpu.VMEM(slots, b16),
            pltpu.VMEM(slots, b16),
            pltpu.VMEM((4, D, D), f32),
            pltpu.VMEM((8, D), f32),
            pltpu.VMEM((128, D), f32),
            *[pltpu.VMEM((LEN, D), b16)] * 3,
            *half * 4,
            pltpu.VMEM((2 * area, *block), b16),
            pltpu.VMEM((area, *block), b16),
            pltpu.VMEM((area, *block), b16),
            pltpu.VMEM((area, *block), b16),
            pltpu.VMEM((side, *block), b16),
            pltpu.VMEM(block, b16),
            dma((2,)),
            *[dma((slots[0],))] * 4,
            *[dma((KINDS, 2))] * 2,
            dma,
            *[dma((area,))] * 4,
            *[dma((side,))] * 2,
            *[dma((n,))] * 2,
        ],
        compiler_params=pltpu.CompilerParams(collective_id=1, has_side_effects=True, vmem_limit_bytes=63 << 20),
        cost_estimate=CHEAP,
        name="finish",
    )(lengths, *rows_in, *kept, outs, backs, *grads)


def pack_expert(up, down, up_bias, down_bias, start, dtype):
    part = up.shape[0]
    tail = jnp.zeros((BIAS_ROWS, D), dtype)
    tail = tail.at[0, :part].set(up_bias.astype(dtype))
    tail = lax.dynamic_update_slice(tail, down_bias.astype(dtype)[None], (1, start))
    return jnp.concatenate([up.astype(dtype), down.astype(dtype), tail], axis=0)


def along(x, *pairs):
    return lax.ppermute(x, "dp", pairs)


def body(
    tokens, out_grad, routes, lengths,
    attention, gain_bias, router, expert_up, up_bias, expert_down, down_bias,
    first_attention, first_gain_bias, first_router, first_expert_up, first_up_bias, first_expert_down, first_down_bias,
    square_attention, square_gain_bias, square_router, square_expert_up, square_up_bias, square_expert_down, square_down_bias,
):
    experts = router.shape[0]
    capacity = 4 * ROWS // experts
    count = tokens.shape[0]
    blocks = count // ROWS
    part = expert_up.shape[1]
    narrow = down_bias.shape[1]
    cols = attention.shape[1]
    devices = D // cols
    n_dp = lax.axis_size("dp")
    assert n_dp == 4 and expert_up.shape[0] == 1
    me = lax.axis_index("dp")
    mine = lax.axis_index("expert")
    both = ("dp", "expert")

    side = math.isqrt(experts // 2)
    inside = cols if cols % 8 == 0 else 0
    small_rows = -(-(8 + experts) // 16) * 16
    flat_len = (7 + experts) * cols
    if inside:
        small = jnp.zeros((small_rows, D), b16)
        column = (me * experts + mine) * cols
        small = lax.dynamic_update_slice(small, gain_bias.astype(b16), (0, column))
        small = lax.dynamic_update_slice(small, router.astype(b16), (8, column))
    else:
        extra = -(-(4 * cols + -(-flat_len // D)) // 16) * 16 - 4 * cols
        small = jnp.concatenate([gain_bias, router], axis=0).astype(b16).reshape(-1)
        small = jnp.pad(small, (0, extra * D - flat_len)).reshape(extra, D)
    packed = jnp.concatenate([attention.astype(b16).reshape(4 * cols, D), small], axis=0)
    own = pack_expert(expert_up[0], expert_down[0], up_bias[0], down_bias[0], me * narrow, b16)

    positions = slots_of(routes, experts, capacity)
    slot_ids = jnp.arange(experts * capacity, dtype=jnp.int32)
    hit = positions[:, :, :, None] == slot_ids
    split = jnp.any(hit, axis=2).astype(b16).reshape(blocks, ROWS, experts, capacity)
    marked = jnp.any(routes[:, :, None] == jnp.arange(128, dtype=jnp.int32), axis=1).astype(b16)

    def by_slot(rows):
        sent = jnp.einsum("btec,btd->ebcd", split, rows.reshape(blocks, ROWS, -1), preferred_element_type=f32)
        return sent.astype(b16)

    places = positions.transpose(0, 2, 1)
    inner = (me == 1) | (me == 2)
    if inside:
        weights_b, vector_all, router_all, *got = begin(
            n_dp, side, cols, lengths, packed, own, by_slot(out_grad), by_slot(marked), tokens, routes, places
        )
        kept, out_b, back_b, grads, near_in = got[:9], got[9], got[10], got[11:19], got[19:]
    else:
        whole, second, third_inner, grad_slots, marks = gather_dense(
            packed, own, by_slot(out_grad), by_slot(marked), n_dp, side
        )
        weights_b = whole[:, : 4 * cols].reshape(devices, 4, cols, D).transpose(1, 0, 2, 3).reshape(4, D, D)
        small = whole[:, 4 * cols :].reshape(devices, extra * D)[:, :flat_len].reshape(devices, 7 + experts, cols)
        small = small.transpose(1, 0, 2).reshape(7 + experts, D)
        vector_all = jnp.pad(small[:7].astype(f32), ((0, 1), (0, 0)))
        router_all = jnp.pad(small[7:], ((0, 128 - experts), (0, 0)))
        *kept, slots_out = attention_forward(
            lengths, tokens, weights_b, vector_all, router_all, routes, places, experts, capacity
        )
        slots_in = lax.all_to_all(slots_out, "expert", split_axis=0, concat_axis=0, tiled=True)
        slots_in = slots_in.reshape(experts * blocks * capacity, D)
        grad_slots = grad_slots.reshape(experts * blocks * capacity, D)
        marks = marks.reshape(experts * blocks * capacity, 128)
        third_outer = along(third_inner, (1, 0), (2, 3))
        fourth_inner = along(second, (1, 2), (2, 1))
        fourth_outer = along(fourth_inner, (1, 0), (2, 3))
        slot_logits = jnp.einsum("sd,ed->se", slots_in, router_all, preferred_element_type=f32)
        this = jnp.arange(128, dtype=jnp.int32) == mine
        margin = jnp.sum(slot_logits * jnp.where(this, 1.0, -marks.astype(f32)), axis=-1)
        dout = (jax.nn.sigmoid(margin)[:, None] * grad_slots.astype(f32)).astype(b16)
        grad_down_bias = jnp.sum(dout.astype(f32), axis=0)
        row = 2 * part + 1
        down_bias_full = own[row].astype(f32) + second[row].astype(f32)
        down_bias_full += jnp.where(inner, third_inner[row], third_outer[row]).astype(f32)
        down_bias_full += jnp.where(inner, fourth_inner[row], fourth_outer[row]).astype(f32)
        biases = jnp.stack([grad_down_bias, down_bias_full])
        weights = [(own,), (second,), (third_inner, third_outer), (fourth_inner, fourth_outer)]
        sums = None
        grads = []
        for i in range(4):
            *sums, grad_up, grad_down = expert_part(
                weights[i], slots_in, dout, biases, sums, i == 3, b16 if i else f32, f"expert_part_{i}"
            )
            grads += [grad_up, grad_down]
        out_b, back_b = sums
        near_in = [along(g, (0, 1), (3, 2)) for g in grads[2:4]]

    slots_shape = (experts, blocks, capacity, D)
    output, input_grad, dense, *came = finish(
        n_dp, side, cols, small_rows, lengths,
        (tokens, out_grad, weights_b, vector_all, router_all, routes, positions.reshape(count, 2)),
        kept, out_b.reshape(slots_shape), back_b.reshape(slots_shape), grads[2:],
    )
    totals = [
        grads[i]
        + jnp.where(inner, near_in[i].astype(f32) + came[i].astype(f32), came[2 + i].astype(f32))
        for i in range(2)
    ]
    shard_up = totals[0][None]
    shard_down = totals[1][:part][None]
    shard_up_bias = totals[1][part, :part][None]
    shard_down_bias = lax.dynamic_slice(totals[1], (part + 1, me * narrow), (1, narrow))
    if cols % 8:
        small = lax.psum(dense[:small_rows], both)
        big = dense[small_rows:].reshape(4, D, D).astype(b16)
        big = lax.psum_scatter(big, both, scatter_dimension=1, tiled=True).astype(f32)
        dense = jnp.concatenate([big.reshape(4 * cols, D), small], axis=0)
    shard_weights = dense[: 4 * cols].reshape(4, cols, D)
    small = lax.dynamic_slice(
        dense[4 * cols :], (0, (me * experts + mine) * cols), (small_rows, cols)
    )
    shard_vector, shard_router = small[:7], small[8 : 8 + experts]

    params = (attention, gain_bias, router, expert_up, up_bias, expert_down, down_bias)
    grads = (shard_weights, shard_vector, shard_router, shard_up, shard_up_bias, shard_down, shard_down_bias)
    firsts = (first_attention, first_gain_bias, first_router, first_expert_up, first_up_bias, first_expert_down, first_down_bias)
    squares = (square_attention, square_gain_bias, square_router, square_expert_up, square_up_bias, square_expert_down, square_down_bias)
    hidden_units = n_dp * part
    rates = (1.6 * D ** (-0.5), 0.3, 0.5 * D ** (-0.5), 1.5 * D ** (-0.5), 0.25, 0.5 * hidden_units ** (-0.5), 0.25)
    updated = [adam_step(params[i], grads[i], firsts[i], squares[i], rates[i]) for i in range(7)]
    return (output, input_grad, *grads, *(u[0] for u in updated), *(u[1] for u in updated), *(u[2] for u in updated))


def solution(mesh):
    rows = P(("dp", "expert"), None)
    state = (
        P(None, ("dp", "expert"), None),
        P(None, ("dp", "expert")),
        P(None, ("dp", "expert")),
        P("expert", "dp", None),
        P("expert", "dp"),
        P("expert", "dp", None),
        P("expert", "dp"),
    )
    return jax.shard_map(
        body,
        mesh=mesh,
        in_specs=(rows, rows, rows, P(("dp", "expert")), *state, *state, *state),
        out_specs=(rows, rows, *state, *state, *state, *state),
        check_vma=False,
    )
```

```python
import functools
import math

import jax
import jax.numpy as jnp
from jax import lax
from jax.experimental import pallas as pl
from jax.experimental.pallas import tpu as pltpu
from jax.sharding import PartitionSpec as P

D = 768
HEADS = 12
HEAD_DIM = 64
LEN = 256
STEP = 3
ROWS = 256
BIAS_ROWS = 16

NORM_EPS = 1e-06
NEG_FILL = -1000000000.0
BETA_ONE = 0.9
BETA_TWO = 0.95
WEIGHT_DECAY = 0.1
ADAM_EPS = 1e-08
GELU_C = 0.7978845608028654
GELU_K = 0.044715
f32 = jnp.float32
b16 = jnp.bfloat16
MESH = pl.DeviceIdType.MESH


def adam_step(weight, grad, first, square, rate):
    new_first = BETA_ONE * first + (1.0 - BETA_ONE) * grad
    new_square = BETA_TWO * square + (1.0 - BETA_TWO) * grad * grad
    first_hat = new_first / (1.0 - BETA_ONE**STEP)
    square_hat = new_square / (1.0 - BETA_TWO**STEP)
    update = -rate * (first_hat / (jnp.sqrt(square_hat) + ADAM_EPS) + WEIGHT_DECAY * weight)
    return (weight + update, new_first, new_square)


def slots_of(routes, experts, capacity):
    flat = routes.reshape(-1, 2 * ROWS)
    onehot = (flat[:, :, None] == jnp.arange(experts, dtype=jnp.int32)).astype(b16)
    row = lax.broadcasted_iota(jnp.int32, (2 * ROWS, 2 * ROWS), 0)
    col = lax.broadcasted_iota(jnp.int32, (2 * ROWS, 2 * ROWS), 1)
    earlier = (col < row).astype(b16)
    before = jnp.einsum("ij,bje->bie", earlier, onehot, preferred_element_type=f32)
    slot = jnp.sum(before * onehot.astype(f32), axis=-1).astype(jnp.int32)
    return (flat * capacity + slot).reshape(-1, ROWS, 2)


def where_am_i():
    side = math.isqrt(lax.axis_size("expert") // 2)
    spot = lax.axis_index("expert")
    return side, lax.axis_index("dp"), spot // (2 * side), spot // 2 % side, spot % 2


def greet(peers):
    barrier = pltpu.get_barrier_semaphore()
    for peer in peers:
        pl.semaphore_signal(barrier, inc=1, device_id=peer, device_id_type=MESH)
    pl.semaphore_wait(barrier, len(peers))


def peers_of(n, side, z, y, x, core):
    def at(z_, y_, x_, core_):
        return (z_, (y_ * side + x_) * 2 + core_)

    along_z = [at((z + k) % n, y, x, core) for k in range(1, n)]
    first = [at(z, (y + core * k) % side, (x + (1 - core) * k) % side, core) for k in range(1, side)]
    second = [at(z, (y + (1 - core) * k) % side, (x + core * k) % side, core) for k in range(1, side)]
    return along_z, first, second, at(z, y, x, 1 - core)


def remote(src, dst, send, recv, peer):
    return pltpu.make_async_remote_copy(
        src_ref=src, dst_ref=dst, send_sem=send, recv_sem=recv, device_id=peer, device_id_type=MESH
    )


def spread_blocks(n, in_ref, block_at, sems, meanwhile, at_last):
    z_s, z_r, a_s, a_r, b_s, b_r, c_s, c_r = sems
    side, z, y, x, core = where_am_i()
    along_z, first, second, sibling = peers_of(n, side, z, y, x, core)
    sent = []

    def block(j, ka, kb, core_):
        y_ = (y - core * ka - (1 - core) * kb + 2 * side) % side
        x_ = (x - (1 - core) * ka - core * kb + 2 * side) % side
        return block_at(((((z - j + n) % n) * side + y_) * side + x_) * 2 + core_)

    def send(src, dst, send_sem, recv_sem, peer):
        copy = remote(src, dst, send_sem, recv_sem, peer)
        copy.start()
        sent.append(copy)

    def pass_on(src, dst, j, ka, kb):
        if kb == 0:
            if ka == 0:
                for k in range(1, side):
                    send(src, dst, a_s.at[j * side + k], a_r.at[j * side + k], first[k - 1])
            for k in range(1, side):
                place = (j * side + ka) * side + k
                send(src, dst, b_s.at[place], b_r.at[place], second[k - 1])
        place = (j * side + kb) * side + ka
        send(src, dst, c_s.at[place], c_r.at[place], sibling)

    for k in range(1, n):
        send(in_ref, block(0, 0, 0, core), z_s.at[k], z_r.at[k], along_z[k - 1])
    meanwhile()
    pass_on(in_ref, block(0, 0, 0, core), 0, 0, 0)
    for j in range(1, n):
        here = block(j, 0, 0, core)
        remote(here, here, z_s.at[j], z_r.at[j], sibling).wait_recv()
        pass_on(here, here, j, 0, 0)
    for j in range(n):
        for ka in range(1, side):
            here = block(j, ka, 0, core)
            remote(here, here, a_s.at[j * side + ka], a_r.at[j * side + ka], sibling).wait_recv()
            pass_on(here, here, j, ka, 0)
    for j in range(n):
        for ka in range(side):
            for kb in range(1, side):
                here = block(j, ka, kb, core)
                place = (j * side + ka) * side + kb
                remote(here, here, b_s.at[place], b_r.at[place], sibling).wait_recv()
                pass_on(here, here, j, ka, kb)
    at_last()
    for j in range(n):
        for ka in range(side):
            for kb in range(side):
                here = block(j, ka, kb, 1 - core)
                place = (j * side + ka) * side + kb
                remote(here, here, c_s.at[place], c_r.at[place], sibling).wait_recv()
    return sent


def spread_sems(n, side):
    dma = pltpu.SemaphoreType.DMA
    return [*[dma((n,))] * 2, *[dma((n * side,))] * 2, *[dma((n * side * side,))] * 4]


def exchange_all(pairs, sent):
    z, mine = lax.axis_index("dp"), lax.axis_index("expert")
    experts = lax.axis_size("expert")
    for k in range(1, experts):
        to = (mine + k) % experts
        for src, dst, send, recv in pairs:
            copy = remote(src(to), dst(mine), send.at[k], recv.at[k], (z, to))
            copy.start()
            sent.append(copy)


def wait_all(pairs):
    z, mine = lax.axis_index("dp"), lax.axis_index("expert")
    experts = lax.axis_size("expert")
    for k in range(1, experts):
        came = (mine - k + experts) % experts
        for _, dst, send, recv in pairs:
            remote(dst(came), dst(came), send.at[k], recv.at[k], (z, came)).wait_recv()


def gather_kernel(
    n, in_ref, own_ref, slots_ref, marks_ref, out_ref, second_ref, third_ref, slots_in, marks_in,
    local_sem, part_s, part_r, slot_s, slot_r, mark_s, mark_r, *sems,
):
    side, z, y, x, core = where_am_i()
    mine = lax.axis_index("expert")
    experts = slots_ref.shape[0]
    greet([*peers_of(n, side, z, y, x, core)[0], *[(z, (mine + k) % experts) for k in range(1, experts)]])
    me = ((z * side + y) * side + x) * 2 + core
    stays = [
        pltpu.make_async_copy(in_ref, out_ref.at[me], local_sem.at[0]),
        pltpu.make_async_copy(slots_ref.at[mine], slots_in.at[mine], local_sem.at[1]),
        pltpu.make_async_copy(marks_ref.at[mine], marks_in.at[mine], local_sem.at[2]),
    ]
    for copy in stays:
        copy.start()
    beside = remote(own_ref, second_ref, part_s.at[0], part_r.at[0], (z + 1 - 2 * (z % 2), mine))
    across = remote(own_ref, third_ref, part_s.at[1], part_r.at[1], ((n - 1 - z) % n, mine))
    inner = (z + 1) // 2 % 2 == 1
    pairs = [
        (lambda e: slots_ref.at[e], lambda e: slots_in.at[e], slot_s, slot_r),
        (lambda e: marks_ref.at[e], lambda e: marks_in.at[e], mark_s, mark_r),
    ]
    more = []

    def weights_on():
        beside.start()

        @pl.when(inner)
        def _():
            across.start()

    sent = spread_blocks(n, in_ref, lambda d: out_ref.at[d], sems, weights_on, lambda: exchange_all(pairs, more))
    wait_all(pairs)
    for copy in [*sent, *more]:
        copy.wait_send()
    for copy in stays:
        copy.wait()
    beside.wait()

    @pl.when(inner)
    def _():
        across.wait()


def gather_dense(packed, own, slots, marks, n, side):
    devices = n * side * side * 2
    experts = slots.shape[0]
    dma = pltpu.SemaphoreType.DMA
    sems = [dma((3,)), *[dma((2,))] * 2, *[dma((experts,))] * 4, *spread_sems(n, side)]
    vmem, hbm = pl.BlockSpec(memory_space=pltpu.VMEM), pl.BlockSpec(memory_space=pl.ANY)
    gathered = jax.ShapeDtypeStruct((devices, *packed.shape), packed.dtype)
    return pl.pallas_call(
        functools.partial(gather_kernel, n),
        out_shape=[gathered, *[jax.ShapeDtypeStruct(v.shape, v.dtype) for v in (own, own, slots, marks)]],
        in_specs=[vmem, hbm, hbm, hbm],
        out_specs=[vmem, *[hbm] * 4],
        scratch_shapes=sems,
        compiler_params=pltpu.CompilerParams(collective_id=0, has_side_effects=True, vmem_limit_bytes=60 << 20),
        cost_estimate=CHEAP,
        name="gather_dense",
    )(packed, own, slots, marks)


TILE = 512


def dot(a, b, contract):
    return lax.dot_general(a, b, (contract, ((), ())), preferred_element_type=f32)


NN = ((1,), (0,))
NT = ((1,), (1,))
TN = ((0,), (0,))


def expert_tile(x, dout, up, up_bias, down):
    pre = dot(x, up, NT) + up_bias
    grad_hidden = dot(dout, down, NT)
    square = pre * pre
    inner = jnp.tanh(pre * (GELU_C + GELU_C * GELU_K * square))
    half = 0.5 * pre
    hidden = (half + half * inner).astype(b16)
    slope = 0.5 + 0.5 * inner + half * (1.0 - inner * inner) * (GELU_C + 3.0 * GELU_C * GELU_K * square)
    grad_pre = (slope * grad_hidden).astype(b16)
    return hidden, grad_pre, dot(hidden, down, NN), dot(grad_pre, up, NN)


def bias_rows(first, second):
    row = lax.broadcasted_iota(jnp.int32, (BIAS_ROWS, D), 0)
    return jnp.where(row == 0, first, jnp.where(row == 1, second, 0.0))


def expert_kernel(sources, first, last, part, *refs):
    refs = list(refs)
    weights = [refs.pop(0) for _ in range(sources)]
    x_ref, dout_ref, bias_ref = refs[:3]
    refs = refs[3:]
    sums = [None, None] if first else [refs.pop(0), refs.pop(0)]
    out_ref, grad_x_ref, grad_up_ref, grad_down_ref, w_ref, up_acc, down_acc, bias_acc, sem = refs
    step = pl.program_id(0)

    @pl.when(step == 0)
    def _():
        if sources == 1:
            copy = pltpu.make_async_copy(weights[0], w_ref, sem)
            copy.start()
            copy.wait()
        else:
            me = lax.axis_index("dp")
            inner = (me + 1) // 2 % 2

            @pl.when(inner == 1)
            def _():
                pltpu.make_async_copy(weights[0], w_ref, sem).start()

            @pl.when(inner == 0)
            def _():
                pltpu.make_async_copy(weights[1], w_ref, sem).start()

            pltpu.make_async_copy(weights[0], w_ref, sem).wait()
        up_acc[...] = jnp.zeros_like(up_acc)
        down_acc[...] = jnp.zeros_like(down_acc)
        bias_acc[...] = jnp.zeros_like(bias_acc)

    x = x_ref[...]
    dout = dout_ref[...]
    up = w_ref[:part]
    down = w_ref[part : 2 * part]
    up_bias = w_ref[2 * part :][0:1, :part].astype(f32)
    hidden, grad_pre_b, out, grad_x = expert_tile(x, dout, up, up_bias, down)
    if not first:
        out = out + sums[0][...]
        grad_x = grad_x + sums[1][...]
    if last:
        out = out + bias_ref[1:2, :]
    out_ref[...] = out.astype(out_ref.dtype)
    grad_x_ref[...] = grad_x.astype(grad_x_ref.dtype)
    down_acc[...] += dot(hidden, dout, TN)
    up_acc[...] += dot(grad_pre_b, x, TN)
    bias_acc[0:1, :] += jnp.sum(grad_pre_b.astype(f32), axis=0, keepdims=True)

    @pl.when(step == pl.num_programs(0) - 1)
    def _():
        grad_up_ref[...] = up_acc[...].astype(grad_up_ref.dtype)
        grad_down_ref[:part] = down_acc[...].astype(grad_down_ref.dtype)
        tail = bias_rows(bias_acc[0:1, :], bias_ref[0:1, :])
        grad_down_ref[part:] = tail.astype(grad_down_ref.dtype)


def expert_part(weights, x, dout, biases, sums, last, grad_type, name):
    first = sums is None
    slots = x.shape[0]
    rows = weights[0].shape[0]
    part = (rows - BIAS_ROWS) // 2
    tile = pl.BlockSpec((TILE, D), lambda i: (i, 0))
    kept = b16 if last else f32
    n = len(weights)
    return pl.pallas_call(
        functools.partial(expert_kernel, n, first, last, part),
        grid=(slots // TILE,),
        in_specs=[
            *[pl.BlockSpec(memory_space=pl.ANY)] * n,
            tile,
            tile,
            pl.BlockSpec((2, D), lambda i: (0, 0)),
            *([] if first else [tile, tile]),
        ],
        out_specs=[
            tile,
            tile,
            pl.BlockSpec((part, D), lambda i: (0, 0)),
            pl.BlockSpec((part + BIAS_ROWS, D), lambda i: (0, 0)),
        ],
        out_shape=[
            jax.ShapeDtypeStruct((slots, D), kept),
            jax.ShapeDtypeStruct((slots, D), kept),
            jax.ShapeDtypeStruct((part, D), grad_type),
            jax.ShapeDtypeStruct((part + BIAS_ROWS, D), grad_type),
        ],
        scratch_shapes=[
            pltpu.VMEM((rows, D), b16),
            pltpu.VMEM((part, D), f32),
            pltpu.VMEM((part, D), f32),
            pltpu.VMEM((8, part), f32),
            pltpu.SemaphoreType.DMA,
        ],
        compiler_params=pltpu.CompilerParams(vmem_limit_bytes=56 << 20, dimension_semantics=("arbitrary",)),
        cost_estimate=pl.CostEstimate(flops=48 * slots * part * D, bytes_accessed=slots * D * 20, transcendentals=0),
        name=name,
    )(*weights, x, dout, biases, *([] if first else sums))


SCALE = HEAD_DIM ** (-0.5)
PAIRS = HEADS // 2
WIDE = 2 * HEAD_DIM
CHEAP = pl.CostEstimate(flops=0, bytes_accessed=1024, transcendentals=0)


def normal(values):
    center = values - jnp.mean(values, axis=-1, keepdims=True)
    rate = lax.rsqrt(jnp.mean(center * center, axis=-1, keepdims=True) + NORM_EPS)
    return center * rate, rate


def lanes_like(values):
    return lax.broadcasted_iota(jnp.int32, values.shape, values.ndim - 1)


def scores_of(part_q, pair_k, length):
    scores = dot(part_q, pair_k, NT) * SCALE
    return jnp.where(lanes_like(scores) < length, scores, NEG_FILL)


def halves(pair):
    low = lanes_like(pair) < HEAD_DIM
    zero = jnp.zeros_like(pair)
    return jnp.where(low, pair, zero), jnp.where(low, zero, pair)


def joined(even, odd):
    return jnp.where(lanes_like(even) < HEAD_DIM, even, odd)


def sequence_forward(
    s, lengths_ref, tokens_ref, weights_ref, vector_ref, router_ref, routes_ref, places_ref,
    normed_ref, q_ref, k_ref, v_ref, context_ref, lse_ref, resid_ref, normed_two_ref, gates_ref, slots_ref,
):
    at = pl.ds(s * LEN, LEN)
    length = lengths_ref[s]
    rows = tokens_ref[at, :].astype(f32)
    hat, _ = normal(rows)
    normed = (hat * vector_ref[0:1, :] + vector_ref[1:2, :]).astype(b16)
    normed_ref[at, :] = normed
    q_ref[at, :] = (dot(normed, weights_ref[0], NN) + vector_ref[2:3, :]).astype(b16)
    k_ref[at, :] = dot(normed, weights_ref[1], NN).astype(b16)
    v_ref[at, :] = (dot(normed, weights_ref[2], NN) + vector_ref[3:4, :]).astype(b16)
    lse = jnp.zeros((LEN, 128), f32)
    for pair in range(PAIRS):
        lanes = slice(pair * WIDE, (pair + 1) * WIDE)
        keys, values = k_ref[at, lanes], v_ref[at, lanes]
        mixed = []
        for half, part in enumerate(halves(q_ref[at, lanes])):
            scores = scores_of(part, keys, length)
            top = jnp.max(scores, axis=-1, keepdims=True)
            total = top + jnp.log(jnp.sum(jnp.exp(scores - top), axis=-1, keepdims=True))
            chance = jnp.exp(scores - total).astype(b16)
            mixed.append(dot(chance, values, NN))
            lse = jnp.where(lanes_like(lse) == 2 * pair + half, total, lse)
        context_ref[at, lanes] = joined(*mixed).astype(b16)
    lse_ref[at, :] = lse
    resid = rows + (dot(context_ref[at, :], weights_ref[3], NN) + vector_ref[4:5, :])
    resid_ref[at, :] = resid
    hat, _ = normal(resid)
    normed_two = (hat * vector_ref[5:6, :] + vector_ref[6:7, :]).astype(b16)
    normed_two_ref[at, :] = normed_two
    logits = dot(normed_two, router_ref[...], NT)
    names = lanes_like(logits)
    routes = routes_ref[at, :]
    first = jnp.sum(jnp.where(names == routes[:, 0:1], logits, 0.0), axis=-1, keepdims=True)
    second = jnp.sum(jnp.where(names == routes[:, 1:2], logits, 0.0), axis=-1, keepdims=True)
    gates_ref[at, :] = jnp.where(names == 0, jax.nn.sigmoid(first - second), jax.nn.sigmoid(second - first))
    experts, _, capacity, _ = slots_ref.shape
    slots = experts * capacity
    ids = lax.broadcasted_iota(jnp.int32, (slots, ROWS), 0)
    places = places_ref[s]
    chosen = jnp.where((ids == places[0:1, :]) | (ids == places[1:2, :]), 1.0, 0.0).astype(b16)
    sent = dot(chosen, normed_two, NN).astype(b16)
    slots_ref[:, s] = sent.reshape(experts, capacity, D)


def kept_shapes(count, experts, capacity):
    return [
        *[jax.ShapeDtypeStruct((count, D), b16)] * 5,
        jax.ShapeDtypeStruct((count, 128), f32),
        jax.ShapeDtypeStruct((count, D), f32),
        jax.ShapeDtypeStruct((count, D), b16),
        jax.ShapeDtypeStruct((count, 128), f32),
        jax.ShapeDtypeStruct((experts, count // ROWS, capacity, D), b16),
    ]


def attention_forward(lengths, tokens, weights, vector, router, routes, places, experts, capacity):
    count = tokens.shape[0]
    vmem = pl.BlockSpec(memory_space=pltpu.VMEM)

    def kernel(*refs):
        for s in range(count // LEN):
            sequence_forward(s, *refs)

    return pl.pallas_call(
        kernel,
        in_specs=[pl.BlockSpec(memory_space=pltpu.SMEM), *[vmem] * 6],
        out_specs=[vmem] * 10,
        out_shape=kept_shapes(count, experts, capacity),
        compiler_params=pltpu.CompilerParams(vmem_limit_bytes=48 << 20),
        cost_estimate=CHEAP,
        name="attention_forward",
    )(lengths, tokens, weights, vector, router, routes, places)


def norm_back(grad, hat, rate, gain):
    inner = grad * gain
    return rate * (
        inner
        - jnp.mean(inner, axis=-1, keepdims=True)
        - hat * jnp.mean(inner * hat, axis=-1, keepdims=True)
    )


def two_terms(values):
    high = values.astype(b16)
    return high, (values - high.astype(f32)).astype(b16)


def column_sum(values):
    return jnp.sum(values, axis=0, keepdims=True)


def sequence_backward(
    s, lengths_ref, tokens_ref, grad_ref, weights_ref, vector_ref, router_ref, routes_ref, places_ref,
    normed_ref, q_ref, k_ref, v_ref, context_ref, lse_ref, resid_ref, normed_two_ref, gates_ref, outs_ref, returned_ref,
    output_ref, input_grad_ref, weights_acc, vector_acc, router_acc, dq_ref, dk_ref, dv_ref,
):
    at = pl.ds(s * LEN, LEN)
    length = lengths_ref[s]
    experts, _, capacity, _ = outs_ref.shape
    slots = experts * capacity
    ids = lax.broadcasted_iota(jnp.int32, (ROWS, slots), 1)
    outs = outs_ref[:, s].reshape(slots, D)
    grad_out = grad_ref[at, :].astype(f32)
    places = places_ref[at, :]
    take = [jnp.where(ids == places[:, k : k + 1], 1.0, 0.0).astype(b16) for k in range(2)]
    out = [dot(t, outs, NN) for t in take]
    both_gates = gates_ref[at, :]
    gates = [both_gates[:, k : k + 1] for k in range(2)]
    resid = resid_ref[at, :]
    output_ref[at, :] = resid + gates[0] * out[0] + gates[1] * out[1]
    slopes = [
        jnp.sum(grad_out * out[k], axis=-1, keepdims=True) * (gates[k] * (1.0 - gates[k])) for k in range(2)
    ]
    pull = slopes[0] - slopes[1]
    names = lax.broadcasted_iota(jnp.int32, (ROWS, 128), 1)
    routes = routes_ref[at, :]
    grad_logits = jnp.where(names == routes[:, 0:1], pull, jnp.where(names == routes[:, 1:2], -pull, 0.0))
    high, low = two_terms(grad_logits)
    normed_two = normed_two_ref[at, :]
    router = router_ref[...]
    router_acc[...] += dot(high, normed_two, TN) + dot(low, normed_two, TN)
    returned = returned_ref[:, s].reshape(slots, D)
    grad_two = dot(take[0] + take[1], returned, NN) + (dot(high, router, NN) + dot(low, router, NN))
    hat, rate = normal(resid)
    vector_acc[5:6, :] += column_sum(grad_two * hat)
    vector_acc[6:7, :] += column_sum(grad_two)
    grad_resid = grad_out + norm_back(grad_two, hat, rate, vector_ref[5:6, :])
    input_grad_ref[at, :] = grad_resid
    branch = grad_resid.astype(b16)
    vector_acc[4:5, :] += column_sum(branch.astype(f32))
    weights_acc[3] += dot(context_ref[at, :], branch, TN)
    grad_context = dot(branch, weights_ref[3], NT).astype(b16)
    for pair in range(PAIRS):
        lanes = slice(pair * WIDE, (pair + 1) * WIDE)
        queries, keys, values = q_ref[at, lanes], k_ref[at, lanes], v_ref[at, lanes]
        given = grad_context[:, lanes]
        grads = []
        for half, (part, part_given) in enumerate(zip(halves(queries), halves(given))):
            head = 2 * pair + half
            chance = jnp.exp(scores_of(part, keys, length) - lse_ref[at, head : head + 1])
            grad_v = dot(chance.astype(b16), given, TN)
            grad_chance = dot(part_given, values, NT)
            mean = jnp.sum(chance * grad_chance, axis=-1, keepdims=True)
            grad_scores = (chance * (grad_chance - mean)).astype(b16)
            grads.append((dot(grad_scores, keys, NN), dot(grad_scores, queries, TN), grad_v))
        dq_ref[:, lanes] = (joined(grads[0][0], grads[1][0]) * SCALE).astype(b16)
        dk_ref[:, lanes] = (joined(grads[0][1], grads[1][1]) * SCALE).astype(b16)
        dv_ref[:, lanes] = joined(grads[0][2], grads[1][2]).astype(b16)
    normed = normed_ref[at, :]
    grad_one = jnp.zeros((LEN, D), f32)
    for k, ref in enumerate((dq_ref, dk_ref, dv_ref)):
        weights_acc[k] += dot(normed, ref[...], TN)
        grad_one += dot(ref[...], weights_ref[k], NT)
    vector_acc[2:3, :] += column_sum(dq_ref[...].astype(f32))
    vector_acc[3:4, :] += column_sum(dv_ref[...].astype(f32))
    hat, rate = normal(tokens_ref[at, :].astype(f32))
    vector_acc[0:1, :] += column_sum(grad_one * hat)
    vector_acc[1:2, :] += column_sum(grad_one)
    input_grad_ref[at, :] += norm_back(grad_one, hat, rate, vector_ref[0:1, :])


def begin_kernel(
    n, cols, seqs, part, lengths_ref, in_ref, own_ref, slots_ref, marks_ref, tokens_ref, routes_ref, places_ref,
    *refs,
):
    kept_out, refs = refs[:12], refs[12:]
    here, refs = refs[-12:], refs[:-12]
    weights_ref, vector_ref, router_ref, *attention_refs = here
    (
        out_ref, back_ref, mine_up, mine_down, near_up, near_down, middle_up, middle_down, far_up, far_down,
    near_up_in, near_down_in, middle_in,
    pool, acc, second_ref, third_ref, fourth_ref, going, x_in, dout_in, marks_in, out_acc, back_acc, bias_acc, tail_ref,
    local_sem, part_s, part_r, slot_s, slot_r, mark_s, mark_r, x_s, x_r, near_s, near_r, store_s, *sems,
    ) = refs
    side, z, y, x, core = where_am_i()
    mine = lax.axis_index("expert")
    experts, _, capacity, _ = slots_ref.shape
    slots = experts * seqs * capacity
    greet([*peers_of(n, side, z, y, x, core)[0], *[(z, (mine + k) % experts) for k in range(1, experts)]])
    me = ((z * side + y) * side + x) * 2 + core
    block_rows = in_ref.shape[0]
    stage_rows = 2 * part + BIAS_ROWS

    def block_at(device):
        return pool.at[pl.ds(pl.multiple_of(device * block_rows, 16), block_rows), :]

    def sender(ref, e, b=0, blocks=seqs):
        return ref.at[pl.ds(pl.multiple_of((e * seqs + b) * capacity, 16), blocks * capacity), :]

    flat_slots = slots_ref.reshape(slots, D)
    flat_marks = marks_ref.reshape(slots, 128)
    stays = [
        pltpu.make_async_copy(in_ref, block_at(me), local_sem.at[0]),
        pltpu.make_async_copy(sender(flat_slots, mine), sender(dout_in, mine), local_sem.at[1]),
        pltpu.make_async_copy(sender(flat_marks, mine), sender(marks_in, mine), local_sem.at[2]),
    ]
    for copy in stays:
        copy.start()
    inner = (z + 1) // 2 % 2 == 1
    outer = jnp.logical_not(inner)
    inward, across, outward = (1 + z // 2, mine), (3 - z, mine), (3 * (z // 2), mine)

    def hop(k, src, dst, peer):
        return remote(src, dst, part_s.at[k], part_r.at[k], peer)

    beside = hop(0, own_ref, second_ref, (z + 1 - 2 * (z % 2), mine))
    own_across = hop(1, own_ref, third_ref, across)
    third_on = hop(2, third_ref, third_ref, outward)
    second_across = hop(3, second_ref, fourth_ref, across)
    cut = part // 3 * 2
    spans = [(0, cut), (part, cut), (2 * part, BIAS_ROWS), (cut, part - cut), (part + cut, part - cut)]
    fourth_on = [
        hop(4 + i, fourth_ref.at[pl.ds(at, length), :], fourth_ref.at[pl.ds(at, length), :], outward)
        for i, (at, length) in enumerate(spans)
    ]

    def weights_on():
        beside.start()

        @pl.when(inner)
        def _():
            own_across.start()

    early = [
        (lambda e: sender(flat_slots, e), lambda e: sender(dout_in, e), slot_s, slot_r),
        (lambda e: sender(flat_marks, e), lambda e: sender(marks_in, e), mark_s, mark_r),
    ]
    more = []
    sent = spread_blocks(n, in_ref, block_at, sems, weights_on, lambda: exchange_all(early, more))
    stays[0].wait()

    for pair in range(2):
        def spread(device, carry):
            rows = block_at(device)[2 * pair * cols : 2 * (pair + 1) * cols, :].astype(f32)
            place = pl.ds(pl.multiple_of(device * cols, 8), cols)
            acc[0, place, :] = rows[:cols]
            acc[1, place, :] = rows[cols:]
            return carry

        lax.fori_loop(0, n * experts, spread, 0)
        weights_ref[2 * pair] = acc[0].astype(b16)
        weights_ref[2 * pair + 1] = acc[1].astype(b16)

    def gather_small(device, total):
        return total + block_at(device)[4 * cols :, :].astype(f32)

    small = lax.fori_loop(0, n * experts, gather_small, jnp.zeros((block_rows - 4 * cols, D), f32))
    vector_ref[...] = small[:8]
    router_ref[...] = jnp.zeros_like(router_ref)
    router_ref[: block_rows - 4 * cols - 8, :] = small[8:].astype(b16)

    late = []
    for s in range(seqs):
        sequence_forward(
            s, lengths_ref, tokens_ref, weights_ref, vector_ref, router_ref, routes_ref, places_ref, *attention_refs, going
        )
        dst = functools.partial(sender, x_in, b=s, blocks=1)
        late.append((functools.partial(lambda e, s: going.at[e, s], s=s), dst, x_s.at[s], x_r.at[s]))
        exchange_all(late[-1:], more)
        stays.append(pltpu.make_async_copy(going.at[mine, s], dst(mine), local_sem.at[3 + s]))
        stays[-1].start()
    stores = [pltpu.make_async_copy(src, dst, store_s.at[11 + k]) for k, (src, dst) in enumerate(zip(here, kept_out))]
    for copy in stores:
        copy.start()
    beside.wait()

    @pl.when(inner)
    def _():
        second_across.start()
        own_across.wait()
        third_on.start()

    wait_all(early)
    wait_all(late)
    for copy in [*sent, *more]:
        copy.wait_send()
    for copy in stays[1:]:
        copy.wait()

    up_acc, down_acc = acc.at[0], acc.at[1]
    tiles = slots // TILE
    down_bias = jnp.zeros((1, D), f32)
    outs = [(mine_up, mine_down), (near_up, near_down), (middle_up, middle_down), (far_up, far_down)]
    near_in = (near_up_in, near_down_in)
    bias_acc[...] = jnp.zeros_like(bias_acc)
    pieces = [(1, 0, part), (0, 0, part), (2, 0, part), (3, 0, cut), (3, cut, part)]
    for p, low, high in pieces:
        begins = p == 1
        w_ref = (own_ref, second_ref, third_ref, fourth_ref)[p]
        last = p == 3 and high == part
        if p == 0:

            @pl.when(inner)
            def _():
                second_across.wait()
                for copy in fourth_on:
                    copy.start()

        if p == 2:

            @pl.when(outer)
            def _():
                third_on.wait_recv()

        if p == 3:

            @pl.when(outer)
            def _():
                for copy in fourth_on[3:] if low else fourth_on[:3]:
                    copy.wait_recv()

        if low == 0:
            up_acc[...] = jnp.zeros_like(up_acc)
            down_acc[...] = jnp.zeros_like(down_acc)
            bias_acc[0:1, :] = jnp.zeros((1, D), f32)

        biases = w_ref[2 * part :, :].astype(f32)
        up_bias = biases[0:1, low:high]
        if low == 0:
            down_bias = down_bias + biases[1:2, :]

        def tile(t, carry):
            rows = pl.ds(pl.multiple_of(t * TILE, TILE), TILE)
            x = x_in[rows, :]
            if begins:
                logits = dot(x, router_ref[...], NT)
                signs = jnp.where(lanes_like(logits) == mine, 1.0, -marks_in[rows, :].astype(f32))
                margin = jnp.sum(logits * signs, axis=-1, keepdims=True)
                dout = (jax.nn.sigmoid(margin) * dout_in[rows, :].astype(f32)).astype(b16)
                dout_in[rows, :] = dout
                bias_acc[1:2, :] += column_sum(dout.astype(f32))
            else:
                dout = dout_in[rows, :]
            hidden, grad_pre, out, back = expert_tile(
                x, dout, w_ref[low:high, :], up_bias, w_ref[part + low : part + high, :]
            )
            down_acc[low:high, :] += dot(hidden, dout, TN)
            up_acc[low:high, :] += dot(grad_pre, x, TN)
            bias_acc[0:1, low:high] += column_sum(grad_pre.astype(f32))
            if begins:
                out_acc[rows, :] = out
                back_acc[rows, :] = back
            elif not last:
                out_acc[rows, :] += out
                back_acc[rows, :] += back
            else:
                x_in[rows, :] = (out_acc[rows, :] + out + down_bias).astype(b16)
                dout_in[rows, :] = (back_acc[rows, :] + back).astype(b16)
            return carry

        lax.fori_loop(0, tiles, tile, 0)
        if high < part:
            continue
        tail = bias_rows(bias_acc[0:1, :], bias_acc[1:2, :])
        base = stage_rows if p == 2 else 0
        if p == 0:
            tail_ref[...] = tail
            now = [
                pltpu.make_async_copy(up_acc, mine_up, store_s.at[0]),
                pltpu.make_async_copy(down_acc, mine_down.at[pl.ds(0, part), :], store_s.at[1]),
                pltpu.make_async_copy(tail_ref, mine_down.at[pl.ds(part, BIAS_ROWS), :], store_s.at[2]),
            ]
            for copy in now:
                copy.start()
            for copy in now:
                copy.wait()
        else:
            if p == 3:
                for copy in stores[12:14]:
                    copy.wait()
                del stores[12:14]

                @pl.when(outer)
                def _():
                    for copy in nears[:2]:
                        copy.wait_send()

            pool[base : base + part, :] = up_acc[...].astype(b16)
            pool[base + part : base + 2 * part, :] = down_acc[...].astype(b16)
            pool[base + 2 * part : base + stage_rows, :] = tail.astype(b16)
            halves_of = [pool.at[pl.ds(base, part), :], pool.at[pl.ds(base + part, part + BIAS_ROWS), :]]
            for h in range(2):
                stores.append(pltpu.make_async_copy(halves_of[h], outs[p][h], store_s.at[1 + 2 * p + h]))
                stores[-1].start()
            if p == 1:
                nears = [remote(halves_of[h], near_in[h], near_s.at[h], near_r.at[h], inward) for h in range(2)]

                @pl.when(outer)
                def _():
                    for copy in nears:
                        copy.start()

            if p == 2:
                middle = remote(halves_of[0], middle_in, near_s.at[2], near_r.at[2], inward)
                nears.append(middle)

                @pl.when(outer)
                def _():
                    middle.start()

    for src, dst, k in ((x_in, out_ref, 9), (dout_in, back_ref, 10)):
        stores.append(pltpu.make_async_copy(src, dst, store_s.at[k]))
        stores[-1].start()
    for copy in stores:
        copy.wait()

    @pl.when(inner)
    def _():
        for copy in [third_on, *fourth_on]:
            copy.wait_send()
        for copy in nears:
            copy.wait_recv()

    @pl.when(outer)
    def _():
        nears[2].wait_send()


def begin(n, side, cols, lengths, packed, own, slots, marks, tokens, routes, places):
    devices = n * side * side * 2
    experts, blocks, capacity, _ = slots.shape
    count = tokens.shape[0]
    total = experts * blocks * capacity
    part = (own.shape[0] - BIAS_ROWS) // 2
    dma = pltpu.SemaphoreType.DMA
    vmem, hbm = pl.BlockSpec(memory_space=pltpu.VMEM), pl.BlockSpec(memory_space=pl.ANY)
    *kept, going = kept_shapes(count, experts, capacity)
    held = [
        jax.ShapeDtypeStruct((4, D, D), b16),
        jax.ShapeDtypeStruct((8, D), f32),
        jax.ShapeDtypeStruct((128, D), b16),
        *kept,
    ]

    def halves_in(dtype):
        return [jax.ShapeDtypeStruct((part, D), dtype), jax.ShapeDtypeStruct((part + BIAS_ROWS, D), dtype)]

    return pl.pallas_call(
        functools.partial(begin_kernel, n, cols, blocks, part),
        out_shape=[
            *held,
            *[jax.ShapeDtypeStruct((total, D), b16)] * 2,
            *halves_in(f32),
            *halves_in(b16) * 4,
            halves_in(b16)[0],
        ],
        in_specs=[pl.BlockSpec(memory_space=pltpu.SMEM), vmem, vmem, hbm, hbm, vmem, vmem, vmem],
        out_specs=[hbm] * 25,
        scratch_shapes=[
            pltpu.VMEM((max(devices * packed.shape[0], 2 * own.shape[0]), D), b16),
            pltpu.VMEM((2, D, D), f32),
            *[pltpu.VMEM(own.shape, b16)] * 3,
            pltpu.VMEM(going.shape, b16),
            *[pltpu.VMEM((total, D), b16)] * 2,
            pltpu.VMEM((total, 128), b16),
            *[pltpu.VMEM((total, D), f32)] * 2,
            pltpu.VMEM((8, D), f32),
            pltpu.VMEM((BIAS_ROWS, D), f32),
            dma((3 + blocks,)),
            *[dma((9,))] * 2,
            *[dma((experts,))] * 4,
            *[dma((blocks, experts))] * 2,
            *[dma((3,))] * 2,
            dma((23,)),
            *spread_sems(n, side),
            *[pltpu.VMEM(v.shape, v.dtype) for v in held],
        ],
        compiler_params=pltpu.CompilerParams(collective_id=0, has_side_effects=True, vmem_limit_bytes=63 << 20),
        cost_estimate=CHEAP,
        name="begin",
    )(lengths, packed, own, slots, marks, tokens, routes, places)


KINDS = 5
FAR, MIDDLE, FAR_ON, MIDDLE_ON, FAR_LAST = range(KINDS)


def finish_kernel(
    n, cols, extra, seqs, lengths_ref, vector_ref, router_ref, routes_ref, places_ref, *refs,
):
    brought, refs = refs[:12], refs[12:]
    here, refs = refs[-12:], refs[:-12]
    tokens_ref, grad_ref, weights_ref, *attention_refs = here
    (
        outs_ref, backs_ref,
        near_up, near_down, middle_up, middle_down, far_up, far_down, middle_came,
        output_ref, input_grad_ref, dense_ref, middle_up_in, middle_down_in, end_up_in, end_down_in,
        outs_in, backs_in, weights_acc, vector_acc, router_acc, dq_ref, dk_ref, dv_ref,
        far_up_buf, far_down_buf, middle_up_buf, middle_down_buf, on_up_buf, on_down_buf, load_up, load_down,
        parts, stage, c_buf, b_buf, a_buf, z_buf,
        own_s, out_s, out_r, back_s, back_r, chain_s, chain_r, load_s, came_s, c_s, c_r, b_s, b_r, a_s, a_r, z_s, z_r,
    ) = refs
    inside = cols % 8 == 0
    side, z, y, x, core = where_am_i()
    mine = lax.axis_index("expert")
    experts = outs_in.shape[0]
    along_z, first, second, sibling = peers_of(n, side, z, y, x, core)
    plane = [(z, (mine + k) % experts) for k in range(1, experts)]
    greet([*along_z, *plane])
    area = side * side if inside else 0
    sent = []

    def send(src, dst, send_sem, recv_sem, peer):
        copy = remote(src, dst, send_sem, recv_sem, peer)
        copy.start()
        sent.append(copy)

    def by_sequence(s):
        return [
            (lambda e: outs_ref.at[e, s], lambda e: outs_in.at[e, s], out_s.at[s], out_r.at[s]),
            (lambda e: backs_ref.at[e, s], lambda e: backs_in.at[e, s], back_s.at[s], back_r.at[s]),
        ]

    for s in range(seqs):
        exchange_all(by_sequence(s), sent)
    own = [
        pltpu.make_async_copy(outs_ref.at[mine], outs_in.at[mine], own_s.at[0]),
        pltpu.make_async_copy(backs_ref.at[mine], backs_in.at[mine], own_s.at[1]),
    ]
    own += [pltpu.make_async_copy(src, dst, own_s.at[2 + k]) for k, (src, dst) in enumerate(zip(brought, here))]
    for copy in own:
        copy.start()

    inner = (z + 1) // 2 % 2 == 1
    outer = jnp.logical_not(inner)
    inward = (z - z + 1 + z // 2, mine)
    across = (3 - z, mine)
    outward = (3 * (z // 2), mine)
    near, middle, far = (near_up, near_down), (middle_up, middle_down), (far_up, far_down)
    middle_in = (middle_up_in, middle_down_in)
    end_in = (end_up_in, end_down_in)
    far_buf, middle_buf, on_buf = (far_up_buf, far_down_buf), (middle_up_buf, middle_down_buf), (on_up_buf, on_down_buf)
    loads = (load_up, load_down)

    whole = [(h, 0, far[h].shape[0]) for h in range(2)]
    split = far[0].shape[0] // 32 * 16
    quarters = [(h, at, split if at == 0 else far[h].shape[0] - split) for h in range(2) for at in (0, split)]

    def hop(kind, k, piece, src, dst, peer):
        h, at, length = piece
        rows = pl.ds(at, length)
        return remote(src[h].at[rows, :], dst[h].at[rows, :], chain_s.at[kind, k], chain_r.at[kind, k], peer)

    from_ends = [(FAR, whole, far, far_buf), (MIDDLE, quarters, middle, middle_buf)]

    @pl.when(outer)
    def _():
        for kind, cuts, src, dst in from_ends:
            for k, piece_ in enumerate(cuts):
                if kind == FAR or piece_[0]:
                    hop(kind, k, piece_, src, dst, inward).start()

    def chain_step(kind, k, piece_, buf, term, next_kind, target, peer):
        @pl.when(inner)
        def _():
            h, at, length = piece_
            rows = pl.ds(at, length)
            load = pltpu.make_async_copy(term[h].at[rows, :], loads[h].at[rows, :], load_s)
            load.start()
            if kind == MIDDLE and h == 0:
                came = pltpu.make_async_copy(middle_came.at[rows, :], buf[h].at[rows, :], came_s)
                came.start()
                came.wait()
            else:
                hop(kind, k, piece_, buf, buf, across).wait_recv()
            load.wait()
            buf[h][rows, :] = (buf[h][rows, :].astype(f32) + loads[h][rows, :].astype(f32)).astype(b16)
            hop(next_kind, k, piece_, buf, target, peer).start()

    def step_far(k):
        chain_step(FAR, k, whole[k], far_buf, far, FAR_ON, on_buf, across)

    def step_on(k):
        chain_step(FAR_ON, k, whole[k], on_buf, near, FAR_LAST, end_in, outward)

    def step_middle(k):
        chain_step(MIDDLE, k, quarters[k], middle_buf, middle, MIDDLE_ON, middle_in, across)

    weights_acc[...] = jnp.zeros_like(weights_acc)
    vector_acc[...] = jnp.zeros_like(vector_acc)
    router_acc[...] = jnp.zeros_like(router_acc)
    step_middle(0)
    step_middle(1)
    step_far(0)
    for copy in own:
        copy.wait()
    for s in range(seqs):
        wait_all(by_sequence(s))
        sequence_backward(
            s, lengths_ref, tokens_ref, grad_ref, weights_ref, vector_ref, router_ref, routes_ref, places_ref,
            *attention_refs, outs_in, backs_in,
            output_ref, input_grad_ref, weights_acc, vector_acc, router_acc, dq_ref, dk_ref, dv_ref,
        )
        if s == 0:
            step_far(1)
            step_on(0)
    step_on(1)

    small = jnp.concatenate([vector_acc[...], router_acc[: extra - 8, :]], axis=0).astype(b16)
    if not inside:
        dense_ref[:extra, :] = jnp.concatenate([vector_acc[...], router_acc[: extra - 8, :]], axis=0)
        for k in range(4):
            dense_ref[extra + k * D : extra + (k + 1) * D, :] = weights_acc[k]
        step_middle(2)
        step_middle(3)
    for core_ in range(2 if inside else 0):
        for y_ in range(side):
            for x_ in range(side):
                for z_ in range(n):
                    owner = ((z_ * side + y_) * side + x_) * 2 + core_
                    rows = [weights_acc[k, owner * cols : (owner + 1) * cols, :] for k in range(4)]
                    place = parts.at[(core_ * side + y_) * side + x_, z_]
                    place[: 4 * cols, :] = jnp.concatenate(rows, axis=0).astype(b16)
                    place[4 * cols :, :] = small

    def piece(ka, kb, core_):
        y_ = (y + core * ka + (1 - core) * kb) % side
        x_ = (x + (1 - core) * ka + core * kb) % side
        return (core_ * side + y_) * side + x_

    order = [(ka, kb) for kb in [*range(1, side), 0] for ka in [*range(1, side), 0]][:area]
    for ka, kb in order:
        place = ka * side + kb
        send(parts.at[piece(kb, ka, 1 - core)], c_buf.at[place], c_s.at[place], c_r.at[place], sibling)
    for ka, kb in order:
        place = ka * side + kb
        remote(c_buf.at[place], c_buf.at[place], c_s.at[place], c_r.at[place], sibling).wait_recv()
        mine_ = piece(ka, kb, core)
        if kb:
            stage[place] = (parts[mine_].astype(f32) + c_buf[place].astype(f32)).astype(b16)
            send(stage.at[place], b_buf.at[place], b_s.at[place], b_r.at[place], second[kb - 1])
        else:
            total = parts[mine_].astype(f32) + c_buf[place].astype(f32)
            if ka:
                step_middle(2)
            for k in range(1, side):
                slot = ka * side + k
                remote(b_buf.at[slot], b_buf.at[slot], b_s.at[slot], b_r.at[slot], sibling).wait_recv()
                total = total + b_buf[slot].astype(f32)
            if ka:
                stage[place] = total.astype(b16)
                send(stage.at[place], a_buf.at[ka], a_s.at[ka], a_r.at[ka], first[ka - 1])
            else:
                step_middle(3)
                for k in range(1, side):
                    remote(a_buf.at[k], a_buf.at[k], a_s.at[k], a_r.at[k], sibling).wait_recv()
                    total = total + a_buf[k].astype(f32)
                stage[place] = total.astype(b16)
    if inside:
        for k in range(1, n):
            send(stage.at[0, (z + k) % n], z_buf.at[k], z_s.at[k], z_r.at[k], along_z[k - 1])
        result = stage[0, z].astype(f32)
        for k in range(1, n):
            remote(z_buf.at[k], z_buf.at[k], z_s.at[k], z_r.at[k], sibling).wait_recv()
            result = result + z_buf[k].astype(f32)
        dense_ref[...] = result
    for copy in sent:
        copy.wait_send()

    @pl.when(outer)
    def _():
        for kind, cuts, src, dst in from_ends:
            for k, piece_ in enumerate(cuts):
                if kind == FAR or piece_[0]:
                    hop(kind, k, piece_, src, dst, inward).wait_send()
        for k, piece_ in enumerate(whole):
            hop(FAR_LAST, k, piece_, end_in, end_in, inward).wait_recv()

    @pl.when(inner)
    def _():
        for k, piece_ in enumerate(whole):
            hop(FAR_ON, k, piece_, far_buf, on_buf, across).wait_send()
            hop(FAR_LAST, k, piece_, on_buf, end_in, outward).wait_send()
        for k, piece_ in enumerate(quarters):
            hop(MIDDLE_ON, k, piece_, middle_buf, middle_in, across).wait()


def finish(n, side, cols, extra, lengths, small, rows_in, kept, outs, backs, grads):
    count = rows_in[0].shape[0]
    held = (*rows_in, *kept)
    slots = outs.shape
    vmem = pl.BlockSpec(memory_space=pltpu.VMEM)
    hbm = pl.BlockSpec(memory_space=pl.ANY)
    shapes = [jax.ShapeDtypeStruct(g.shape, b16) for g in grads[:2]]
    inside = cols % 8 == 0
    rows = 4 * cols + extra if inside else 4 * D + extra
    block = (n, rows, D) if inside else (1, 16, 128)
    dma = pltpu.SemaphoreType.DMA
    half = [pltpu.VMEM(g.shape, b16) for g in grads[:2]]
    area = side * side
    return pl.pallas_call(
        functools.partial(finish_kernel, n, cols, extra, count // LEN),
        in_specs=[
            pl.BlockSpec(memory_space=pltpu.SMEM),
            *[vmem] * len(small),
            *[hbm] * (len(held) + 2 + len(grads)),
        ],
        out_specs=[vmem, vmem, vmem, *[hbm] * 4],
        out_shape=[
            jax.ShapeDtypeStruct((count, D), f32),
            jax.ShapeDtypeStruct((count, D), f32),
            jax.ShapeDtypeStruct((rows, D), f32),
            *shapes * 2,
        ],
        scratch_shapes=[
            pltpu.VMEM(slots, b16),
            pltpu.VMEM(slots, b16),
            pltpu.VMEM((4, D, D), f32),
            pltpu.VMEM((8, D), f32),
            pltpu.VMEM((128, D), f32),
            *[pltpu.VMEM((LEN, D), b16)] * 3,
            *half * 4,
            pltpu.VMEM((2 * area, *block), b16),
            pltpu.VMEM((area, *block), b16),
            pltpu.VMEM((area, *block), b16),
            pltpu.VMEM((area, *block), b16),
            pltpu.VMEM((side, *block), b16),
            pltpu.VMEM(block, b16),
            dma((2 + len(held),)),
            *[dma((slots[1], slots[0]))] * 4,
            *[dma((KINDS, 4))] * 2,
            dma,
            dma,
            *[dma((area,))] * 4,
            *[dma((side,))] * 2,
            *[dma((n,))] * 2,
            *[pltpu.VMEM(v.shape, v.dtype) for v in held],
        ],
        compiler_params=pltpu.CompilerParams(collective_id=1, has_side_effects=True, vmem_limit_bytes=63 << 20),
        cost_estimate=CHEAP,
        name="finish",
    )(lengths, *small, *held, outs, backs, *grads)


def pack_expert(up, down, up_bias, down_bias, start, dtype):
    part = up.shape[0]
    tail = jnp.zeros((BIAS_ROWS, D), dtype)
    tail = tail.at[0, :part].set(up_bias.astype(dtype))
    tail = lax.dynamic_update_slice(tail, down_bias.astype(dtype)[None], (1, start))
    return jnp.concatenate([up.astype(dtype), down.astype(dtype), tail], axis=0)


def along(x, *pairs):
    return lax.ppermute(x, "dp", pairs)


def body(
    tokens, out_grad, routes, lengths,
    attention, gain_bias, router, expert_up, up_bias, expert_down, down_bias,
    first_attention, first_gain_bias, first_router, first_expert_up, first_up_bias, first_expert_down, first_down_bias,
    square_attention, square_gain_bias, square_router, square_expert_up, square_up_bias, square_expert_down, square_down_bias,
):
    experts = router.shape[0]
    capacity = 4 * ROWS // experts
    count = tokens.shape[0]
    blocks = count // ROWS
    part = expert_up.shape[1]
    narrow = down_bias.shape[1]
    cols = attention.shape[1]
    devices = D // cols
    n_dp = lax.axis_size("dp")
    assert n_dp == 4 and expert_up.shape[0] == 1
    me = lax.axis_index("dp")
    mine = lax.axis_index("expert")
    both = ("dp", "expert")

    side = math.isqrt(experts // 2)
    inside = cols if cols % 8 == 0 else 0
    small_rows = -(-(8 + experts) // 16) * 16
    flat_len = (7 + experts) * cols
    if inside:
        small = jnp.zeros((small_rows, D), b16)
        column = (me * experts + mine) * cols
        small = lax.dynamic_update_slice(small, gain_bias.astype(b16), (0, column))
        small = lax.dynamic_update_slice(small, router.astype(b16), (8, column))
    else:
        extra = -(-(4 * cols + -(-flat_len // D)) // 16) * 16 - 4 * cols
        small = jnp.concatenate([gain_bias, router], axis=0).astype(b16).reshape(-1)
        small = jnp.pad(small, (0, extra * D - flat_len)).reshape(extra, D)
    packed = jnp.concatenate([attention.astype(b16).reshape(4 * cols, D), small], axis=0)
    own = pack_expert(expert_up[0], expert_down[0], up_bias[0], down_bias[0], me * narrow, b16)

    positions = slots_of(routes, experts, capacity)
    slot_ids = jnp.arange(experts * capacity, dtype=jnp.int32)
    hit = positions[:, :, :, None] == slot_ids
    split = jnp.any(hit, axis=2).astype(b16).reshape(blocks, ROWS, experts, capacity)
    marked = jnp.any(routes[:, :, None] == jnp.arange(128, dtype=jnp.int32), axis=1).astype(b16)

    def by_slot(rows):
        sent = jnp.einsum("btec,btd->ebcd", split, rows.reshape(blocks, ROWS, -1), preferred_element_type=f32)
        return sent.astype(b16)

    places = positions.transpose(0, 2, 1)
    inner = (me == 1) | (me == 2)
    if inside:
        weights_b, vector_all, router_all, *got = begin(
            n_dp, side, cols, lengths, packed, own, by_slot(out_grad), by_slot(marked), tokens, routes, places
        )
        kept, out_b, back_b, grads, near_in, middle_in = got[:9], got[9], got[10], got[11:19], got[19:21], got[21]
    else:
        whole, second, third_inner, grad_slots, marks = gather_dense(
            packed, own, by_slot(out_grad), by_slot(marked), n_dp, side
        )
        weights_b = whole[:, : 4 * cols].reshape(devices, 4, cols, D).transpose(1, 0, 2, 3).reshape(4, D, D)
        small = whole[:, 4 * cols :].reshape(devices, extra * D)[:, :flat_len].reshape(devices, 7 + experts, cols)
        small = small.transpose(1, 0, 2).reshape(7 + experts, D)
        vector_all = jnp.pad(small[:7].astype(f32), ((0, 1), (0, 0)))
        router_all = jnp.pad(small[7:], ((0, 128 - experts), (0, 0)))
        *kept, slots_out = attention_forward(
            lengths, tokens, weights_b, vector_all, router_all, routes, places, experts, capacity
        )
        slots_in = lax.all_to_all(slots_out, "expert", split_axis=0, concat_axis=0, tiled=True)
        slots_in = slots_in.reshape(experts * blocks * capacity, D)
        grad_slots = grad_slots.reshape(experts * blocks * capacity, D)
        marks = marks.reshape(experts * blocks * capacity, 128)
        third_outer = along(third_inner, (1, 0), (2, 3))
        fourth_inner = along(second, (1, 2), (2, 1))
        fourth_outer = along(fourth_inner, (1, 0), (2, 3))
        slot_logits = jnp.einsum("sd,ed->se", slots_in, router_all, preferred_element_type=f32)
        this = jnp.arange(128, dtype=jnp.int32) == mine
        margin = jnp.sum(slot_logits * jnp.where(this, 1.0, -marks.astype(f32)), axis=-1)
        dout = (jax.nn.sigmoid(margin)[:, None] * grad_slots.astype(f32)).astype(b16)
        grad_down_bias = jnp.sum(dout.astype(f32), axis=0)
        row = 2 * part + 1
        down_bias_full = own[row].astype(f32) + second[row].astype(f32)
        down_bias_full += jnp.where(inner, third_inner[row], third_outer[row]).astype(f32)
        down_bias_full += jnp.where(inner, fourth_inner[row], fourth_outer[row]).astype(f32)
        biases = jnp.stack([grad_down_bias, down_bias_full])
        weights = [(own,), (second,), (third_inner, third_outer), (fourth_inner, fourth_outer)]
        sums = None
        grads = []
        for i in range(4):
            *sums, grad_up, grad_down = expert_part(
                weights[i], slots_in, dout, biases, sums, i == 3, b16 if i else f32, f"expert_part_{i}"
            )
            grads += [grad_up, grad_down]
        out_b, back_b = sums
        near_in = [along(g, (0, 1), (3, 2)) for g in grads[2:4]]
        middle_in = along(grads[4], (0, 1), (3, 2))

    slots_shape = (experts, blocks, capacity, D)
    output, input_grad, dense, *came = finish(
        n_dp, side, cols, small_rows, lengths,
        (vector_all, router_all, routes, positions.reshape(count, 2)), (tokens, out_grad, weights_b),
        kept, out_b.reshape(slots_shape), back_b.reshape(slots_shape), [*grads[2:], middle_in],
    )
    totals = [
        grads[i]
        + jnp.where(inner, near_in[i].astype(f32) + came[i].astype(f32), came[2 + i].astype(f32))
        for i in range(2)
    ]
    shard_up = totals[0][None]
    shard_down = totals[1][:part][None]
    shard_up_bias = totals[1][part, :part][None]
    shard_down_bias = lax.dynamic_slice(totals[1], (part + 1, me * narrow), (1, narrow))
    if cols % 8:
        small = lax.psum(dense[:small_rows], both)
        big = dense[small_rows:].reshape(4, D, D).astype(b16)
        big = lax.psum_scatter(big, both, scatter_dimension=1, tiled=True).astype(f32)
        dense = jnp.concatenate([big.reshape(4 * cols, D), small], axis=0)
    shard_weights = dense[: 4 * cols].reshape(4, cols, D)
    small = lax.dynamic_slice(
        dense[4 * cols :], (0, (me * experts + mine) * cols), (small_rows, cols)
    )
    shard_vector, shard_router = small[:7], small[8 : 8 + experts]

    params = (attention, gain_bias, router, expert_up, up_bias, expert_down, down_bias)
    grads = (shard_weights, shard_vector, shard_router, shard_up, shard_up_bias, shard_down, shard_down_bias)
    firsts = (first_attention, first_gain_bias, first_router, first_expert_up, first_up_bias, first_expert_down, first_down_bias)
    squares = (square_attention, square_gain_bias, square_router, square_expert_up, square_up_bias, square_expert_down, square_down_bias)
    hidden_units = n_dp * part
    rates = (1.6 * D ** (-0.5), 0.3, 0.5 * D ** (-0.5), 1.5 * D ** (-0.5), 0.25, 0.5 * hidden_units ** (-0.5), 0.25)
    updated = [adam_step(params[i], grads[i], firsts[i], squares[i], rates[i]) for i in range(7)]
    return (output, input_grad, *grads, *(u[0] for u in updated), *(u[1] for u in updated), *(u[2] for u in updated))


def solution(mesh):
    rows = P(("dp", "expert"), None)
    state = (
        P(None, ("dp", "expert"), None),
        P(None, ("dp", "expert")),
        P(None, ("dp", "expert")),
        P("expert", "dp", None),
        P("expert", "dp"),
        P("expert", "dp", None),
        P("expert", "dp"),
    )
    return jax.shard_map(
        body,
        mesh=mesh,
        in_specs=(rows, rows, rows, P(("dp", "expert")), *state, *state, *state),
        out_specs=(rows, rows, *state, *state, *state, *state),
        check_vma=False,
    )
```

```python
import functools
import math

import jax
import jax.numpy as jnp
from jax import lax
from jax.experimental import pallas as pl
from jax.experimental.pallas import tpu as pltpu
from jax.sharding import PartitionSpec as P

D = 768
HEADS = 12
HEAD_DIM = 64
LEN = 256
STEP = 3
ROWS = 256
BIAS_ROWS = 16

NORM_EPS = 1e-06
NEG_FILL = -1000000000.0
BETA_ONE = 0.9
BETA_TWO = 0.95
WEIGHT_DECAY = 0.1
ADAM_EPS = 1e-08
GELU_C = 0.7978845608028654
GELU_K = 0.044715
f32 = jnp.float32
b16 = jnp.bfloat16
MESH = pl.DeviceIdType.MESH


def adam_step(weight, grad, first, square, rate):
    new_first = BETA_ONE * first + (1.0 - BETA_ONE) * grad
    new_square = BETA_TWO * square + (1.0 - BETA_TWO) * grad * grad
    first_hat = new_first / (1.0 - BETA_ONE**STEP)
    square_hat = new_square / (1.0 - BETA_TWO**STEP)
    update = -rate * (first_hat / (jnp.sqrt(square_hat) + ADAM_EPS) + WEIGHT_DECAY * weight)
    return (weight + update, new_first, new_square)


def slots_of(routes, experts, capacity):
    flat = routes.reshape(-1, 2 * ROWS)
    onehot = (flat[:, :, None] == jnp.arange(experts, dtype=jnp.int32)).astype(b16)
    row = lax.broadcasted_iota(jnp.int32, (2 * ROWS, 2 * ROWS), 0)
    col = lax.broadcasted_iota(jnp.int32, (2 * ROWS, 2 * ROWS), 1)
    earlier = (col < row).astype(b16)
    before = jnp.einsum("ij,bje->bie", earlier, onehot, preferred_element_type=f32)
    slot = jnp.sum(before * onehot.astype(f32), axis=-1).astype(jnp.int32)
    return (flat * capacity + slot).reshape(-1, ROWS, 2)


def where_am_i():
    side = math.isqrt(lax.axis_size("expert") // 2)
    spot = lax.axis_index("expert")
    return side, lax.axis_index("dp"), spot // (2 * side), spot // 2 % side, spot % 2


def greet(peers):
    barrier = pltpu.get_barrier_semaphore()
    for peer in peers:
        pl.semaphore_signal(barrier, inc=1, device_id=peer, device_id_type=MESH)
    pl.semaphore_wait(barrier, len(peers))


def peers_of(n, side, z, y, x, core):
    def at(z_, y_, x_, core_):
        return (z_, (y_ * side + x_) * 2 + core_)

    along_z = [at((z + k) % n, y, x, core) for k in range(1, n)]
    first = [at(z, (y + core * k) % side, (x + (1 - core) * k) % side, core) for k in range(1, side)]
    second = [at(z, (y + (1 - core) * k) % side, (x + core * k) % side, core) for k in range(1, side)]
    return along_z, first, second, at(z, y, x, 1 - core)


def remote(src, dst, send, recv, peer):
    return pltpu.make_async_remote_copy(
        src_ref=src, dst_ref=dst, send_sem=send, recv_sem=recv, device_id=peer, device_id_type=MESH
    )


def spread_blocks(n, in_ref, block_at, sems, meanwhile, at_last):
    z_s, z_r, a_s, a_r, b_s, b_r, c_s, c_r = sems
    side, z, y, x, core = where_am_i()
    along_z, first, second, sibling = peers_of(n, side, z, y, x, core)
    sent = []

    def block(j, ka, kb, core_):
        y_ = (y - core * ka - (1 - core) * kb + 2 * side) % side
        x_ = (x - (1 - core) * ka - core * kb + 2 * side) % side
        return block_at(((((z - j + n) % n) * side + y_) * side + x_) * 2 + core_)

    def send(src, dst, send_sem, recv_sem, peer):
        copy = remote(src, dst, send_sem, recv_sem, peer)
        copy.start()
        sent.append(copy)

    def pass_on(src, dst, j, ka, kb):
        if kb == 0:
            if ka == 0:
                for k in range(1, side):
                    send(src, dst, a_s.at[j * side + k], a_r.at[j * side + k], first[k - 1])
            for k in range(1, side):
                place = (j * side + ka) * side + k
                send(src, dst, b_s.at[place], b_r.at[place], second[k - 1])
        place = (j * side + kb) * side + ka
        send(src, dst, c_s.at[place], c_r.at[place], sibling)

    for k in range(1, n):
        send(in_ref, block(0, 0, 0, core), z_s.at[k], z_r.at[k], along_z[k - 1])
    meanwhile()
    pass_on(in_ref, block(0, 0, 0, core), 0, 0, 0)
    for j in range(1, n):
        here = block(j, 0, 0, core)
        remote(here, here, z_s.at[j], z_r.at[j], sibling).wait_recv()
        pass_on(here, here, j, 0, 0)
    for j in range(n):
        for ka in range(1, side):
            here = block(j, ka, 0, core)
            remote(here, here, a_s.at[j * side + ka], a_r.at[j * side + ka], sibling).wait_recv()
            pass_on(here, here, j, ka, 0)
    for j in range(n):
        for ka in range(side):
            for kb in range(1, side):
                here = block(j, ka, kb, core)
                place = (j * side + ka) * side + kb
                remote(here, here, b_s.at[place], b_r.at[place], sibling).wait_recv()
                pass_on(here, here, j, ka, kb)
    at_last()
    for j in range(n):
        for ka in range(side):
            for kb in range(side):
                here = block(j, ka, kb, 1 - core)
                place = (j * side + ka) * side + kb
                remote(here, here, c_s.at[place], c_r.at[place], sibling).wait_recv()
    return sent


def spread_sems(n, side):
    dma = pltpu.SemaphoreType.DMA
    return [*[dma((n,))] * 2, *[dma((n * side,))] * 2, *[dma((n * side * side,))] * 4]


def exchange_all(pairs, sent):
    z, mine = lax.axis_index("dp"), lax.axis_index("expert")
    experts = lax.axis_size("expert")
    for k in range(1, experts):
        to = (mine + k) % experts
        for src, dst, send, recv in pairs:
            copy = remote(src(to), dst(mine), send.at[k], recv.at[k], (z, to))
            copy.start()
            sent.append(copy)


def wait_all(pairs):
    z, mine = lax.axis_index("dp"), lax.axis_index("expert")
    experts = lax.axis_size("expert")
    for k in range(1, experts):
        came = (mine - k + experts) % experts
        for _, dst, send, recv in pairs:
            remote(dst(came), dst(came), send.at[k], recv.at[k], (z, came)).wait_recv()


def gather_kernel(
    n, in_ref, own_ref, slots_ref, marks_ref, out_ref, second_ref, third_ref, slots_in, marks_in,
    local_sem, part_s, part_r, slot_s, slot_r, mark_s, mark_r, *sems,
):
    side, z, y, x, core = where_am_i()
    mine = lax.axis_index("expert")
    experts = slots_ref.shape[0]
    greet([*peers_of(n, side, z, y, x, core)[0], *[(z, (mine + k) % experts) for k in range(1, experts)]])
    me = ((z * side + y) * side + x) * 2 + core
    stays = [
        pltpu.make_async_copy(in_ref, out_ref.at[me], local_sem.at[0]),
        pltpu.make_async_copy(slots_ref.at[mine], slots_in.at[mine], local_sem.at[1]),
        pltpu.make_async_copy(marks_ref.at[mine], marks_in.at[mine], local_sem.at[2]),
    ]
    for copy in stays:
        copy.start()
    beside = remote(own_ref, second_ref, part_s.at[0], part_r.at[0], (z + 1 - 2 * (z % 2), mine))
    across = remote(own_ref, third_ref, part_s.at[1], part_r.at[1], ((n - 1 - z) % n, mine))
    inner = (z + 1) // 2 % 2 == 1
    pairs = [
        (lambda e: slots_ref.at[e], lambda e: slots_in.at[e], slot_s, slot_r),
        (lambda e: marks_ref.at[e], lambda e: marks_in.at[e], mark_s, mark_r),
    ]
    more = []

    def weights_on():
        beside.start()

        @pl.when(inner)
        def _():
            across.start()

    sent = spread_blocks(n, in_ref, lambda d: out_ref.at[d], sems, weights_on, lambda: exchange_all(pairs, more))
    wait_all(pairs)
    for copy in [*sent, *more]:
        copy.wait_send()
    for copy in stays:
        copy.wait()
    beside.wait()

    @pl.when(inner)
    def _():
        across.wait()


def gather_dense(packed, own, slots, marks, n, side):
    devices = n * side * side * 2
    experts = slots.shape[0]
    dma = pltpu.SemaphoreType.DMA
    sems = [dma((3,)), *[dma((2,))] * 2, *[dma((experts,))] * 4, *spread_sems(n, side)]
    vmem, hbm = pl.BlockSpec(memory_space=pltpu.VMEM), pl.BlockSpec(memory_space=pl.ANY)
    gathered = jax.ShapeDtypeStruct((devices, *packed.shape), packed.dtype)
    return pl.pallas_call(
        functools.partial(gather_kernel, n),
        out_shape=[gathered, *[jax.ShapeDtypeStruct(v.shape, v.dtype) for v in (own, own, slots, marks)]],
        in_specs=[vmem, hbm, hbm, hbm],
        out_specs=[vmem, *[hbm] * 4],
        scratch_shapes=sems,
        compiler_params=pltpu.CompilerParams(collective_id=0, has_side_effects=True, vmem_limit_bytes=60 << 20),
        cost_estimate=CHEAP,
        name="gather_dense",
    )(packed, own, slots, marks)


TILE = 512


def dot(a, b, contract):
    return lax.dot_general(a, b, (contract, ((), ())), preferred_element_type=f32)


NN = ((1,), (0,))
NT = ((1,), (1,))
TN = ((0,), (0,))


def expert_tile(x, dout, up, up_bias, down):
    pre = dot(x, up, NT) + up_bias
    grad_hidden = dot(dout, down, NT)
    square = pre * pre
    inner = jnp.tanh(pre * (GELU_C + GELU_C * GELU_K * square))
    half = 0.5 * pre
    hidden = (half + half * inner).astype(b16)
    slope = 0.5 + 0.5 * inner + half * (1.0 - inner * inner) * (GELU_C + 3.0 * GELU_C * GELU_K * square)
    grad_pre = (slope * grad_hidden).astype(b16)
    return hidden, grad_pre, dot(hidden, down, NN), dot(grad_pre, up, NN)


def bias_rows(first, second):
    row = lax.broadcasted_iota(jnp.int32, (BIAS_ROWS, D), 0)
    return jnp.where(row == 0, first, jnp.where(row == 1, second, 0.0))


def expert_kernel(sources, first, last, part, *refs):
    refs = list(refs)
    weights = [refs.pop(0) for _ in range(sources)]
    x_ref, dout_ref, bias_ref = refs[:3]
    refs = refs[3:]
    sums = [None, None] if first else [refs.pop(0), refs.pop(0)]
    out_ref, grad_x_ref, grad_up_ref, grad_down_ref, w_ref, up_acc, down_acc, bias_acc, sem = refs
    step = pl.program_id(0)

    @pl.when(step == 0)
    def _():
        if sources == 1:
            copy = pltpu.make_async_copy(weights[0], w_ref, sem)
            copy.start()
            copy.wait()
        else:
            me = lax.axis_index("dp")
            inner = (me + 1) // 2 % 2

            @pl.when(inner == 1)
            def _():
                pltpu.make_async_copy(weights[0], w_ref, sem).start()

            @pl.when(inner == 0)
            def _():
                pltpu.make_async_copy(weights[1], w_ref, sem).start()

            pltpu.make_async_copy(weights[0], w_ref, sem).wait()
        up_acc[...] = jnp.zeros_like(up_acc)
        down_acc[...] = jnp.zeros_like(down_acc)
        bias_acc[...] = jnp.zeros_like(bias_acc)

    x = x_ref[...]
    dout = dout_ref[...]
    up = w_ref[:part]
    down = w_ref[part : 2 * part]
    up_bias = w_ref[2 * part :][0:1, :part].astype(f32)
    hidden, grad_pre_b, out, grad_x = expert_tile(x, dout, up, up_bias, down)
    if not first:
        out = out + sums[0][...]
        grad_x = grad_x + sums[1][...]
    if last:
        out = out + bias_ref[1:2, :]
    out_ref[...] = out.astype(out_ref.dtype)
    grad_x_ref[...] = grad_x.astype(grad_x_ref.dtype)
    down_acc[...] += dot(hidden, dout, TN)
    up_acc[...] += dot(grad_pre_b, x, TN)
    bias_acc[0:1, :] += jnp.sum(grad_pre_b.astype(f32), axis=0, keepdims=True)

    @pl.when(step == pl.num_programs(0) - 1)
    def _():
        grad_up_ref[...] = up_acc[...].astype(grad_up_ref.dtype)
        grad_down_ref[:part] = down_acc[...].astype(grad_down_ref.dtype)
        tail = bias_rows(bias_acc[0:1, :], bias_ref[0:1, :])
        grad_down_ref[part:] = tail.astype(grad_down_ref.dtype)


def expert_part(weights, x, dout, biases, sums, last, grad_type, name):
    first = sums is None
    slots = x.shape[0]
    rows = weights[0].shape[0]
    part = (rows - BIAS_ROWS) // 2
    tile = pl.BlockSpec((TILE, D), lambda i: (i, 0))
    kept = b16 if last else f32
    n = len(weights)
    return pl.pallas_call(
        functools.partial(expert_kernel, n, first, last, part),
        grid=(slots // TILE,),
        in_specs=[
            *[pl.BlockSpec(memory_space=pl.ANY)] * n,
            tile,
            tile,
            pl.BlockSpec((2, D), lambda i: (0, 0)),
            *([] if first else [tile, tile]),
        ],
        out_specs=[
            tile,
            tile,
            pl.BlockSpec((part, D), lambda i: (0, 0)),
            pl.BlockSpec((part + BIAS_ROWS, D), lambda i: (0, 0)),
        ],
        out_shape=[
            jax.ShapeDtypeStruct((slots, D), kept),
            jax.ShapeDtypeStruct((slots, D), kept),
            jax.ShapeDtypeStruct((part, D), grad_type),
            jax.ShapeDtypeStruct((part + BIAS_ROWS, D), grad_type),
        ],
        scratch_shapes=[
            pltpu.VMEM((rows, D), b16),
            pltpu.VMEM((part, D), f32),
            pltpu.VMEM((part, D), f32),
            pltpu.VMEM((8, part), f32),
            pltpu.SemaphoreType.DMA,
        ],
        compiler_params=pltpu.CompilerParams(vmem_limit_bytes=56 << 20, dimension_semantics=("arbitrary",)),
        cost_estimate=pl.CostEstimate(flops=48 * slots * part * D, bytes_accessed=slots * D * 20, transcendentals=0),
        name=name,
    )(*weights, x, dout, biases, *([] if first else sums))


SCALE = HEAD_DIM ** (-0.5)
PAIRS = HEADS // 2
WIDE = 2 * HEAD_DIM
CHEAP = pl.CostEstimate(flops=0, bytes_accessed=1024, transcendentals=0)


def normal(values):
    center = values - jnp.mean(values, axis=-1, keepdims=True)
    rate = lax.rsqrt(jnp.mean(center * center, axis=-1, keepdims=True) + NORM_EPS)
    return center * rate, rate


def lanes_like(values):
    return lax.broadcasted_iota(jnp.int32, values.shape, values.ndim - 1)


def scores_of(part_q, pair_k, length):
    scores = dot(part_q, pair_k, NT) * SCALE
    return jnp.where(lanes_like(scores) < length, scores, NEG_FILL)


def halves(pair):
    low = lanes_like(pair) < HEAD_DIM
    zero = jnp.zeros_like(pair)
    return jnp.where(low, pair, zero), jnp.where(low, zero, pair)


def joined(even, odd):
    return jnp.where(lanes_like(even) < HEAD_DIM, even, odd)


def sequence_forward(
    s, lengths_ref, tokens_ref, weights_ref, vector_ref, router_ref, routes_ref, places_ref,
    normed_ref, q_ref, k_ref, v_ref, context_ref, lse_ref, resid_ref, normed_two_ref, gates_ref, slots_ref,
):
    at = pl.ds(s * LEN, LEN)
    length = lengths_ref[s]
    rows = tokens_ref[at, :].astype(f32)
    hat, _ = normal(rows)
    normed = (hat * vector_ref[0:1, :] + vector_ref[1:2, :]).astype(b16)
    normed_ref[at, :] = normed
    q_ref[at, :] = (dot(normed, weights_ref[0], NN) + vector_ref[2:3, :]).astype(b16)
    k_ref[at, :] = dot(normed, weights_ref[1], NN).astype(b16)
    v_ref[at, :] = (dot(normed, weights_ref[2], NN) + vector_ref[3:4, :]).astype(b16)
    lse = jnp.zeros((LEN, 128), f32)
    for pair in range(PAIRS):
        lanes = slice(pair * WIDE, (pair + 1) * WIDE)
        keys, values = k_ref[at, lanes], v_ref[at, lanes]
        mixed = []
        for half, part in enumerate(halves(q_ref[at, lanes])):
            scores = scores_of(part, keys, length)
            top = jnp.max(scores, axis=-1, keepdims=True)
            total = top + jnp.log(jnp.sum(jnp.exp(scores - top), axis=-1, keepdims=True))
            chance = jnp.exp(scores - total).astype(b16)
            mixed.append(dot(chance, values, NN))
            lse = jnp.where(lanes_like(lse) == 2 * pair + half, total, lse)
        context_ref[at, lanes] = joined(*mixed).astype(b16)
    lse_ref[at, :] = lse
    resid = rows + (dot(context_ref[at, :], weights_ref[3], NN) + vector_ref[4:5, :])
    resid_ref[at, :] = resid
    hat, _ = normal(resid)
    normed_two = (hat * vector_ref[5:6, :] + vector_ref[6:7, :]).astype(b16)
    normed_two_ref[at, :] = normed_two
    logits = dot(normed_two, router_ref[...], NT)
    names = lanes_like(logits)
    routes = routes_ref[at, :]
    first = jnp.sum(jnp.where(names == routes[:, 0:1], logits, 0.0), axis=-1, keepdims=True)
    second = jnp.sum(jnp.where(names == routes[:, 1:2], logits, 0.0), axis=-1, keepdims=True)
    gates_ref[at, :] = jnp.where(names == 0, jax.nn.sigmoid(first - second), jax.nn.sigmoid(second - first))
    experts, _, capacity, _ = slots_ref.shape
    slots = experts * capacity
    ids = lax.broadcasted_iota(jnp.int32, (slots, ROWS), 0)
    places = places_ref[s]
    chosen = jnp.where((ids == places[0:1, :]) | (ids == places[1:2, :]), 1.0, 0.0).astype(b16)
    sent = dot(chosen, normed_two, NN).astype(b16)
    slots_ref[:, s] = sent.reshape(experts, capacity, D)


def kept_shapes(count, experts, capacity):
    return [
        *[jax.ShapeDtypeStruct((count, D), b16)] * 5,
        jax.ShapeDtypeStruct((count, 128), f32),
        jax.ShapeDtypeStruct((count, D), f32),
        jax.ShapeDtypeStruct((count, D), b16),
        jax.ShapeDtypeStruct((count, 128), f32),
        jax.ShapeDtypeStruct((experts, count // ROWS, capacity, D), b16),
    ]


def attention_forward(lengths, tokens, weights, vector, router, routes, places, experts, capacity):
    count = tokens.shape[0]
    vmem = pl.BlockSpec(memory_space=pltpu.VMEM)

    def kernel(*refs):
        for s in range(count // LEN):
            sequence_forward(s, *refs)

    return pl.pallas_call(
        kernel,
        in_specs=[pl.BlockSpec(memory_space=pltpu.SMEM), *[vmem] * 6],
        out_specs=[vmem] * 10,
        out_shape=kept_shapes(count, experts, capacity),
        compiler_params=pltpu.CompilerParams(vmem_limit_bytes=48 << 20),
        cost_estimate=CHEAP,
        name="attention_forward",
    )(lengths, tokens, weights, vector, router, routes, places)


def norm_back(grad, hat, rate, gain):
    inner = grad * gain
    return rate * (
        inner
        - jnp.mean(inner, axis=-1, keepdims=True)
        - hat * jnp.mean(inner * hat, axis=-1, keepdims=True)
    )


def two_terms(values):
    high = values.astype(b16)
    return high, (values - high.astype(f32)).astype(b16)


def column_sum(values):
    return jnp.sum(values, axis=0, keepdims=True)


def sequence_backward(
    s, lengths_ref, tokens_ref, grad_ref, weights_ref, vector_ref, router_ref, routes_ref, places_ref,
    normed_ref, q_ref, k_ref, v_ref, context_ref, lse_ref, resid_ref, normed_two_ref, gates_ref, outs_ref, returned_ref,
    output_ref, input_grad_ref, weights_acc, vector_acc, router_acc, dq_ref, dk_ref, dv_ref,
):
    at = pl.ds(s * LEN, LEN)
    length = lengths_ref[s]
    experts, _, capacity, _ = outs_ref.shape
    slots = experts * capacity
    ids = lax.broadcasted_iota(jnp.int32, (ROWS, slots), 1)
    outs = outs_ref[:, s].reshape(slots, D)
    grad_out = grad_ref[at, :].astype(f32)
    places = places_ref[at, :]
    take = [jnp.where(ids == places[:, k : k + 1], 1.0, 0.0).astype(b16) for k in range(2)]
    out = [dot(t, outs, NN) for t in take]
    both_gates = gates_ref[at, :]
    gates = [both_gates[:, k : k + 1] for k in range(2)]
    resid = resid_ref[at, :]
    output_ref[at, :] = resid + gates[0] * out[0] + gates[1] * out[1]
    slopes = [
        jnp.sum(grad_out * out[k], axis=-1, keepdims=True) * (gates[k] * (1.0 - gates[k])) for k in range(2)
    ]
    pull = slopes[0] - slopes[1]
    names = lax.broadcasted_iota(jnp.int32, (ROWS, 128), 1)
    routes = routes_ref[at, :]
    grad_logits = jnp.where(names == routes[:, 0:1], pull, jnp.where(names == routes[:, 1:2], -pull, 0.0))
    high, low = two_terms(grad_logits)
    normed_two = normed_two_ref[at, :]
    router = router_ref[...]
    router_acc[...] += dot(high, normed_two, TN) + dot(low, normed_two, TN)
    returned = returned_ref[:, s].reshape(slots, D)
    grad_two = dot(take[0] + take[1], returned, NN) + (dot(high, router, NN) + dot(low, router, NN))
    hat, rate = normal(resid)
    vector_acc[5:6, :] += column_sum(grad_two * hat)
    vector_acc[6:7, :] += column_sum(grad_two)
    grad_resid = grad_out + norm_back(grad_two, hat, rate, vector_ref[5:6, :])
    input_grad_ref[at, :] = grad_resid
    branch = grad_resid.astype(b16)
    vector_acc[4:5, :] += column_sum(branch.astype(f32))
    weights_acc[3] += dot(context_ref[at, :], branch, TN)
    grad_context = dot(branch, weights_ref[3], NT).astype(b16)
    for pair in range(PAIRS):
        lanes = slice(pair * WIDE, (pair + 1) * WIDE)
        queries, keys, values = q_ref[at, lanes], k_ref[at, lanes], v_ref[at, lanes]
        given = grad_context[:, lanes]
        grads = []
        for half, (part, part_given) in enumerate(zip(halves(queries), halves(given))):
            head = 2 * pair + half
            chance = jnp.exp(scores_of(part, keys, length) - lse_ref[at, head : head + 1])
            grad_v = dot(chance.astype(b16), given, TN)
            grad_chance = dot(part_given, values, NT)
            mean = jnp.sum(chance * grad_chance, axis=-1, keepdims=True)
            grad_scores = (chance * (grad_chance - mean)).astype(b16)
            grads.append((dot(grad_scores, keys, NN), dot(grad_scores, queries, TN), grad_v))
        dq_ref[:, lanes] = (joined(grads[0][0], grads[1][0]) * SCALE).astype(b16)
        dk_ref[:, lanes] = (joined(grads[0][1], grads[1][1]) * SCALE).astype(b16)
        dv_ref[:, lanes] = joined(grads[0][2], grads[1][2]).astype(b16)
    normed = normed_ref[at, :]
    grad_one = jnp.zeros((LEN, D), f32)
    for k, ref in enumerate((dq_ref, dk_ref, dv_ref)):
        weights_acc[k] += dot(normed, ref[...], TN)
        grad_one += dot(ref[...], weights_ref[k], NT)
    vector_acc[2:3, :] += column_sum(dq_ref[...].astype(f32))
    vector_acc[3:4, :] += column_sum(dv_ref[...].astype(f32))
    hat, rate = normal(tokens_ref[at, :].astype(f32))
    vector_acc[0:1, :] += column_sum(grad_one * hat)
    vector_acc[1:2, :] += column_sum(grad_one)
    input_grad_ref[at, :] += norm_back(grad_one, hat, rate, vector_ref[0:1, :])


def begin_kernel(
    n, cols, seqs, part, lengths_ref, in_ref, own_ref, slots_ref, marks_ref, tokens_ref, routes_ref, places_ref,
    *refs,
):
    kept_out, refs = refs[:12], refs[12:]
    here, refs = refs[-12:], refs[:-12]
    weights_ref, vector_ref, router_ref, *attention_refs = here
    (
        out_ref, back_ref, mine_up, mine_down, near_up, near_down, middle_up, middle_down, far_up, far_down,
    near_up_in, near_down_in, middle_in,
    pool, acc, second_ref, third_ref, fourth_ref, going, x_in, dout_in, marks_in, out_acc, back_acc, bias_acc, tail_ref,
    local_sem, part_s, part_r, slot_s, slot_r, mark_s, mark_r, x_s, x_r, near_s, near_r, store_s, *sems,
    ) = refs
    side, z, y, x, core = where_am_i()
    mine = lax.axis_index("expert")
    experts, _, capacity, _ = slots_ref.shape
    slots = experts * seqs * capacity
    greet([*peers_of(n, side, z, y, x, core)[0], *[(z, (mine + k) % experts) for k in range(1, experts)]])
    me = ((z * side + y) * side + x) * 2 + core
    block_rows = in_ref.shape[0]
    stage_rows = 2 * part + BIAS_ROWS

    def block_at(device):
        return pool.at[pl.ds(pl.multiple_of(device * block_rows, 16), block_rows), :]

    def sender(ref, e, b=0, blocks=seqs):
        return ref.at[pl.ds(pl.multiple_of((e * seqs + b) * capacity, 16), blocks * capacity), :]

    flat_slots = slots_ref.reshape(slots, D)
    flat_marks = marks_ref.reshape(slots, 128)
    stays = [
        pltpu.make_async_copy(in_ref, block_at(me), local_sem.at[0]),
        pltpu.make_async_copy(sender(flat_slots, mine), sender(dout_in, mine), local_sem.at[1]),
        pltpu.make_async_copy(sender(flat_marks, mine), sender(marks_in, mine), local_sem.at[2]),
    ]
    for copy in stays:
        copy.start()
    inner = (z + 1) // 2 % 2 == 1
    outer = jnp.logical_not(inner)
    inward, across, outward = (1 + z // 2, mine), (3 - z, mine), (3 * (z // 2), mine)

    def hop(k, src, dst, peer):
        return remote(src, dst, part_s.at[k], part_r.at[k], peer)

    beside = hop(0, own_ref, second_ref, (z + 1 - 2 * (z % 2), mine))
    own_across = hop(1, own_ref, third_ref, across)
    third_on = hop(2, third_ref, third_ref, outward)
    second_across = hop(3, second_ref, fourth_ref, across)
    cut = part // 3 * 2
    spans = [(0, cut), (part, cut), (2 * part, BIAS_ROWS), (cut, part - cut), (part + cut, part - cut)]
    fourth_on = [
        hop(4 + i, fourth_ref.at[pl.ds(at, length), :], fourth_ref.at[pl.ds(at, length), :], outward)
        for i, (at, length) in enumerate(spans)
    ]

    def weights_on():
        beside.start()

        @pl.when(inner)
        def _():
            own_across.start()

    early = [
        (lambda e: sender(flat_slots, e), lambda e: sender(dout_in, e), slot_s, slot_r),
        (lambda e: sender(flat_marks, e), lambda e: sender(marks_in, e), mark_s, mark_r),
    ]
    more = []
    sent = spread_blocks(n, in_ref, block_at, sems, weights_on, lambda: exchange_all(early, more))
    stays[0].wait()

    for pair in range(2):
        def spread(device, carry):
            rows = block_at(device)[2 * pair * cols : 2 * (pair + 1) * cols, :].astype(f32)
            place = pl.ds(pl.multiple_of(device * cols, 8), cols)
            acc[0, place, :] = rows[:cols]
            acc[1, place, :] = rows[cols:]
            return carry

        lax.fori_loop(0, n * experts, spread, 0)
        weights_ref[2 * pair] = acc[0].astype(b16)
        weights_ref[2 * pair + 1] = acc[1].astype(b16)

    def gather_small(device, total):
        return total + block_at(device)[4 * cols :, :].astype(f32)

    small = lax.fori_loop(0, n * experts, gather_small, jnp.zeros((block_rows - 4 * cols, D), f32))
    vector_ref[...] = small[:8]
    router_ref[...] = jnp.zeros_like(router_ref)
    router_ref[: block_rows - 4 * cols - 8, :] = small[8:].astype(b16)

    late = []
    for s in range(seqs):
        sequence_forward(
            s, lengths_ref, tokens_ref, weights_ref, vector_ref, router_ref, routes_ref, places_ref, *attention_refs, going
        )
        dst = functools.partial(sender, x_in, b=s, blocks=1)
        late.append((functools.partial(lambda e, s: going.at[e, s], s=s), dst, x_s.at[s], x_r.at[s]))
        exchange_all(late[-1:], more)
        stays.append(pltpu.make_async_copy(going.at[mine, s], dst(mine), local_sem.at[3 + s]))
        stays[-1].start()
    stores = [pltpu.make_async_copy(src, dst, store_s.at[11 + k]) for k, (src, dst) in enumerate(zip(here, kept_out))]
    for copy in stores:
        copy.start()
    beside.wait()

    @pl.when(inner)
    def _():
        second_across.start()
        own_across.wait()
        third_on.start()

    wait_all(early)
    wait_all(late)
    for copy in [*sent, *more]:
        copy.wait_send()
    for copy in stays[1:]:
        copy.wait()

    up_acc, down_acc = acc.at[0], acc.at[1]
    tiles = slots // TILE
    down_bias = jnp.zeros((1, D), f32)
    outs = [(mine_up, mine_down), (near_up, near_down), (middle_up, middle_down), (far_up, far_down)]
    near_in = (near_up_in, near_down_in)
    bias_acc[...] = jnp.zeros_like(bias_acc)
    pieces = [(1, 0, part), (0, 0, part), (2, 0, part), (3, 0, cut), (3, cut, part)]
    for p, low, high in pieces:
        begins = p == 1
        w_ref = (own_ref, second_ref, third_ref, fourth_ref)[p]
        last = p == 3 and high == part
        if p == 0:

            @pl.when(inner)
            def _():
                second_across.wait()
                for copy in fourth_on:
                    copy.start()

        if p == 2:

            @pl.when(outer)
            def _():
                third_on.wait_recv()

        if p == 3:

            @pl.when(outer)
            def _():
                for copy in fourth_on[3:] if low else fourth_on[:3]:
                    copy.wait_recv()

        if low == 0:
            up_acc[...] = jnp.zeros_like(up_acc)
            down_acc[...] = jnp.zeros_like(down_acc)
            bias_acc[0:1, :] = jnp.zeros((1, D), f32)

        biases = w_ref[2 * part :, :].astype(f32)
        up_bias = biases[0:1, low:high]
        if low == 0:
            down_bias = down_bias + biases[1:2, :]

        def tile(t, carry):
            rows = pl.ds(pl.multiple_of(t * TILE, TILE), TILE)
            x = x_in[rows, :]
            if begins:
                logits = dot(x, router_ref[...], NT)
                signs = jnp.where(lanes_like(logits) == mine, 1.0, -marks_in[rows, :].astype(f32))
                margin = jnp.sum(logits * signs, axis=-1, keepdims=True)
                dout = (jax.nn.sigmoid(margin) * dout_in[rows, :].astype(f32)).astype(b16)
                dout_in[rows, :] = dout
                bias_acc[1:2, :] += column_sum(dout.astype(f32))
            else:
                dout = dout_in[rows, :]
            hidden, grad_pre, out, back = expert_tile(
                x, dout, w_ref[low:high, :], up_bias, w_ref[part + low : part + high, :]
            )
            down_acc[low:high, :] += dot(hidden, dout, TN)
            up_acc[low:high, :] += dot(grad_pre, x, TN)
            bias_acc[0:1, low:high] += column_sum(grad_pre.astype(f32))
            if begins:
                out_acc[rows, :] = out
                back_acc[rows, :] = back
            elif not last:
                out_acc[rows, :] += out
                back_acc[rows, :] += back
            else:
                x_in[rows, :] = (out_acc[rows, :] + out + down_bias).astype(b16)
                dout_in[rows, :] = (back_acc[rows, :] + back).astype(b16)
            return carry

        lax.fori_loop(0, tiles, tile, 0)
        if high < part:
            continue
        tail = bias_rows(bias_acc[0:1, :], bias_acc[1:2, :])
        base = stage_rows if p == 2 else 0
        if p == 0:
            tail_ref[...] = tail
            now = [
                pltpu.make_async_copy(up_acc, mine_up, store_s.at[0]),
                pltpu.make_async_copy(down_acc, mine_down.at[pl.ds(0, part), :], store_s.at[1]),
                pltpu.make_async_copy(tail_ref, mine_down.at[pl.ds(part, BIAS_ROWS), :], store_s.at[2]),
            ]
            for copy in now:
                copy.start()
            for copy in now:
                copy.wait()
        else:
            if p == 3:
                for copy in stores[12:14]:
                    copy.wait()
                del stores[12:14]

                @pl.when(outer)
                def _():
                    for copy in nears[:2]:
                        copy.wait_send()

            pool[base : base + part, :] = up_acc[...].astype(b16)
            pool[base + part : base + 2 * part, :] = down_acc[...].astype(b16)
            pool[base + 2 * part : base + stage_rows, :] = tail.astype(b16)
            halves_of = [pool.at[pl.ds(base, part), :], pool.at[pl.ds(base + part, part + BIAS_ROWS), :]]
            for h in range(2):
                stores.append(pltpu.make_async_copy(halves_of[h], outs[p][h], store_s.at[1 + 2 * p + h]))
                stores[-1].start()
            if p == 1:
                nears = [remote(halves_of[h], near_in[h], near_s.at[h], near_r.at[h], inward) for h in range(2)]

                @pl.when(outer)
                def _():
                    for copy in nears:
                        copy.start()

            if p == 2:
                middle = remote(halves_of[0], middle_in, near_s.at[2], near_r.at[2], inward)
                nears.append(middle)

                @pl.when(outer)
                def _():
                    middle.start()

    for src, dst, k in ((x_in, out_ref, 9), (dout_in, back_ref, 10)):
        stores.append(pltpu.make_async_copy(src, dst, store_s.at[k]))
        stores[-1].start()
    for copy in stores:
        copy.wait()

    @pl.when(inner)
    def _():
        for copy in [third_on, *fourth_on]:
            copy.wait_send()
        for copy in nears:
            copy.wait_recv()

    @pl.when(outer)
    def _():
        nears[2].wait_send()


def begin(n, side, cols, lengths, packed, own, slots, marks, tokens, routes, places):
    devices = n * side * side * 2
    experts, blocks, capacity, _ = slots.shape
    count = tokens.shape[0]
    total = experts * blocks * capacity
    part = (own.shape[0] - BIAS_ROWS) // 2
    dma = pltpu.SemaphoreType.DMA
    vmem, hbm = pl.BlockSpec(memory_space=pltpu.VMEM), pl.BlockSpec(memory_space=pl.ANY)
    *kept, going = kept_shapes(count, experts, capacity)
    held = [
        jax.ShapeDtypeStruct((4, D, D), b16),
        jax.ShapeDtypeStruct((8, D), f32),
        jax.ShapeDtypeStruct((128, D), b16),
        *kept,
    ]

    def halves_in(dtype):
        return [jax.ShapeDtypeStruct((part, D), dtype), jax.ShapeDtypeStruct((part + BIAS_ROWS, D), dtype)]

    return pl.pallas_call(
        functools.partial(begin_kernel, n, cols, blocks, part),
        out_shape=[
            *held,
            *[jax.ShapeDtypeStruct((total, D), b16)] * 2,
            *halves_in(f32),
            *halves_in(b16) * 4,
            halves_in(b16)[0],
        ],
        in_specs=[pl.BlockSpec(memory_space=pltpu.SMEM), vmem, vmem, hbm, hbm, vmem, vmem, vmem],
        out_specs=[hbm] * 25,
        scratch_shapes=[
            pltpu.VMEM((max(devices * packed.shape[0], 2 * own.shape[0]), D), b16),
            pltpu.VMEM((2, D, D), f32),
            *[pltpu.VMEM(own.shape, b16)] * 3,
            pltpu.VMEM(going.shape, b16),
            *[pltpu.VMEM((total, D), b16)] * 2,
            pltpu.VMEM((total, 128), b16),
            *[pltpu.VMEM((total, D), f32)] * 2,
            pltpu.VMEM((8, D), f32),
            pltpu.VMEM((BIAS_ROWS, D), f32),
            dma((3 + blocks,)),
            *[dma((9,))] * 2,
            *[dma((experts,))] * 4,
            *[dma((blocks, experts))] * 2,
            *[dma((3,))] * 2,
            dma((23,)),
            *spread_sems(n, side),
            *[pltpu.VMEM(v.shape, v.dtype) for v in held],
        ],
        compiler_params=pltpu.CompilerParams(collective_id=0, has_side_effects=True, vmem_limit_bytes=63 << 20),
        cost_estimate=CHEAP,
        name="begin",
    )(lengths, packed, own, slots, marks, tokens, routes, places)


KINDS = 5
FAR, MIDDLE, FAR_ON, MIDDLE_ON, FAR_LAST = range(KINDS)


def finish_kernel(
    n, cols, extra, seqs, lengths_ref, vector_ref, router_ref, routes_ref, places_ref, *refs,
):
    brought, refs = refs[:12], refs[12:]
    here, refs = refs[-12:], refs[:-12]
    tokens_ref, grad_ref, weights_ref, *attention_refs = here
    (
        outs_ref, backs_ref,
        near_up, near_down, middle_up, middle_down, far_up, far_down, middle_came,
        output_ref, input_grad_ref, dense_ref, middle_up_in, middle_down_in, end_up_in, end_down_in,
        outs_in, backs_in, weights_acc, vector_acc, router_acc, dq_ref, dk_ref, dv_ref,
        far_up_buf, far_down_buf, middle_up_buf, middle_down_buf, on_up_buf, on_down_buf, load_up, load_down,
        parts, stage, c_buf, b_buf, a_buf, z_buf,
        own_s, out_s, out_r, back_s, back_r, chain_s, chain_r, load_s, came_s, c_s, c_r, b_s, b_r, a_s, a_r, z_s, z_r,
    ) = refs
    inside = cols % 8 == 0
    side, z, y, x, core = where_am_i()
    mine = lax.axis_index("expert")
    experts = outs_in.shape[0]
    along_z, first, second, sibling = peers_of(n, side, z, y, x, core)
    plane = [(z, (mine + k) % experts) for k in range(1, experts)]
    greet([*along_z, *plane])
    area = side * side if inside else 0
    sent = []

    def send(src, dst, send_sem, recv_sem, peer):
        copy = remote(src, dst, send_sem, recv_sem, peer)
        copy.start()
        sent.append(copy)

    def by_sequence(s):
        return [
            (lambda e: outs_ref.at[e, s], lambda e: outs_in.at[e, s], out_s.at[s], out_r.at[s]),
            (lambda e: backs_ref.at[e, s], lambda e: backs_in.at[e, s], back_s.at[s], back_r.at[s]),
        ]

    for s in range(seqs):
        exchange_all(by_sequence(s), sent)
    own = [
        pltpu.make_async_copy(outs_ref.at[mine], outs_in.at[mine], own_s.at[0]),
        pltpu.make_async_copy(backs_ref.at[mine], backs_in.at[mine], own_s.at[1]),
    ]
    own += [pltpu.make_async_copy(src, dst, own_s.at[2 + k]) for k, (src, dst) in enumerate(zip(brought, here))]
    for copy in own:
        copy.start()

    inner = (z + 1) // 2 % 2 == 1
    outer = jnp.logical_not(inner)
    inward = (z - z + 1 + z // 2, mine)
    across = (3 - z, mine)
    outward = (3 * (z // 2), mine)
    near, middle, far = (near_up, near_down), (middle_up, middle_down), (far_up, far_down)
    middle_in = (middle_up_in, middle_down_in)
    end_in = (end_up_in, end_down_in)
    far_buf, middle_buf, on_buf = (far_up_buf, far_down_buf), (middle_up_buf, middle_down_buf), (on_up_buf, on_down_buf)
    loads = (load_up, load_down)

    whole = [(h, 0, far[h].shape[0]) for h in range(2)]
    split = far[0].shape[0] // 32 * 16
    quarters = [(h, at, split if at == 0 else far[h].shape[0] - split) for h in range(2) for at in (0, split)]

    def hop(kind, k, piece, src, dst, peer):
        h, at, length = piece
        rows = pl.ds(at, length)
        return remote(src[h].at[rows, :], dst[h].at[rows, :], chain_s.at[kind, k], chain_r.at[kind, k], peer)

    from_ends = [(FAR, whole, far, far_buf), (MIDDLE, quarters, middle, middle_buf)]

    @pl.when(outer)
    def _():
        for kind, cuts, src, dst in from_ends:
            for k, piece_ in enumerate(cuts):
                if kind == FAR or piece_[0]:
                    hop(kind, k, piece_, src, dst, inward).start()

    def chain_step(kind, k, piece_, buf, term, next_kind, target, peer):
        @pl.when(inner)
        def _():
            h, at, length = piece_
            rows = pl.ds(at, length)
            load = pltpu.make_async_copy(term[h].at[rows, :], loads[h].at[rows, :], load_s)
            load.start()
            if kind == MIDDLE and h == 0:
                came = pltpu.make_async_copy(middle_came.at[rows, :], buf[h].at[rows, :], came_s)
                came.start()
                came.wait()
            else:
                hop(kind, k, piece_, buf, buf, across).wait_recv()
            load.wait()
            buf[h][rows, :] = (buf[h][rows, :].astype(f32) + loads[h][rows, :].astype(f32)).astype(b16)
            hop(next_kind, k, piece_, buf, target, peer).start()

    def step_far(k):
        chain_step(FAR, k, whole[k], far_buf, far, FAR_ON, on_buf, across)

    def step_on(k):
        chain_step(FAR_ON, k, whole[k], on_buf, near, FAR_LAST, end_in, outward)

    def step_middle(k):
        chain_step(MIDDLE, k, quarters[k], middle_buf, middle, MIDDLE_ON, middle_in, across)

    weights_acc[...] = jnp.zeros_like(weights_acc)
    vector_acc[...] = jnp.zeros_like(vector_acc)
    router_acc[...] = jnp.zeros_like(router_acc)
    step_middle(0)
    step_middle(1)
    step_far(0)
    for copy in own:
        copy.wait()
    for s in range(seqs):
        wait_all(by_sequence(s))
        sequence_backward(
            s, lengths_ref, tokens_ref, grad_ref, weights_ref, vector_ref, router_ref, routes_ref, places_ref,
            *attention_refs, outs_in, backs_in,
            output_ref, input_grad_ref, weights_acc, vector_acc, router_acc, dq_ref, dk_ref, dv_ref,
        )
        if s == 0:
            step_far(1)
            step_on(0)
    step_on(1)
    step_middle(2)
    step_middle(3)

    small = jnp.concatenate([vector_acc[...], router_acc[: extra - 8, :]], axis=0).astype(b16)
    if not inside:
        dense_ref[:extra, :] = jnp.concatenate([vector_acc[...], router_acc[: extra - 8, :]], axis=0)
        for k in range(4):
            dense_ref[extra + k * D : extra + (k + 1) * D, :] = weights_acc[k]
    for core_ in range(2 if inside else 0):
        for y_ in range(side):
            for x_ in range(side):
                for z_ in range(n):
                    owner = ((z_ * side + y_) * side + x_) * 2 + core_
                    rows = [weights_acc[k, owner * cols : (owner + 1) * cols, :] for k in range(4)]
                    place = parts.at[(core_ * side + y_) * side + x_, z_]
                    place[: 4 * cols, :] = jnp.concatenate(rows, axis=0).astype(b16)
                    place[4 * cols :, :] = small

    def piece(ka, kb, core_):
        y_ = (y + core * ka + (1 - core) * kb) % side
        x_ = (x + (1 - core) * ka + core * kb) % side
        return (core_ * side + y_) * side + x_

    order = [(ka, kb) for kb in [*range(1, side), 0] for ka in [*range(1, side), 0]][:area]
    for ka, kb in order:
        place = ka * side + kb
        send(parts.at[piece(kb, ka, 1 - core)], c_buf.at[place], c_s.at[place], c_r.at[place], sibling)
    for ka, kb in order:
        place = ka * side + kb
        remote(c_buf.at[place], c_buf.at[place], c_s.at[place], c_r.at[place], sibling).wait_recv()
        mine_ = piece(ka, kb, core)
        if kb:
            stage[place] = (parts[mine_].astype(f32) + c_buf[place].astype(f32)).astype(b16)
            send(stage.at[place], b_buf.at[place], b_s.at[place], b_r.at[place], second[kb - 1])
        else:
            total = parts[mine_].astype(f32) + c_buf[place].astype(f32)
            for k in range(1, side):
                slot = ka * side + k
                remote(b_buf.at[slot], b_buf.at[slot], b_s.at[slot], b_r.at[slot], sibling).wait_recv()
                total = total + b_buf[slot].astype(f32)
            if ka:
                stage[place] = total.astype(b16)
                send(stage.at[place], a_buf.at[ka], a_s.at[ka], a_r.at[ka], first[ka - 1])
            else:
                for k in range(1, side):
                    remote(a_buf.at[k], a_buf.at[k], a_s.at[k], a_r.at[k], sibling).wait_recv()
                    total = total + a_buf[k].astype(f32)
                stage[place] = total.astype(b16)
    if inside:
        for k in range(1, n):
            send(stage.at[0, (z + k) % n], z_buf.at[k], z_s.at[k], z_r.at[k], along_z[k - 1])
        result = stage[0, z].astype(f32)
        for k in range(1, n):
            remote(z_buf.at[k], z_buf.at[k], z_s.at[k], z_r.at[k], sibling).wait_recv()
            result = result + z_buf[k].astype(f32)
        dense_ref[...] = result
    for copy in sent:
        copy.wait_send()

    @pl.when(outer)
    def _():
        for kind, cuts, src, dst in from_ends:
            for k, piece_ in enumerate(cuts):
                if kind == FAR or piece_[0]:
                    hop(kind, k, piece_, src, dst, inward).wait_send()
        for k, piece_ in enumerate(whole):
            hop(FAR_LAST, k, piece_, end_in, end_in, inward).wait_recv()

    @pl.when(inner)
    def _():
        for k, piece_ in enumerate(whole):
            hop(FAR_ON, k, piece_, far_buf, on_buf, across).wait_send()
            hop(FAR_LAST, k, piece_, on_buf, end_in, outward).wait_send()
        for k, piece_ in enumerate(quarters):
            hop(MIDDLE_ON, k, piece_, middle_buf, middle_in, across).wait()


def finish(n, side, cols, extra, lengths, small, rows_in, kept, outs, backs, grads):
    count = rows_in[0].shape[0]
    held = (*rows_in, *kept)
    slots = outs.shape
    vmem = pl.BlockSpec(memory_space=pltpu.VMEM)
    hbm = pl.BlockSpec(memory_space=pl.ANY)
    shapes = [jax.ShapeDtypeStruct(g.shape, b16) for g in grads[:2]]
    inside = cols % 8 == 0
    rows = 4 * cols + extra if inside else 4 * D + extra
    block = (n, rows, D) if inside else (1, 16, 128)
    dma = pltpu.SemaphoreType.DMA
    half = [pltpu.VMEM(g.shape, b16) for g in grads[:2]]
    area = side * side
    return pl.pallas_call(
        functools.partial(finish_kernel, n, cols, extra, count // LEN),
        in_specs=[
            pl.BlockSpec(memory_space=pltpu.SMEM),
            *[vmem] * len(small),
            *[hbm] * (len(held) + 2 + len(grads)),
        ],
        out_specs=[vmem, vmem, vmem, *[hbm] * 4],
        out_shape=[
            jax.ShapeDtypeStruct((count, D), f32),
            jax.ShapeDtypeStruct((count, D), f32),
            jax.ShapeDtypeStruct((rows, D), f32),
            *shapes * 2,
        ],
        scratch_shapes=[
            pltpu.VMEM(slots, b16),
            pltpu.VMEM(slots, b16),
            pltpu.VMEM((4, D, D), f32),
            pltpu.VMEM((8, D), f32),
            pltpu.VMEM((128, D), f32),
            *[pltpu.VMEM((LEN, D), b16)] * 3,
            *half * 4,
            pltpu.VMEM((2 * area, *block), b16),
            pltpu.VMEM((area, *block), b16),
            pltpu.VMEM((area, *block), b16),
            pltpu.VMEM((area, *block), b16),
            pltpu.VMEM((side, *block), b16),
            pltpu.VMEM(block, b16),
            dma((2 + len(held),)),
            *[dma((slots[1], slots[0]))] * 4,
            *[dma((KINDS, 4))] * 2,
            dma,
            dma,
            *[dma((area,))] * 4,
            *[dma((side,))] * 2,
            *[dma((n,))] * 2,
            *[pltpu.VMEM(v.shape, v.dtype) for v in held],
        ],
        compiler_params=pltpu.CompilerParams(collective_id=1, has_side_effects=True, vmem_limit_bytes=63 << 20),
        cost_estimate=CHEAP,
        name="finish",
    )(lengths, *small, *held, outs, backs, *grads)


def pack_expert(up, down, up_bias, down_bias, start, dtype):
    part = up.shape[0]
    tail = jnp.zeros((BIAS_ROWS, D), dtype)
    tail = tail.at[0, :part].set(up_bias.astype(dtype))
    tail = lax.dynamic_update_slice(tail, down_bias.astype(dtype)[None], (1, start))
    return jnp.concatenate([up.astype(dtype), down.astype(dtype), tail], axis=0)


def along(x, *pairs):
    return lax.ppermute(x, "dp", pairs)


def body(
    tokens, out_grad, routes, lengths,
    attention, gain_bias, router, expert_up, up_bias, expert_down, down_bias,
    first_attention, first_gain_bias, first_router, first_expert_up, first_up_bias, first_expert_down, first_down_bias,
    square_attention, square_gain_bias, square_router, square_expert_up, square_up_bias, square_expert_down, square_down_bias,
):
    experts = router.shape[0]
    capacity = 4 * ROWS // experts
    count = tokens.shape[0]
    blocks = count // ROWS
    part = expert_up.shape[1]
    narrow = down_bias.shape[1]
    cols = attention.shape[1]
    devices = D // cols
    n_dp = lax.axis_size("dp")
    assert n_dp == 4 and expert_up.shape[0] == 1
    me = lax.axis_index("dp")
    mine = lax.axis_index("expert")
    both = ("dp", "expert")

    side = math.isqrt(experts // 2)
    inside = cols if cols % 8 == 0 else 0
    small_rows = -(-(8 + experts) // 16) * 16
    flat_len = (7 + experts) * cols
    if inside:
        small = jnp.zeros((small_rows, D), b16)
        column = (me * experts + mine) * cols
        small = lax.dynamic_update_slice(small, gain_bias.astype(b16), (0, column))
        small = lax.dynamic_update_slice(small, router.astype(b16), (8, column))
    else:
        extra = -(-(4 * cols + -(-flat_len // D)) // 16) * 16 - 4 * cols
        small = jnp.concatenate([gain_bias, router], axis=0).astype(b16).reshape(-1)
        small = jnp.pad(small, (0, extra * D - flat_len)).reshape(extra, D)
    packed = jnp.concatenate([attention.astype(b16).reshape(4 * cols, D), small], axis=0)
    own = pack_expert(expert_up[0], expert_down[0], up_bias[0], down_bias[0], me * narrow, b16)

    positions = slots_of(routes, experts, capacity)
    slot_ids = jnp.arange(experts * capacity, dtype=jnp.int32)
    hit = positions[:, :, :, None] == slot_ids
    split = jnp.any(hit, axis=2).astype(b16).reshape(blocks, ROWS, experts, capacity)
    marked = jnp.any(routes[:, :, None] == jnp.arange(128, dtype=jnp.int32), axis=1).astype(b16)

    def by_slot(rows):
        sent = jnp.einsum("btec,btd->ebcd", split, rows.reshape(blocks, ROWS, -1), preferred_element_type=f32)
        return sent.astype(b16)

    places = positions.transpose(0, 2, 1)
    inner = (me == 1) | (me == 2)
    if inside:
        weights_b, vector_all, router_all, *got = begin(
            n_dp, side, cols, lengths, packed, own, by_slot(out_grad), by_slot(marked), tokens, routes, places
        )
        kept, out_b, back_b, grads, near_in, middle_in = got[:9], got[9], got[10], got[11:19], got[19:21], got[21]
    else:
        whole, second, third_inner, grad_slots, marks = gather_dense(
            packed, own, by_slot(out_grad), by_slot(marked), n_dp, side
        )
        weights_b = whole[:, : 4 * cols].reshape(devices, 4, cols, D).transpose(1, 0, 2, 3).reshape(4, D, D)
        small = whole[:, 4 * cols :].reshape(devices, extra * D)[:, :flat_len].reshape(devices, 7 + experts, cols)
        small = small.transpose(1, 0, 2).reshape(7 + experts, D)
        vector_all = jnp.pad(small[:7].astype(f32), ((0, 1), (0, 0)))
        router_all = jnp.pad(small[7:], ((0, 128 - experts), (0, 0)))
        *kept, slots_out = attention_forward(
            lengths, tokens, weights_b, vector_all, router_all, routes, places, experts, capacity
        )
        slots_in = lax.all_to_all(slots_out, "expert", split_axis=0, concat_axis=0, tiled=True)
        slots_in = slots_in.reshape(experts * blocks * capacity, D)
        grad_slots = grad_slots.reshape(experts * blocks * capacity, D)
        marks = marks.reshape(experts * blocks * capacity, 128)
        third_outer = along(third_inner, (1, 0), (2, 3))
        fourth_inner = along(second, (1, 2), (2, 1))
        fourth_outer = along(fourth_inner, (1, 0), (2, 3))
        slot_logits = jnp.einsum("sd,ed->se", slots_in, router_all, preferred_element_type=f32)
        this = jnp.arange(128, dtype=jnp.int32) == mine
        margin = jnp.sum(slot_logits * jnp.where(this, 1.0, -marks.astype(f32)), axis=-1)
        dout = (jax.nn.sigmoid(margin)[:, None] * grad_slots.astype(f32)).astype(b16)
        grad_down_bias = jnp.sum(dout.astype(f32), axis=0)
        row = 2 * part + 1
        down_bias_full = own[row].astype(f32) + second[row].astype(f32)
        down_bias_full += jnp.where(inner, third_inner[row], third_outer[row]).astype(f32)
        down_bias_full += jnp.where(inner, fourth_inner[row], fourth_outer[row]).astype(f32)
        biases = jnp.stack([grad_down_bias, down_bias_full])
        weights = [(own,), (second,), (third_inner, third_outer), (fourth_inner, fourth_outer)]
        sums = None
        grads = []
        for i in range(4):
            *sums, grad_up, grad_down = expert_part(
                weights[i], slots_in, dout, biases, sums, i == 3, b16 if i else f32, f"expert_part_{i}"
            )
            grads += [grad_up, grad_down]
        out_b, back_b = sums
        near_in = [along(g, (0, 1), (3, 2)) for g in grads[2:4]]
        middle_in = along(grads[4], (0, 1), (3, 2))

    slots_shape = (experts, blocks, capacity, D)
    output, input_grad, dense, *came = finish(
        n_dp, side, cols, small_rows, lengths,
        (vector_all, router_all, routes, positions.reshape(count, 2)), (tokens, out_grad, weights_b),
        kept, out_b.reshape(slots_shape), back_b.reshape(slots_shape), [*grads[2:], middle_in],
    )
    totals = [
        grads[i]
        + jnp.where(inner, near_in[i].astype(f32) + came[i].astype(f32), came[2 + i].astype(f32))
        for i in range(2)
    ]
    shard_up = totals[0][None]
    shard_down = totals[1][:part][None]
    shard_up_bias = totals[1][part, :part][None]
    shard_down_bias = lax.dynamic_slice(totals[1], (part + 1, me * narrow), (1, narrow))
    if cols % 8:
        small = lax.psum(dense[:small_rows], both)
        big = dense[small_rows:].reshape(4, D, D).astype(b16)
        big = lax.psum_scatter(big, both, scatter_dimension=1, tiled=True).astype(f32)
        dense = jnp.concatenate([big.reshape(4 * cols, D), small], axis=0)
    shard_weights = dense[: 4 * cols].reshape(4, cols, D)
    small = lax.dynamic_slice(
        dense[4 * cols :], (0, (me * experts + mine) * cols), (small_rows, cols)
    )
    shard_vector, shard_router = small[:7], small[8 : 8 + experts]

    params = (attention, gain_bias, router, expert_up, up_bias, expert_down, down_bias)
    grads = (shard_weights, shard_vector, shard_router, shard_up, shard_up_bias, shard_down, shard_down_bias)
    firsts = (first_attention, first_gain_bias, first_router, first_expert_up, first_up_bias, first_expert_down, first_down_bias)
    squares = (square_attention, square_gain_bias, square_router, square_expert_up, square_up_bias, square_expert_down, square_down_bias)
    hidden_units = n_dp * part
    rates = (1.6 * D ** (-0.5), 0.3, 0.5 * D ** (-0.5), 1.5 * D ** (-0.5), 0.25, 0.5 * hidden_units ** (-0.5), 0.25)
    updated = [adam_step(params[i], grads[i], firsts[i], squares[i], rates[i]) for i in range(7)]
    return (output, input_grad, *grads, *(u[0] for u in updated), *(u[1] for u in updated), *(u[2] for u in updated))


def solution(mesh):
    rows = P(("dp", "expert"), None)
    state = (
        P(None, ("dp", "expert"), None),
        P(None, ("dp", "expert")),
        P(None, ("dp", "expert")),
        P("expert", "dp", None),
        P("expert", "dp"),
        P("expert", "dp", None),
        P("expert", "dp"),
    )
    return jax.shard_map(
        body,
        mesh=mesh,
        in_specs=(rows, rows, rows, P(("dp", "expert")), *state, *state, *state),
        out_specs=(rows, rows, *state, *state, *state, *state),
        check_vma=False,
    )
```
